128 devices in a mesh: dp: 4 (over x), fsdp: 4 (over z_hi, core), seq: 8 (over z_lo, y).
Axes of the slice: x: 4, y: 4, z: 4 (z_hi: 2, z_lo: 2; z = z_hi * 2 + z_lo), core: 2. Of those that a mesh axis runs over, the one named last changes fastest.
Arguments:
- frames: bfloat16 [16, 2048, 1536], P(('dp', 'fsdp'), 'seq'), may hold values from -6 to 6
- projection: bfloat16 [1536, 3072], P('fsdp'), may hold values from -1 to 1
- lengths: int32 [16], P(('dp', 'fsdp')), may hold values from 512 to 2048
- cotangent: bfloat16 [16, 2048, 1024], P(('dp', 'fsdp'), 'seq'), may hold values from -24 to 24
Outputs:
- context: bfloat16 [16, 2048, 1024], P(('dp', 'fsdp'), 'seq')
- input_gradient: float32 [16, 2048, 1536], P(('dp', 'fsdp'), 'seq')
- projection_gradient: float32 [1536, 3072], P(('dp', 'fsdp', 'seq'))
The draws below stay inside these ranges and needn't reach their ends.
All inputs are finite; a program needn't handle non-finite values.
Results may differ from the reference program's by a relative error of at most 0.007.
The reference program's roundings to bfloat16 on the way (of `normed`, `packed`, `weights`, `masked`, `value_gradient`, `score_gradient`, `query_gradient` and `key_gradient`) count: a program that leaves them out, or rounds other values in their place, can miss the bound.
Values may be sent and summed in bfloat16 or wider, within the bound.
No kernel may reach another device: no remote copies, remote signals or barrier semaphores. Data moves between devices by JAX's collectives and lax.ppermute only.
A program may use at most 128 MiB of HBM per device.

```python
import math
import jax
import jax.numpy as jnp
from jax import lax

D = 1536
HEADS = 16
HD = 64
FRAMES = 2048
RECS = 16


def draw_frames(key, part):
    base = jax.random.normal(jax.random.fold_in(key, 1), (RECS, FRAMES, D), jnp.float32)
    return jnp.clip(base, -6.0, 6.0).astype(jnp.bfloat16)


def draw_projection(key, part):
    base = jax.random.normal(jax.random.fold_in(key, 11), (D, 3, HEADS, HD), jnp.float32) / math.sqrt(D)
    return jnp.clip(base, -1.0, 1.0).reshape(D, 3 * HEADS * HD).astype(jnp.bfloat16)


def draw_cotangent(key, part):
    base = jax.random.normal(jax.random.fold_in(key, 21), (RECS, FRAMES, HEADS * HD), jnp.float32)
    return jnp.clip(4.0 * base, -24.0, 24.0).astype(jnp.bfloat16)


def set_ends(values, key, smallest, largest):
    dims = values.shape
    spot = [jax.random.randint(jax.random.fold_in(key, axis), (), 0, dims[axis]) for axis in range(len(dims))]
    values = values.at[tuple(spot)].set(smallest)
    longest = dims.index(max(dims))
    spot[longest] = (spot[longest] + 1) % dims[longest]
    return values.at[tuple(spot)].set(largest)


def setup_inputs(seed: int = 0) -> dict:
    splits = jax.random.split(jax.random.key(seed), 5)
    return {
        "frames": draw_frames(jax.random.fold_in(splits[4], 71), 0),
        "projection": draw_projection(jax.random.fold_in(splits[4], 71), 0),
        "lengths": set_ends(jax.random.randint(splits[2], (RECS,), FRAMES // 4, FRAMES + 1), jax.random.fold_in(splits[2], 1), FRAMES // 4, FRAMES).astype(jnp.int32),
        "cotangent": draw_cotangent(jax.random.fold_in(splits[4], 71), 0),
    }


EPS = 1e-05

def attend_rows(query_rows, key_rows, valid):
    factor = 1.0 / math.sqrt(HD)
    scores = jnp.einsum('qhd,khd->hqk', query_rows.astype(jnp.float32), key_rows.astype(jnp.float32)) * factor
    scores = jnp.where(valid[None, None, :], scores, -jnp.inf)
    row_peak = lax.optimization_barrier(jnp.max(scores, axis=2, keepdims=True))
    exponentials = jnp.exp(scores - row_peak)
    return exponentials / lax.optimization_barrier(jnp.sum(exponentials, axis=2, keepdims=True))

def reference(frames, projection, lengths, cotangent):
    feature_width = HEADS * HD
    factor = 1.0 / math.sqrt(HD)

    def one_recording(running, inputs):
        rows_in, length, upstream = inputs
        as_float = rows_in.astype(jnp.float32)
        centered = as_float - lax.optimization_barrier(jnp.mean(as_float, axis=1, keepdims=True))
        inv_std = lax.rsqrt(lax.optimization_barrier(jnp.mean(centered * centered, axis=1, keepdims=True)) + EPS)
        standard = centered * inv_std
        normed = standard.astype(jnp.bfloat16)
        packed = jnp.dot(normed, projection, preferred_element_type=jnp.float32).astype(jnp.bfloat16)
        packed = packed.reshape(FRAMES, 3, HEADS, HD)
        query_rows = packed[:, 0]
        key_rows = packed[:, 1]
        value_rows = packed[:, 2]
        valid = jnp.arange(FRAMES, dtype=jnp.int32) < length
        probabilities = attend_rows(query_rows, key_rows, valid)
        weights = probabilities.astype(jnp.bfloat16)
        mixture = jnp.einsum('hqk,khd->qhd', weights.astype(jnp.float32), value_rows.astype(jnp.float32))
        mixture = jnp.where(valid[:, None, None], mixture, jnp.zeros_like(mixture)).astype(jnp.bfloat16)
        masked = jnp.where(valid[:, None], upstream, jnp.zeros_like(upstream)).reshape(FRAMES, HEADS, HD)
        value_gradient = jnp.einsum('hqk,qhd->khd', weights.astype(jnp.float32), masked.astype(jnp.float32)).astype(jnp.bfloat16)
        prob_gradient = jnp.einsum('qhd,khd->hqk', masked.astype(jnp.float32), value_rows.astype(jnp.float32))
        row_inner = lax.optimization_barrier(jnp.sum(probabilities * prob_gradient, axis=2, keepdims=True))
        score_gradient = (probabilities * (prob_gradient - row_inner) * factor).astype(jnp.bfloat16)
        query_gradient = jnp.einsum('hqk,khd->qhd', score_gradient.astype(jnp.float32), key_rows.astype(jnp.float32)).astype(jnp.bfloat16)
        key_gradient = jnp.einsum('hqk,qhd->khd', score_gradient.astype(jnp.float32), query_rows.astype(jnp.float32)).astype(jnp.bfloat16)
        packed_gradient = jnp.stack([query_gradient, key_gradient, value_gradient], axis=1).reshape(FRAMES, 3 * feature_width)
        normed_gradient = lax.dot_general(packed_gradient, projection, (((1,), (1,)), ((), ())), preferred_element_type=jnp.float32)
        row_mean = lax.optimization_barrier(jnp.mean(normed_gradient, axis=1, keepdims=True))
        projected = lax.optimization_barrier(jnp.mean(normed_gradient * standard, axis=1, keepdims=True))
        input_gradient = inv_std * (normed_gradient - row_mean - standard * projected)
        running = running + lax.dot_general(normed, packed_gradient, (((0,), (0,)), ((), ())), preferred_element_type=jnp.float32)
        return (running, (mixture.reshape(FRAMES, feature_width), input_gradient))
    start_sum = jnp.zeros((D, 3 * feature_width), jnp.float32)
    projection_gradient, outputs = lax.scan(one_recording, start_sum, (frames, lengths, cotangent))
    context, input_gradient = outputs
    return (context, input_gradient, projection_gradient)
```

```python
import jax
import jax.numpy as jnp
from jax import lax
from jax.experimental import pallas as pl
from jax.experimental.pallas import tpu as pltpu
from jax.sharding import PartitionSpec as P

BF = jnp.bfloat16
F32 = jnp.float32
D = 1536
HD = 64
T = 2048
ROWS = 256
SEQ = 8
GW = 128
EPS = 1e-05
BQ = 256
CH = 512
NC = T // CH
VM = pl.BlockSpec(memory_space=pltpu.VMEM)
SM = pl.BlockSpec(memory_space=pltpu.SMEM)
PARAMS = pltpu.CompilerParams(vmem_limit_bytes=56 * 2**20)


def dot(a, b, dims=((1,), (0,))):
    return lax.dot_general(a, b, (dims, ((), ())), preferred_element_type=F32)


def standardize(x):
    centered = x - jnp.mean(x, axis=1, keepdims=True)
    inv_std = lax.rsqrt(jnp.mean(centered * centered, axis=1, keepdims=True) + EPS)
    return centered * inv_std, inv_std


def norm_kernel(x_ref, out_ref):
    out_ref[...] = standardize(x_ref[...].astype(F32))[0].astype(BF)


def project_kernel(pos_ref, w_ref, *refs):
    blocks, out_ref = refs[:SEQ], refs[SEQ]
    for b in range(SEQ):
        first = pl.multiple_of(pos_ref[b] * ROWS, ROWS)
        out_ref[pl.ds(first, ROWS), :] = dot(blocks[b][...], w_ref[...]).astype(BF)


def attention_kernel(
    len_ref, qkv_ref, up_ref, out_ref, ka, vt, kt, qt, ut, s_ref, e_ref, dk_acc, dv_acc
):
    length = len_ref[0]
    lane = lax.broadcasted_iota(jnp.int32, (CH, 128), 1)
    for c in range(NC):
        r = slice(c * CH, (c + 1) * CH)
        k = qkv_ref[r, 128:256].astype(F32)
        row = lax.broadcasted_iota(jnp.int32, (CH, 128), 0) + c * CH
        bias = jnp.where(row < length, 0.0, -1e30)
        for h in range(2):
            other = jnp.where(lane == (1 - h) * HD, bias, 0.0)
            ka[h, r, :] = jnp.where(lane // HD == h, k, other).astype(BF)
        kt[:, r] = k.T.astype(BF)
        v = qkv_ref[r, 256:384].astype(F32).T
        for h in range(2):
            vt[h, 0:HD, r] = v[h * HD : (h + 1) * HD].astype(BF)
            vt[h, HD : HD + 16, r] = jnp.ones((16, CH), BF)
        qt[:, r] = (qkv_ref[r, 0:128].astype(F32) * 0.125).T.astype(BF)
        u = jnp.where(row < length, up_ref[r, :].astype(F32), 0.0)
        ut[:, r] = u.T.astype(BF)
    dk_acc[...] = jnp.zeros_like(dk_acc)
    dv_acc[...] = jnp.zeros_like(dv_acc)
    zeros = jnp.zeros((HD, BQ), BF)
    ones_row = jnp.where(lax.broadcasted_iota(jnp.int32, (HD, BQ), 0) == 0, 1.0, 0.0).astype(BF)

    def place(x, other, h):
        return jnp.concatenate([x, other] if h == 0 else [other, x], axis=0)

    def step(i, carry):
        q0 = pl.multiple_of(i * BQ, BQ)
        cols = pl.ds(q0, BQ)
        contexts, ups, queries, inners = [], [], [], []
        for h in range(2):
            hrows = slice(h * HD, (h + 1) * HD)
            qh = qt[hrows, cols]
            qa = place(qh, ones_row, h)
            peak = None
            for c in range(NC):
                r = slice(c * CH, (c + 1) * CH)
                s = dot(ka[h, r, :], qa)
                s_ref[h, r, :] = s
                t = jnp.max(s.reshape(CH // 8, 8, BQ), axis=0)
                peak = t if peak is None else jnp.maximum(peak, t)
            peak = jnp.max(peak, axis=0, keepdims=True)
            total = None
            for c in range(NC):
                r = slice(c * CH, (c + 1) * CH)
                e = jnp.exp(s_ref[h, r, :] - peak).astype(BF)
                e_ref[h, r, :] = e
                t = dot(vt[h, :, r], e)
                total = t if total is None else total + t
            inverse = 1.0 / total[HD : HD + 1]
            context = total[0:HD] * inverse
            up = (ut[hrows, cols].astype(F32) * inverse).astype(BF)
            inner = jnp.sum(up.astype(F32) * context, axis=0, keepdims=True)
            contexts.append(context)
            ups.append(place(up, zeros, h))
            queries.append(place(qh, zeros, h))
            inners.append(inner)
        dq = [None, None]
        for c in range(NC):
            r = slice(c * CH, (c + 1) * CH)
            dss, es = [], []
            for h in range(2):
                dp = dot(qkv_ref[r, 256:384], ups[h])
                e = e_ref[h, r, :]
                ds = (e.astype(F32) * (dp - inners[h])).astype(BF)
                t = dot(kt[h * HD : (h + 1) * HD, r], ds)
                dq[h] = t if dq[h] is None else dq[h] + t
                dss.append(ds)
                es.append(e)
            nt = ((1,), (1,))
            dv_acc[r, :] += dot(es[0], ups[0], nt) + dot(es[1], ups[1], nt)
            dk_acc[r, :] += dot(dss[0], queries[0], nt) + dot(dss[1], queries[1], nt)
        context = jnp.concatenate(contexts, axis=0)
        col = lax.broadcasted_iota(jnp.int32, (128, BQ), 1) + q0
        context = jnp.where(col < length, context, 0.0)
        out_ref[cols, 384:512] = context.T.astype(BF)
        out_ref[cols, 0:128] = (jnp.concatenate(dq, axis=0) * 0.125).T.astype(BF)
        return carry

    lax.fori_loop(0, T // BQ, step, 0)
    for c in range(NC):
        r = slice(c * CH, (c + 1) * CH)
        out_ref[r, 128:256] = dk_acc[r, :].astype(BF)
        out_ref[r, 256:384] = dv_acc[r, :].astype(BF)


def weight_gradient_kernel(pos_ref, grad_ref, *refs):
    blocks, out_ref, acc = refs[:SEQ], refs[SEQ], refs[SEQ + 1]
    for b in range(SEQ):
        first = pl.multiple_of(pos_ref[b] * ROWS, ROWS)
        gt = grad_ref[pl.ds(first, ROWS), 0:384].astype(F32).T.astype(BF)
        for c in range(3):
            cs = slice(c * 512, (c + 1) * 512)
            t = dot(gt, blocks[b][:, cs])
            if b == 0:
                acc[:, cs] = t
            else:
                acc[:, cs] += t
    for c in range(12):
        cs = slice(c * 128, (c + 1) * 128)
        out_ref[cs, :] = acc[:, cs].T.astype(BF)


def input_gradient_kernel(grads_ref, w_ref, x_ref, ctx_ref, out_ref, packed):
    for s in range(SEQ):
        ctx_ref[:, s * GW : (s + 1) * GW] = grads_ref[s, :, 384:512]
        for kind in range(3):
            to = kind * 1024 + s * GW
            packed[:, to : to + GW] = grads_ref[s, :, kind * GW : (kind + 1) * GW]
    g = packed[...]
    for c in range(4):
        cs = slice(c * 384, (c + 1) * 384)
        out_ref[:, cs] = dot(g, w_ref[cs, :], ((1,), (1,)))
    standard, inv_std = standardize(x_ref[...].astype(F32))
    ng = out_ref[...]
    row_mean = jnp.mean(ng, axis=1, keepdims=True)
    projected = jnp.mean(ng * standard, axis=1, keepdims=True)
    out_ref[...] = inv_std * (ng - row_mean - standard * projected)


def shape(dims, dtype=BF):
    return jax.ShapeDtypeStruct(dims, dtype)


def gather_rows(x):
    up = [(i, (i // 4) * 4 + (i % 4 + 1) % 4) for i in range(8)]
    down = [(i, (i // 4) * 4 + (i % 4 + 3) % 4) for i in range(8)]
    across = [(i, i ^ 4) for i in range(8)]

    def send(v, way):
        return lax.ppermute(v, "seq", way)

    half = ROWS // 2
    below = send(x, up)
    above = send(x, down)
    other = send(x, across)
    far = jnp.concatenate([send(below[:half], up), send(above[half:], down)], axis=0)
    other_below = send(other, up)
    other_above = send(other, down)
    other_far = send(far, across)
    offsets = [(0, 0), (0, 3), (0, 1), (1, 0), (0, 2), (1, 3), (1, 1), (1, 2)]
    return offsets, [x, below, above, other, far, other_below, other_above, other_far]


def body(frames, projection, lengths, cotangent):
    x = frames[0]
    me = lax.axis_index("seq")
    normed = pl.pallas_call(norm_kernel, out_shape=shape((ROWS, D)), in_specs=[VM], out_specs=VM)(x)
    offsets, blocks = gather_rows(normed)
    place = jnp.stack([(me // 4 ^ dz) * 4 + (me % 4 + dy) % 4 for dz, dy in offsets]).astype(jnp.int32)

    columns = lax.dynamic_slice_in_dim(projection.reshape(384, 3, SEQ, GW), me, 1, 2).reshape(384, 384)
    columns = lax.all_gather(columns, "fsdp", axis=0, tiled=True)
    upstream = lax.all_to_all(
        cotangent[0].reshape(ROWS, SEQ, GW).transpose(1, 0, 2), "seq", 0, 0, tiled=True
    ).reshape(T, GW)
    weight_full = lax.all_gather(projection, "fsdp", axis=0, tiled=True)

    qkv = pl.pallas_call(
        project_kernel,
        out_shape=shape((T, 384)),
        in_specs=[SM, VM] + [VM] * SEQ,
        out_specs=VM,
        compiler_params=PARAMS,
    )(place, columns, *blocks)
    grads = pl.pallas_call(
        attention_kernel,
        out_shape=shape((T, 512)),
        in_specs=[SM, VM, VM],
        out_specs=VM,
        scratch_shapes=[
            pltpu.VMEM((2, T, 128), BF),
            pltpu.VMEM((2, HD + 16, T), BF),
            pltpu.VMEM((128, T), BF),
            pltpu.VMEM((128, T), BF),
            pltpu.VMEM((128, T), BF),
            pltpu.VMEM((2, T, BQ), F32),
            pltpu.VMEM((2, T, BQ), BF),
            pltpu.VMEM((T, 128), F32),
            pltpu.VMEM((T, 128), F32),
        ],
        compiler_params=PARAMS,
        cost_estimate=pl.CostEstimate(
            flops=40 * 2 * T * T * HD, bytes_accessed=4 * 2**20, transcendentals=2 * T * T
        ),
    )(lengths, qkv, upstream)
    returned = lax.all_to_all(grads.reshape(SEQ, ROWS, 512), "seq", 0, 0, tiled=True)
    partial = pl.pallas_call(
        weight_gradient_kernel,
        out_shape=shape((D, 384)),
        in_specs=[SM, VM] + [VM] * SEQ,
        out_specs=VM,
        scratch_shapes=[pltpu.VMEM((384, D), F32)],
        compiler_params=PARAMS,
        cost_estimate=pl.CostEstimate(
            flops=2 * T * D * 384, bytes_accessed=10 * 2**20, transcendentals=0
        ),
    )(place, grads, *blocks)
    partial = lax.all_to_all(partial.reshape(16, 96, 384), ("dp", "fsdp"), 0, 0, tiled=True)
    summed = jnp.sum(partial.astype(F32), axis=0)
    spread = lax.all_to_all(summed.reshape(SEQ, 12, 384), "seq", 0, 0, tiled=True)
    projection_gradient = (
        spread.reshape(SEQ, 12, 3, GW).transpose(1, 2, 0, 3).reshape(12, 3072)
    )
    context, input_gradient = pl.pallas_call(
        input_gradient_kernel,
        out_shape=(shape((ROWS, 1024)), shape((ROWS, D), F32)),
        in_specs=[VM, VM, VM],
        out_specs=(VM, VM),
        scratch_shapes=[pltpu.VMEM((ROWS, 3072), BF)],
        compiler_params=PARAMS,
        cost_estimate=pl.CostEstimate(
            flops=2 * ROWS * D * 3072, bytes_accessed=14 * 2**20, transcendentals=0
        ),
    )(returned, weight_full, x)
    return (context[None], input_gradient[None], projection_gradient)


def solution(mesh):
    placed = (
        P(("dp", "fsdp"), "seq", None),
        P("fsdp", None),
        P(("dp", "fsdp")),
        P(("dp", "fsdp"), "seq", None),
    )
    return jax.shard_map(
        body,
        mesh=mesh,
        in_specs=placed,
        out_specs=(
            P(("dp", "fsdp"), "seq", None),
            P(("dp", "fsdp"), "seq", None),
            P(("dp", "fsdp", "seq"), None),
        ),
        check_vma=False,
    )
```

```python
import functools

import jax
import jax.numpy as jnp
from jax import lax
from jax.experimental import pallas as pl
from jax.experimental.pallas import tpu as pltpu
from jax.sharding import PartitionSpec as P

BF = jnp.bfloat16
F32 = jnp.float32
D = 1536
HD = 64
T = 2048
ROWS = 256
SEQ = 8
GW = 128
EPS = 1e-05
BQ = 256
CH = 512
NC = T // CH
VM = pl.BlockSpec(memory_space=pltpu.VMEM)
SM = pl.BlockSpec(memory_space=pltpu.SMEM)


def dot(a, b, dims=((1,), (0,))):
    return lax.dot_general(a, b, (dims, ((), ())), preferred_element_type=F32)


def standardize(x):
    centered = x - jnp.mean(x, axis=1, keepdims=True)
    inv_std = lax.rsqrt(jnp.mean(centered * centered, axis=1, keepdims=True) + EPS)
    return centered * inv_std, inv_std


def norm_kernel(x_ref, out_ref):
    out_ref[...] = standardize(x_ref[...].astype(F32))[0].astype(BF)


def columns_kernel(me_ref, w_ref, out_ref):
    s = me_ref[0] * GW
    q, k, v = (
        w_ref[:, pl.ds(pl.multiple_of(kind * 1024 + s, GW), GW)].astype(F32) for kind in range(3)
    )
    low = lax.broadcasted_iota(jnp.int32, k.shape, 1) < HD
    out_ref[:, 0:128] = jnp.where(low, k, pltpu.roll(v, HD, 1)).astype(BF)
    out_ref[:, 128:256] = jnp.where(low, pltpu.roll(k, HD, 1), v).astype(BF)
    out_ref[:, 256:384] = q.astype(BF)


def project_kernel(n, owner_ref, *refs):
    weights, blocks, out_ref = refs[:4], refs[4 : 4 + n], refs[4 + n]
    first = 0
    for block in blocks:
        count = block.shape[0]
        total = None
        for f in range(4):
            rows = pl.ds(pl.multiple_of(owner_ref[f] * 384, 384), 384)
            t = dot(block[:, rows], weights[f][...])
            total = t if total is None else total + t
        out_ref[first : first + count, :] = total.astype(BF)
        first += count


def attention_kernel(
    head, pos_ref, len_ref, near_ref, far_ref, up_ref, out_ref, kv, ka, vt, kt, qt, ut, s_ref, e_ref, acc
):
    length = len_ref[0]
    hrows = slice(head * HD, (head + 1) * HD)
    lane = lax.broadcasted_iota(jnp.int32, (BQ, 128), 1)
    for b in range(SEQ):
        r = slice(b * BQ, (b + 1) * BQ)
        source = near_ref if b < 4 else far_ref
        own = slice(b % 4 * BQ, (b % 4 + 1) * BQ)
        first = pl.multiple_of(pos_ref[b] * BQ, BQ)
        mine = source[own, head * 128 : (head + 1) * 128]
        kv[r, :] = mine
        keys = mine.astype(F32)
        row = lax.broadcasted_iota(jnp.int32, (BQ, 128), 0) + first
        bias = jnp.where(lane == HD, jnp.where(row < length, 0.0, -1e30), 0.0)
        ka[r, :] = jnp.where(lane < HD, keys, bias).astype(BF)
        flipped = keys.T.astype(BF)
        kt[:, r] = flipped[0:HD]
        vt[0:HD, r] = flipped[HD:128]
        vt[HD : HD + 16, r] = jnp.ones((16, BQ), BF)
        qt[:, r] = (source[own, 256:384].astype(F32) * 0.125).T[hrows].astype(BF)
        u = jnp.where(row < length, up_ref[pl.ds(first, BQ), :].astype(F32), 0.0)
        ut[:, r] = u.T[hrows].astype(BF)
    acc[...] = jnp.zeros_like(acc)
    zeros = jnp.zeros((HD, BQ), BF)
    ones_row = jnp.where(lax.broadcasted_iota(jnp.int32, (HD, BQ), 0) == 0, 1.0, 0.0).astype(BF)
    nt = ((1,), (1,))

    def step(i, carry):
        contexts, ups, queries, inners = [], [], [], []
        starts = [pl.multiple_of((2 * i + j) * BQ, BQ) for j in range(2)]
        for j in range(2):
            cols = pl.ds(starts[j], BQ)
            qh = qt[:, cols]
            qa = jnp.concatenate([qh, ones_row], axis=0)
            peak = None
            for c in range(NC):
                r = slice(c * CH, (c + 1) * CH)
                s = dot(ka[r, :], qa)
                s_ref[j, r, :] = s
                t = jnp.max(s.reshape(CH // 8, 8, BQ), axis=0)
                peak = t if peak is None else jnp.maximum(peak, t)
            peak = jnp.max(peak, axis=0, keepdims=True)
            total = None
            for c in range(NC):
                r = slice(c * CH, (c + 1) * CH)
                e = jnp.exp(s_ref[j, r, :] - peak).astype(BF)
                e_ref[j, r, :] = e
                t = dot(vt[:, r], e)
                total = t if total is None else total + t
            inverse = 1.0 / total[HD : HD + 1]
            context = total[0:HD] * inverse
            up = (ut[:, cols].astype(F32) * inverse).astype(BF)
            inner = jnp.sum(up.astype(F32) * context, axis=0, keepdims=True)
            contexts.append(context)
            ups.append(jnp.concatenate([zeros, up], axis=0))
            queries.append(jnp.concatenate([qh, zeros], axis=0))
            inners.append(inner)
        dq = [None, None]
        for c in range(NC):
            r = slice(c * CH, (c + 1) * CH)
            total = acc[r, :]
            for j in range(2):
                dp = dot(kv[r, :], ups[j])
                e = e_ref[j, r, :]
                ds = (e.astype(F32) * (dp - inners[j])).astype(BF)
                t = dot(kt[:, r], ds)
                dq[j] = t if dq[j] is None else dq[j] + t
                total = total + (dot(ds, queries[j], nt) + dot(e, ups[j], nt))
            acc[r, :] = total
        for j in range(2):
            first = pl.multiple_of(pos_ref[2 * i + j] * BQ, BQ)
            col = lax.broadcasted_iota(jnp.int32, (HD, BQ), 1) + first
            context = jnp.where(col < length, contexts[j], 0.0)
            both = jnp.concatenate([dq[j] * 0.125, context], axis=0)
            out_ref[pl.ds(first, BQ), 0:128] = both.T.astype(BF)
        return carry

    lax.fori_loop(0, T // BQ // 2, step, 0)
    for b in range(SEQ):
        rows = pl.ds(pl.multiple_of(pos_ref[b] * BQ, BQ), BQ)
        out_ref[rows, 128:256] = acc[b * BQ : (b + 1) * BQ, :].astype(BF)


def weight_gradient_kernel(pos_ref, first_ref, second_ref, *refs):
    blocks, (keep_ref, send_ref, acc) = refs[:-3], refs[-3:]
    at = [0] * SEQ
    which = 0
    for i, block in enumerate(blocks):
        count = block.shape[0]
        rows = pl.ds(pl.multiple_of(pos_ref[which] * ROWS + at[which], 128), count)
        both = [g[rows, :].astype(F32).T.astype(BF) for g in (first_ref, second_ref)]
        parts = [g[128:256] for g in both] + [g[0:HD] for g in both]
        flipped = jnp.concatenate(parts, axis=0)
        for c in range(3):
            cs = slice(c * 512, (c + 1) * 512)
            t = dot(flipped, block[:, cs])
            if i == 0:
                acc[:, cs] = t
            else:
                acc[:, cs] += t
        at[which] += count
        which += at[which] == ROWS
    core = pos_ref[SEQ]
    for c in range(4):
        flipped = acc[:, c * 384 : (c + 1) * 384].T
        halves = [[flipped[i * 96 : (i + 1) * 96] for i in (k, k + 2)] for k in range(2)]
        for k in range(2):
            for i in range(2):
                r = slice((c * 2 + i) * 96, (c * 2 + i + 1) * 96)

                @pl.when(core == k)
                def _():
                    keep_ref[r, :] = halves[k][i]

                @pl.when(core != k)
                def _():
                    send_ref[r, :] = halves[k][i].astype(BF)


def add_kernel(keep_ref, got_ref, out_ref):
    out_ref[...] = (keep_ref[...] + got_ref[...].astype(F32)).astype(BF)


def join(first, second, part):
    low = lax.broadcasted_iota(jnp.int32, first.shape, first.ndim - 1) < HD
    if part == 0:
        return jnp.where(low, first, pltpu.roll(second, HD, first.ndim - 1))
    return jnp.where(low, pltpu.roll(first, HD, first.ndim - 1), second)


def combine_kernel(parts_ref, out_ref):
    for s in range(SEQ):
        total = None
        for r in range(8):
            t = parts_ref[r * SEQ + s].astype(F32)
            total = t if total is None else total + t
        at = s * GW
        low, high = total[:, 0:128], total[:, 128:256]
        out_ref[:, at : at + GW] = total[:, 256:384]
        out_ref[:, 1024 + at : 1024 + at + GW] = join(low, high, 0)
        out_ref[:, 2048 + at : 2048 + at + GW] = join(low, high, 1)


def input_gradient_kernel(
    pos_ref, first_ref, second_ref, w0_ref, w1_ref, w2_ref, w3_ref, x_ref, ctx_ref, out_ref, packed
):
    for s in range(SEQ):
        at = s * GW
        a = [first_ref[s, :, i * 128 : (i + 1) * 128].astype(F32) for i in range(2)]
        b = [second_ref[s, :, i * 128 : (i + 1) * 128].astype(F32) for i in range(2)]
        ctx_ref[:, at : at + GW] = join(a[0], b[0], 1).astype(BF)
        packed[:, at : at + GW] = join(a[0], b[0], 0).astype(BF)
        packed[:, 1024 + at : 1024 + at + GW] = join(a[1], b[1], 0).astype(BF)
        packed[:, 2048 + at : 2048 + at + GW] = join(a[1], b[1], 1).astype(BF)
    for f, w_ref in enumerate((w0_ref, w1_ref, w2_ref, w3_ref)):
        to = pl.ds(pl.multiple_of(pos_ref[f] * 384, 384), 384)
        out_ref[:, to] = dot(packed[...], w_ref[...], ((1,), (1,)))
    standard, inv_std = standardize(x_ref[...].astype(F32))
    ng = out_ref[...]
    row_mean = jnp.mean(ng, axis=1, keepdims=True)
    projected = jnp.mean(ng * standard, axis=1, keepdims=True)
    out_ref[...] = inv_std * (ng - row_mean - standard * projected)


def shape(dims, dtype=BF):
    return jax.ShapeDtypeStruct(dims, dtype)


def gather_rows(x, extra):
    up = [(i, (i // 4) * 4 + (i % 4 + 1) % 4) for i in range(8)]
    down = [(i, (i // 4) * 4 + (i % 4 + 3) % 4) for i in range(8)]
    across = [(i, i ^ 4) for i in range(8)]

    def send(v, way):
        return lax.ppermute(v, "seq", way)

    half = ROWS // 2
    below, above, other = send(x, up), send(x, down), send(x, across)
    below, above, other, extra = lax.optimization_barrier((below, above, other, extra))
    far = [send(below[:half], up), send(above[half:], down)]
    other_below, other_above = send(other, up), send(other, down)
    other_far = [send(v, across) for v in far]
    offsets = [(0, 0), (0, 3), (0, 1), (1, 0), (0, 2), (1, 3), (1, 1), (1, 2)]
    return offsets, [x, below, above, other], [*far, other_below, other_above, *other_far], extra


def sibling(v):
    return lax.ppermute(v, "core", [(0, 1), (1, 0)])


def gather_columns(mine):
    over = lax.ppermute(mine, "zh", [(0, 1), (1, 0)])
    return [mine, sibling(mine), over, sibling(over)]


def gather_weight(w):
    swap = [(f * 8 + s, (f ^ 1) * 8 + (s ^ 4)) for f in range(2) for s in range(8)]
    over = lax.ppermute(w, ("zh", "seq"), swap)
    return [w, sibling(w), over, sibling(over)]


def call(kernel, out, in_specs, flops=0, scratch=(), transcendentals=0, vmem=32):
    return pl.pallas_call(
        kernel,
        out_shape=out,
        in_specs=in_specs,
        out_specs=jax.tree.map(lambda _: VM, out),
        scratch_shapes=list(scratch),
        compiler_params=pltpu.CompilerParams(vmem_limit_bytes=vmem * 2**20),
        cost_estimate=pl.CostEstimate(
            flops=flops, bytes_accessed=2**20, transcendentals=transcendentals
        ),
    )


def body(frames, projection, lengths, cotangent):
    x = frames[0]
    me = lax.axis_index("seq")
    core = lax.axis_index("core")
    fsdp = lax.axis_index("zh") * 2 + core
    normed = call(norm_kernel, shape((ROWS, D)), [VM])(x)
    mine = call(columns_kernel, shape((384, 384)), [SM, VM])(me[None].astype(jnp.int32), projection)
    upstream = cotangent[0].reshape(ROWS, SEQ, GW).transpose(1, 0, 2)
    offsets, near, far, (mine, upstream) = gather_rows(normed, (mine, upstream))
    blocks = near + far
    index = [(me // 4 ^ dz) * 4 + (me % 4 + dy) % 4 for dz, dy in offsets]
    place = jnp.stack(index + [core]).astype(jnp.int32)
    owners = jnp.stack([fsdp ^ i for i in range(4)]).astype(jnp.int32)

    columns = gather_columns(mine)
    upstream = lax.all_to_all(upstream, "seq", 0, 0, tiled=True).reshape(T, GW)
    weights = gather_weight(projection)

    def project(rows):
        return call(
            functools.partial(project_kernel, len(rows)),
            shape((T // 2, 384)),
            [SM] + [VM] * (4 + len(rows)),
            T * D * 384,
        )(owners, *columns, *rows)

    near_packed, far_packed = project(near), project(far)

    def attend(head):
        return call(
            functools.partial(attention_kernel, head),
            shape((T, 256)),
            [SM, SM, VM, VM, VM],
            20 * 2 * T * T * HD,
            [
                pltpu.VMEM((T, 128), BF),
                pltpu.VMEM((T, 128), BF),
                pltpu.VMEM((HD + 16, T), BF),
                pltpu.VMEM((HD, T), BF),
                pltpu.VMEM((HD, T), BF),
                pltpu.VMEM((HD, T), BF),
                pltpu.VMEM((2, T, BQ), F32),
                pltpu.VMEM((2, T, BQ), BF),
                pltpu.VMEM((T, 128), F32),
            ],
            T * T,
        )(place, lengths, near_packed, far_packed, upstream)

    def send_back(grads):
        return lax.all_to_all(grads.reshape(SEQ, ROWS, 256), "seq", 0, 0, tiled=True)

    first = attend(0)
    back0 = send_back(first)
    second = attend(1)
    second, back0 = lax.optimization_barrier((second, back0))
    back1 = send_back(second)
    keep, send = call(
        weight_gradient_kernel,
        (shape((768, 384), F32), shape((768, 384))),
        [SM] + [VM] * (2 + len(blocks)),
        2 * T * D * 384,
        [pltpu.VMEM((384, D), F32)],
    )(place, first, second, *blocks)
    got = sibling(send)
    got, back1 = lax.optimization_barrier((got, back1))
    partial = call(add_kernel, shape((768, 384)), [VM, VM])(keep, got)
    partial = lax.all_to_all(
        partial.reshape(64, 12, 384), ("dp", "zh", "seq"), 0, 0, tiled=True
    )
    projection_gradient = call(combine_kernel, shape((12, 3072), F32), [VM])(partial)
    context, input_gradient = call(
        input_gradient_kernel,
        (shape((ROWS, 1024)), shape((ROWS, D), F32)),
        [SM] + [VM] * 7,
        2 * ROWS * D * 3072,
        [pltpu.VMEM((ROWS, 3072), BF)],
    )(owners, back0, back1, *weights, x)
    return (context[None], input_gradient[None], projection_gradient)


def solution(mesh):
    split = jax.sharding.Mesh(mesh.devices.reshape(4, 2, 2, 8), ("dp", "zh", "core", "seq"))
    record = ("dp", "zh", "core")
    placed = (P(record, "seq", None), P(("zh", "core"), None), P(record), P(record, "seq", None))
    return jax.shard_map(
        body,
        mesh=split,
        in_specs=placed,
        out_specs=(P(record, "seq", None), P(record, "seq", None), P((*record, "seq"), None)),
        check_vma=False,
    )
```

```python
import functools

import jax
import jax.numpy as jnp
from jax import lax
from jax.experimental import pallas as pl
from jax.experimental.pallas import tpu as pltpu
from jax.sharding import PartitionSpec as P

BF = jnp.bfloat16
F32 = jnp.float32
D = 1536
HD = 64
T = 2048
ROWS = 256
SEQ = 8
GW = 128
EPS = 1e-05
BQ = 256
CH = 512
NC = T // CH
VM = pl.BlockSpec(memory_space=pltpu.VMEM)
SM = pl.BlockSpec(memory_space=pltpu.SMEM)
ANY = pl.BlockSpec(memory_space=pl.ANY)


def dot(a, b, dims=((1,), (0,))):
    return lax.dot_general(a, b, (dims, ((), ())), preferred_element_type=F32)


def standardize(x):
    centered = x - jnp.mean(x, axis=1, keepdims=True)
    inv_std = lax.rsqrt(jnp.mean(centered * centered, axis=1, keepdims=True) + EPS)
    return centered * inv_std, inv_std


def norm_kernel(x_ref, out_ref):
    out_ref[...] = standardize(x_ref[...].astype(F32))[0].astype(BF)


def columns_kernel(y_ref, w_ref, out_ref):
    for z in range(2):
        s = (z * 4 + y_ref[0]) * GW
        q, k, v = (
            w_ref[:, pl.ds(pl.multiple_of(kind * 1024 + s, GW), GW)].astype(F32) for kind in range(3)
        )
        low = lax.broadcasted_iota(jnp.int32, k.shape, 1) < HD
        at = z * 384
        out_ref[:, at : at + 128] = jnp.where(low, k, pltpu.roll(v, HD, 1)).astype(BF)
        out_ref[:, at + 128 : at + 256] = jnp.where(low, pltpu.roll(k, HD, 1), v).astype(BF)
        out_ref[:, at + 256 : at + 384] = q.astype(BF)


def project_kernel(n, owner_ref, *refs):
    weights, blocks, outs = refs[:4], refs[4 : 4 + n], refs[4 + n :]
    for j in (1, 0):
        cols = pl.ds(pl.multiple_of((owner_ref[4] ^ j) * 384, 384), 384)
        first = 0
        for block in blocks:
            count = block.shape[0]
            total = None
            for f in range(4):
                rows = pl.ds(pl.multiple_of(owner_ref[f] * 384, 384), 384)
                t = dot(block[:, rows], weights[f][:, cols])
                total = t if total is None else total + t
            outs[j][first : first + count, :] = total.astype(BF)
            first += count


def attention_kernel(
    head, pos_ref, len_ref, near_ref, far_ref, other_ref, last_ref, up_ref, out_ref, kv, ka, vt, kt, qt, ut, s_ref, e_ref, acc
):
    length = len_ref[0]
    hrows = slice(head * HD, (head + 1) * HD)
    lane = lax.broadcasted_iota(jnp.int32, (BQ, 128), 1)
    for b in range(SEQ):
        r = slice(b * BQ, (b + 1) * BQ)
        source = (near_ref, far_ref, other_ref, last_ref)[b // 4 * 2 + (b % 4 == 3)]
        own = slice(b % 4 % 3 * BQ, (b % 4 % 3 + 1) * BQ)
        first = pl.multiple_of(pos_ref[b] * BQ, BQ)
        mine = source[own, head * 128 : (head + 1) * 128]
        kv[r, :] = mine
        keys = mine.astype(F32)
        row = lax.broadcasted_iota(jnp.int32, (BQ, 128), 0) + first
        bias = jnp.where(lane == HD, jnp.where(row < length, 0.0, -1e30), 0.0)
        ka[r, :] = jnp.where(lane < HD, keys, bias).astype(BF)
        flipped = keys.T.astype(BF)
        kt[:, r] = flipped[0:HD]
        vt[0:HD, r] = flipped[HD:128]
        vt[HD : HD + 16, r] = jnp.ones((16, BQ), BF)
        qt[:, r] = (source[own, 256:384].astype(F32) * 0.125).T[hrows].astype(BF)
        u = jnp.where(row < length, up_ref[pl.ds(first, BQ), :].astype(F32), 0.0)
        ut[:, r] = u.T[hrows].astype(BF)
    acc[...] = jnp.zeros_like(acc)
    zeros = jnp.zeros((HD, BQ), BF)
    ones_row = jnp.where(lax.broadcasted_iota(jnp.int32, (HD, BQ), 0) == 0, 1.0, 0.0).astype(BF)
    nt = ((1,), (1,))

    def step(i, carry):
        contexts, ups, queries, inners = [], [], [], []
        starts = [pl.multiple_of((2 * i + j) * BQ, BQ) for j in range(2)]
        for j in range(2):
            cols = pl.ds(starts[j], BQ)
            qh = qt[:, cols]
            qa = jnp.concatenate([qh, ones_row], axis=0)
            peak = None
            for c in range(NC):
                r = slice(c * CH, (c + 1) * CH)
                s = dot(ka[r, :], qa)
                s_ref[j, r, :] = s
                t = jnp.max(s.reshape(CH // 8, 8, BQ), axis=0)
                peak = t if peak is None else jnp.maximum(peak, t)
            peak = jnp.max(peak, axis=0, keepdims=True)
            total = None
            for c in range(NC):
                r = slice(c * CH, (c + 1) * CH)
                e = jnp.exp(s_ref[j, r, :] - peak).astype(BF)
                e_ref[j, r, :] = e
                t = dot(vt[:, r], e)
                total = t if total is None else total + t
            inverse = 1.0 / total[HD : HD + 1]
            context = total[0:HD] * inverse
            up = (ut[:, cols].astype(F32) * inverse).astype(BF)
            inner = jnp.sum(up.astype(F32) * context, axis=0, keepdims=True)
            contexts.append(context)
            ups.append(jnp.concatenate([zeros, up], axis=0))
            queries.append(jnp.concatenate([qh, zeros], axis=0))
            inners.append(inner)
        dq = [None, None]
        for c in range(NC):
            r = slice(c * CH, (c + 1) * CH)
            total = acc[r, :]
            for j in range(2):
                dp = dot(kv[r, :], ups[j])
                e = e_ref[j, r, :]
                ds = (e.astype(F32) * (dp - inners[j])).astype(BF)
                t = dot(kt[:, r], ds)
                dq[j] = t if dq[j] is None else dq[j] + t
                total = total + (dot(ds, queries[j], nt) + dot(e, ups[j], nt))
            acc[r, :] = total
        for j in range(2):
            first = pl.multiple_of(pos_ref[2 * i + j] * BQ, BQ)
            col = lax.broadcasted_iota(jnp.int32, (HD, BQ), 1) + first
            context = jnp.where(col < length, contexts[j], 0.0)
            both = jnp.concatenate([dq[j] * 0.125, context], axis=0)
            out_ref[pl.ds(first, BQ), 0:128] = both.T.astype(BF)
        return carry

    lax.fori_loop(0, T // BQ // 2, step, 0)
    for b in range(SEQ):
        rows = pl.ds(pl.multiple_of(pos_ref[b] * BQ, BQ), BQ)
        out_ref[rows, 128:256] = acc[b * BQ : (b + 1) * BQ, :].astype(BF)


def fetch(pairs, sems):
    copies = [pltpu.make_async_copy(a, b, sems.at[i]) for i, (a, b) in enumerate(pairs)]
    for copy in copies:
        copy.start()
    return copies


def weight_gradient_kernel(pos_ref, first_ref, second_ref, *refs):
    sources, (keep_ref, send_ref, acc, held, sems) = refs[:-5], refs[-5:]
    at = [sum(b.shape[0] for b in sources[:i]) for i in range(len(sources))]
    spots = [pl.ds(a, b.shape[0]) for a, b in zip(at, sources)]
    copies = fetch([(b, held.at[spot]) for b, spot in zip(sources, spots)], sems)
    for i, block in enumerate(sources):
        count = block.shape[0]
        first = pos_ref[at[i] // ROWS] * ROWS + at[i] % ROWS
        rows = pl.ds(pl.multiple_of(first, 128), count)
        both = [g[rows, :].astype(F32).T.astype(BF) for g in (first_ref, second_ref)]
        parts = [g[128:256] for g in both] + [g[0:HD] for g in both]
        flipped = jnp.concatenate(parts, axis=0)
        copies[i].wait()
        for c in range(3):
            cs = slice(c * 512, (c + 1) * 512)
            t = dot(flipped, held[at[i] : at[i] + count, cs])
            if i == 0:
                acc[:, cs] = t
            else:
                acc[:, cs] += t
    core = pos_ref[SEQ]
    for c in range(4):
        flipped = acc[:, c * 384 : (c + 1) * 384].T
        halves = [[flipped[i * 96 : (i + 1) * 96] for i in (k, k + 2)] for k in range(2)]
        for k in range(2):
            for i in range(2):
                r = slice((c * 2 + i) * 96, (c * 2 + i + 1) * 96)

                @pl.when(core == k)
                def _():
                    keep_ref[r, :] = halves[k][i]

                @pl.when(core != k)
                def _():
                    send_ref[r, :] = halves[k][i].astype(BF)


def add_kernel(me_ref, keep_ref, got_ref, own_ref, *outs):
    for d in range(8):
        rows = pl.ds(pl.multiple_of((me_ref[0] ^ d) * 96, 96), 96)
        t = keep_ref[rows, :] + got_ref[rows, :].astype(F32)
        if d == 0:
            own_ref[...] = t
        else:
            outs[d - 1][...] = t.astype(BF)


def sum_kernel(own_ref, *refs):
    t = own_ref[...]
    for ref in refs[:-1]:
        t = t + ref[...].astype(F32)
    for s in range(SEQ):
        refs[-1][s] = t[s * 12 : (s + 1) * 12]


def join(first, second, part):
    low = lax.broadcasted_iota(jnp.int32, first.shape, first.ndim - 1) < HD
    if part == 0:
        return jnp.where(low, first, pltpu.roll(second, HD, first.ndim - 1))
    return jnp.where(low, pltpu.roll(first, HD, first.ndim - 1), second)


def combine_kernel(parts_ref, out_ref):
    for s in range(SEQ):
        total = parts_ref[s]
        at = s * GW
        low, high = total[:, 0:128], total[:, 128:256]
        out_ref[:, at : at + GW] = total[:, 256:384]
        out_ref[:, 1024 + at : 1024 + at + GW] = join(low, high, 0)
        out_ref[:, 2048 + at : 2048 + at + GW] = join(low, high, 1)


def input_gradient_kernel(
    pos_ref, first_ref, second_ref, w0, w1, w2, w3, x_ref, ctx_ref, out_ref, packed, held, sems
):
    copies = fetch([(w, held.at[f]) for f, w in enumerate((w0, w1, w2, w3))], sems)
    for s in range(SEQ):
        at = s * GW
        a = [first_ref[s, :, i * 128 : (i + 1) * 128].astype(F32) for i in range(2)]
        b = [second_ref[s, :, i * 128 : (i + 1) * 128].astype(F32) for i in range(2)]
        ctx_ref[:, at : at + GW] = join(a[0], b[0], 1).astype(BF)
        packed[:, at : at + GW] = join(a[0], b[0], 0).astype(BF)
        packed[:, 1024 + at : 1024 + at + GW] = join(a[1], b[1], 0).astype(BF)
        packed[:, 2048 + at : 2048 + at + GW] = join(a[1], b[1], 1).astype(BF)
    for f in range(4):
        to = pl.ds(pl.multiple_of(pos_ref[f] * 384, 384), 384)
        copies[f].wait()
        out_ref[:, to] = dot(packed[...], held[f], ((1,), (1,)))
    standard, inv_std = standardize(x_ref[...].astype(F32))
    ng = out_ref[...]
    row_mean = jnp.mean(ng, axis=1, keepdims=True)
    projected = jnp.mean(ng * standard, axis=1, keepdims=True)
    out_ref[...] = inv_std * (ng - row_mean - standard * projected)


def shape(dims, dtype=BF):
    return jax.ShapeDtypeStruct(dims, dtype)


UP = [(i, (i // 4) * 4 + (i % 4 + 1) % 4) for i in range(8)]
DOWN = [(i, (i // 4) * 4 + (i % 4 + 3) % 4) for i in range(8)]
ACROSS = [(i, i ^ 4) for i in range(8)]
SWAP = [(f * 8 + s, (f ^ 1) * 8 + (s ^ 4)) for f in range(2) for s in range(8)]
OFFSETS = [(dz, dy) for dz in range(2) for dy in (0, 3, 1, 2)]
tie = lax.optimization_barrier


def send(v, way):
    return lax.ppermute(v, "seq", way)


def sibling(v):
    return lax.ppermute(v, "core", [(0, 1), (1, 0)])


def swap(v):
    return lax.ppermute(v, ("zh", "seq"), SWAP)


def call(kernel, out, in_specs, flops=0, scratch=(), transcendentals=0, vmem=56):
    return pl.pallas_call(
        kernel,
        out_shape=out,
        in_specs=in_specs,
        out_specs=jax.tree.map(lambda _: VM, out),
        scratch_shapes=list(scratch),
        compiler_params=pltpu.CompilerParams(vmem_limit_bytes=vmem * 2**20),
        cost_estimate=pl.CostEstimate(
            flops=flops, bytes_accessed=2**20, transcendentals=transcendentals
        ),
    )


def body(frames, projection, lengths, cotangent):
    x = frames[0]
    me = lax.axis_index("seq")
    core = lax.axis_index("core")
    fsdp = lax.axis_index("zh") * 2 + core
    half = ROWS // 2
    normed = call(norm_kernel, shape((ROWS, D)), [VM])(x)
    mine = call(columns_kernel, shape((384, 768)), [SM, VM])(
        (me % 4)[None].astype(jnp.int32), projection
    )
    upstream = cotangent[0].reshape(ROWS, SEQ, GW).transpose(1, 0, 2)
    index = [(me // 4 ^ dz) * 4 + (me % 4 + dy) % 4 for dz, dy in OFFSETS]
    place = jnp.stack(index + [core]).astype(jnp.int32)
    owners = jnp.stack([fsdp ^ i for i in range(4)] + [me // 4]).astype(jnp.int32)

    below, above, other = send(normed, UP), send(normed, DOWN), send(normed, ACROSS)
    mine, upstream, place, owners, below, above = tie((mine, upstream, place, owners, below, above))
    over = swap(mine)
    columns = [mine, sibling(mine), over, sibling(over)]
    far = [send(below[:half], UP), send(above[half:], DOWN)]

    def project(rows):
        count = sum(r.shape[0] for r in rows)
        kept, sent = call(
            functools.partial(project_kernel, len(rows)),
            (shape((count, 384)), shape((count, 384))),
            [SM] + [VM] * (4 + len(rows)),
            4 * count * D * 384,
        )(owners, *columns, *rows)
        return kept, send(sent, ACROSS)

    near_kept, near_got = project([normed, below, above])
    far, other, upstream = tie((far, other, upstream))
    far_kept, far_got = project(far)
    upstream = lax.all_to_all(upstream, "seq", 0, 0, tiled=True).reshape(T, GW)
    other_below, other_above = send(other, UP), send(other, DOWN)
    weight, columns[2] = tie((projection, over))
    weight_over = swap(weight)

    def attend(head):
        return call(
            functools.partial(attention_kernel, head),
            shape((T, 256)),
            [SM, SM] + [VM] * 5,
            20 * 2 * T * T * HD,
            [
                pltpu.VMEM((T, 128), BF),
                pltpu.VMEM((T, 128), BF),
                pltpu.VMEM((HD + 16, T), BF),
                pltpu.VMEM((HD, T), BF),
                pltpu.VMEM((HD, T), BF),
                pltpu.VMEM((HD, T), BF),
                pltpu.VMEM((2, T, BQ), F32),
                pltpu.VMEM((2, T, BQ), BF),
                pltpu.VMEM((T, 128), F32),
            ],
            T * T,
        )(place, lengths, near_kept, far_kept, near_got, far_got, upstream)

    def send_back(grads):
        return lax.all_to_all(grads.reshape(SEQ, ROWS, 256), "seq", 0, 0, tiled=True)

    first = attend(0)
    first, other_below, other_above = tie((first, other_below, other_above))
    back0 = send_back(first)
    other_far = [send(other_below[:half], UP), send(other_above[half:], DOWN)]
    weights = [projection, sibling(projection), weight_over, sibling(weight_over)]
    blocks = [normed, below, above, *far, other, other_below, other_above, *other_far]
    second = attend(1)
    second, back0 = tie((second, back0))
    back1 = send_back(second)
    keep, out = call(
        weight_gradient_kernel,
        (shape((768, 384), F32), shape((768, 384))),
        [SM, VM, VM] + [ANY] * len(blocks),
        2 * T * D * 384,
        [
            pltpu.VMEM((384, D), F32),
            pltpu.VMEM((T, D), BF),
            pltpu.SemaphoreType.DMA((len(blocks),)),
        ],
    )(place, first, second, *blocks)
    got = sibling(out)
    group = lax.axis_index("dp") * 2 + lax.axis_index("zh")
    own, *outs = call(
        add_kernel, (shape((96, 384), F32),) + (shape((96, 384)),) * 7, [SM, VM, VM]
    )(group[None].astype(jnp.int32), keep, got)
    outs = [
        lax.ppermute(v, ("dp", "zh"), [(i, i ^ (d + 1)) for i in range(8)])
        for d, v in enumerate(outs)
    ]
    outs, back1 = tie((outs, back1))
    summed = call(sum_kernel, shape((SEQ, 12, 384), F32), [VM] * 8)(own, *outs)
    summed = lax.all_to_all(summed, "seq", 0, 0, tiled=True)
    projection_gradient = call(combine_kernel, shape((12, 3072), F32), [VM])(summed)
    context, input_gradient = call(
        input_gradient_kernel,
        (shape((ROWS, 1024)), shape((ROWS, D), F32)),
        [SM, VM, VM] + [ANY] * 4 + [VM],
        2 * ROWS * D * 3072,
        [
            pltpu.VMEM((ROWS, 3072), BF),
            pltpu.VMEM((4, 384, 3072), BF),
            pltpu.SemaphoreType.DMA((4,)),
        ],
    )(owners, back0, back1, *weights, x)
    return (context[None], input_gradient[None], projection_gradient)


def solution(mesh):
    split = jax.sharding.Mesh(mesh.devices.reshape(4, 2, 2, 8), ("dp", "zh", "core", "seq"))
    record = ("dp", "zh", "core")
    placed = (P(record, "seq", None), P(("zh", "core"), None), P(record), P(record, "seq", None))
    return jax.shard_map(
        body,
        mesh=split,
        in_specs=placed,
        out_specs=(P(record, "seq", None), P(record, "seq", None), P((*record, "seq"), None)),
        check_vma=False,
    )
```

```python
import functools

import jax
import jax.numpy as jnp
from jax import lax
from jax.experimental import pallas as pl
from jax.experimental.pallas import tpu as pltpu
from jax.sharding import PartitionSpec as P

BF = jnp.bfloat16
F32 = jnp.float32
D = 1536
HD = 64
T = 2048
ROWS = 256
SEQ = 8
GW = 128
EPS = 1e-05
BQ = 256
CH = 512
NC = T // CH
VM = pl.BlockSpec(memory_space=pltpu.VMEM)
SM = pl.BlockSpec(memory_space=pltpu.SMEM)
ANY = pl.BlockSpec(memory_space=pl.ANY)


def dot(a, b, dims=((1,), (0,))):
    return lax.dot_general(a, b, (dims, ((), ())), preferred_element_type=F32)


def standardize(x):
    centered = x - jnp.mean(x, axis=1, keepdims=True)
    inv_std = lax.rsqrt(jnp.mean(centered * centered, axis=1, keepdims=True) + EPS)
    return centered * inv_std, inv_std


def fetch(pairs, sems):
    copies = [pltpu.make_async_copy(a, b, sems.at[i]) for i, (a, b) in enumerate(pairs)]
    for copy in copies:
        copy.start()
    return copies


def prepare_kernel(y_ref, x_ref, w_ref, normed_ref, columns_ref, held, sems):
    pairs = []
    for z in range(2):
        for kind in range(3):
            first = pl.multiple_of(kind * 1024 + (z * 4 + y_ref[0]) * GW, GW)
            pairs.append((w_ref.at[:, pl.ds(first, GW)], held.at[z * 3 + kind]))
    copies = fetch(pairs, sems)
    normed_ref[...] = standardize(x_ref[...].astype(F32))[0].astype(BF)
    for copy in copies:
        copy.wait()
    for z in range(2):
        k, v = (held[z * 3 + kind].astype(F32) for kind in (1, 2))
        low = lax.broadcasted_iota(jnp.int32, k.shape, 1) < HD
        at = z * 384
        columns_ref[:, at : at + 128] = jnp.where(low, k, pltpu.roll(v, HD, 1)).astype(BF)
        columns_ref[:, at + 128 : at + 256] = jnp.where(low, pltpu.roll(k, HD, 1), v).astype(BF)
        columns_ref[:, at + 256 : at + 384] = held[z * 3]


def project_kernel(n, owner_ref, group_ref, *refs):
    weights, blocks, out_ref = refs[:4], refs[4 : 4 + n], refs[4 + n]
    cols = pl.ds(pl.multiple_of(group_ref[0] * 384, 384), 384)
    first = 0
    for block in blocks:
        count = block.shape[0]
        total = None
        for f in range(4):
            rows = pl.ds(pl.multiple_of(owner_ref[f] * 384, 384), 384)
            t = dot(block[:, rows], weights[f][:, cols])
            total = t if total is None else total + t
        out_ref[first : first + count, :] = total.astype(BF)
        first += count


def attention_kernel(
    head, pos_ref, len_ref, kept_ref, other_ref, last_ref, up_ref, out_ref, kv, ka, vt, kt, qt, ut, s_ref, e_ref, acc
):
    length = len_ref[0]
    hrows = slice(head * HD, (head + 1) * HD)
    lane = lax.broadcasted_iota(jnp.int32, (BQ, 128), 1)
    for b in range(SEQ):
        r = slice(b * BQ, (b + 1) * BQ)
        source = kept_ref if b < 4 else last_ref if b == 7 else other_ref
        own = slice(b % 4 * BQ, (b % 4 + 1) * BQ) if b < 7 else slice(0, BQ)
        first = pl.multiple_of(pos_ref[b] * BQ, BQ)
        mine = source[own, head * 128 : (head + 1) * 128]
        kv[r, :] = mine
        keys = mine.astype(F32)
        row = lax.broadcasted_iota(jnp.int32, (BQ, 128), 0) + first
        bias = jnp.where(lane == HD, jnp.where(row < length, 0.0, -1e30), 0.0)
        ka[r, :] = jnp.where(lane < HD, keys, bias).astype(BF)
        flipped = keys.T.astype(BF)
        kt[:, r] = flipped[0:HD]
        vt[0:HD, r] = flipped[HD:128]
        vt[HD : HD + 16, r] = jnp.ones((16, BQ), BF)
        qt[:, r] = (source[own, 256:384].astype(F32) * 0.125).T[hrows].astype(BF)
        u = jnp.where(row < length, up_ref[pl.ds(first, BQ), :].astype(F32), 0.0)
        ut[:, r] = u.T[hrows].astype(BF)
    acc[...] = jnp.zeros_like(acc)
    zeros = jnp.zeros((HD, BQ), BF)
    ones_row = jnp.where(lax.broadcasted_iota(jnp.int32, (HD, BQ), 0) == 0, 1.0, 0.0).astype(BF)
    nt = ((1,), (1,))

    def step(i, carry):
        contexts, ups, queries, inners = [], [], [], []
        starts = [pl.multiple_of((2 * i + j) * BQ, BQ) for j in range(2)]
        for j in range(2):
            cols = pl.ds(starts[j], BQ)
            qh = qt[:, cols]
            qa = jnp.concatenate([qh, ones_row], axis=0)
            peak = None
            for c in range(NC):
                r = slice(c * CH, (c + 1) * CH)
                s = dot(ka[r, :], qa)
                s_ref[j, r, :] = s
                t = jnp.max(s.reshape(CH // 8, 8, BQ), axis=0)
                peak = t if peak is None else jnp.maximum(peak, t)
            peak = jnp.max(peak, axis=0, keepdims=True)
            total = None
            for c in range(NC):
                r = slice(c * CH, (c + 1) * CH)
                e = jnp.exp(s_ref[j, r, :] - peak).astype(BF)
                e_ref[j, r, :] = e
                t = dot(vt[:, r], e)
                total = t if total is None else total + t
            inverse = 1.0 / total[HD : HD + 1]
            context = total[0:HD] * inverse
            up = (ut[:, cols].astype(F32) * inverse).astype(BF)
            inner = jnp.sum(up.astype(F32) * context, axis=0, keepdims=True)
            contexts.append(context)
            ups.append(jnp.concatenate([zeros, up], axis=0))
            queries.append(jnp.concatenate([qh, zeros], axis=0))
            inners.append(inner)
        dq = [None, None]
        for c in range(NC):
            r = slice(c * CH, (c + 1) * CH)
            total = acc[r, :]
            for j in range(2):
                dp = dot(kv[r, :], ups[j])
                e = e_ref[j, r, :]
                ds = (e.astype(F32) * (dp - inners[j])).astype(BF)
                t = dot(kt[:, r], ds)
                dq[j] = t if dq[j] is None else dq[j] + t
                total = total + (dot(ds, queries[j], nt) + dot(e, ups[j], nt))
            acc[r, :] = total
        for j in range(2):
            first = pl.multiple_of(pos_ref[2 * i + j] * BQ, BQ)
            col = lax.broadcasted_iota(jnp.int32, (HD, BQ), 1) + first
            context = jnp.where(col < length, contexts[j], 0.0)
            both = jnp.concatenate([dq[j] * 0.125, context], axis=0)
            out_ref[pl.ds(first, BQ), 0:128] = both.T.astype(BF)
        return carry

    lax.fori_loop(0, T // BQ // 2, step, 0)
    for b in range(SEQ):
        rows = pl.ds(pl.multiple_of(pos_ref[b] * BQ, BQ), BQ)
        out_ref[rows, 128:256] = acc[b * BQ : (b + 1) * BQ, :].astype(BF)


def weight_gradient_kernel(pos_ref, first_ref, second_ref, *refs):
    sources, (keep_ref, send_ref, acc, held, sems) = refs[:-5], refs[-5:]
    at = [sum(b.shape[0] for b in sources[:i]) for i in range(len(sources))]
    spots = [pl.ds(a, b.shape[0]) for a, b in zip(at, sources)]
    copies = fetch([(b, held.at[spot]) for b, spot in zip(sources, spots)], sems)
    for i, block in enumerate(sources):
        count = block.shape[0]
        first = pos_ref[at[i] // ROWS] * ROWS + at[i] % ROWS
        rows = pl.ds(pl.multiple_of(first, 128), count)
        both = [g[rows, :].astype(F32).T.astype(BF) for g in (first_ref, second_ref)]
        parts = [g[128:256] for g in both] + [g[0:HD] for g in both]
        flipped = jnp.concatenate(parts, axis=0)
        copies[i].wait()
        for c in range(3):
            cs = slice(c * 512, (c + 1) * 512)
            t = dot(flipped, held[at[i] : at[i] + count, cs])
            if i == 0:
                acc[:, cs] = t
            else:
                acc[:, cs] += t
    core = pos_ref[SEQ]
    for c in range(4):
        flipped = acc[:, c * 384 : (c + 1) * 384].T
        halves = [[flipped[i * 96 : (i + 1) * 96] for i in (k, k + 2)] for k in range(2)]
        for k in range(2):
            for i in range(2):
                r = slice((c * 2 + i) * 96, (c * 2 + i + 1) * 96)

                @pl.when(core == k)
                def _():
                    keep_ref[r, :] = halves[k][i]

                @pl.when(core != k)
                def _():
                    send_ref[r, :] = halves[k][i].astype(BF)


def join(first, second, part):
    low = lax.broadcasted_iota(jnp.int32, first.shape, first.ndim - 1) < HD
    if part == 0:
        return jnp.where(low, first, pltpu.roll(second, HD, first.ndim - 1))
    return jnp.where(low, pltpu.roll(first, HD, first.ndim - 1), second)


def add_kernel(keep_ref, got_ref, out_ref):
    for i in range(64 // 8):
        rows = slice(i * 96, (i + 1) * 96)
        t = keep_ref[rows, :] + got_ref[rows, :].astype(F32)
        for s in range(SEQ):
            out_ref[i * SEQ + s] = t[s * 12 : (s + 1) * 12].astype(BF)


def combine_kernel(parts_ref, out_ref):
    for s in range(SEQ):
        total = None
        for r in range(8):
            t = parts_ref[r * SEQ + s].astype(F32)
            total = t if total is None else total + t
        at = s * GW
        low, high = total[:, 0:128], total[:, 128:256]
        out_ref[:, at : at + GW] = total[:, 256:384]
        out_ref[:, 1024 + at : 1024 + at + GW] = join(low, high, 0)
        out_ref[:, 2048 + at : 2048 + at + GW] = join(low, high, 1)


def input_gradient_kernel(
    pos_ref, first_ref, second_ref, w0, w1, w2, w3, x_ref, ctx_ref, out_ref, packed, held, sems
):
    copies = fetch([(w, held.at[f]) for f, w in enumerate((w0, w1, w2, w3))], sems)
    for s in range(SEQ):
        at = s * GW
        a = [first_ref[s, :, i * 128 : (i + 1) * 128].astype(F32) for i in range(2)]
        b = [second_ref[s, :, i * 128 : (i + 1) * 128].astype(F32) for i in range(2)]
        ctx_ref[:, at : at + GW] = join(a[0], b[0], 1).astype(BF)
        packed[:, at : at + GW] = join(a[0], b[0], 0).astype(BF)
        packed[:, 1024 + at : 1024 + at + GW] = join(a[1], b[1], 0).astype(BF)
        packed[:, 2048 + at : 2048 + at + GW] = join(a[1], b[1], 1).astype(BF)
    for f in range(4):
        to = pl.ds(pl.multiple_of(pos_ref[f] * 384, 384), 384)
        copies[f].wait()
        out_ref[:, to] = dot(packed[...], held[f], ((1,), (1,)))
    standard, inv_std = standardize(x_ref[...].astype(F32))
    ng = out_ref[...]
    row_mean = jnp.mean(ng, axis=1, keepdims=True)
    projected = jnp.mean(ng * standard, axis=1, keepdims=True)
    out_ref[...] = inv_std * (ng - row_mean - standard * projected)


def shape(dims, dtype=BF):
    return jax.ShapeDtypeStruct(dims, dtype)


UP = [(i, (i // 4) * 4 + (i % 4 + 1) % 4) for i in range(8)]
DOWN = [(i, (i // 4) * 4 + (i % 4 + 3) % 4) for i in range(8)]
ACROSS = [(i, i ^ 4) for i in range(8)]
SWAP = [(f * 8 + s, (f ^ 1) * 8 + (s ^ 4)) for f in range(2) for s in range(8)]
OFFSETS = [(dz, dy) for dz in range(2) for dy in (0, 3, 1, 2)]
HEAD_FLOPS = (10**9, 10**10)
tie = lax.optimization_barrier


def send(v, way):
    return lax.ppermute(v, "seq", way)


def sibling(v):
    return lax.ppermute(v, "core", [(0, 1), (1, 0)])


def swap(v):
    return lax.ppermute(v, ("zh", "seq"), SWAP)


def call(kernel, out, in_specs, flops=0, scratch=(), transcendentals=0, vmem=56):
    return pl.pallas_call(
        kernel,
        out_shape=out,
        in_specs=in_specs,
        out_specs=jax.tree.map(lambda _: VM, out),
        scratch_shapes=list(scratch),
        compiler_params=pltpu.CompilerParams(vmem_limit_bytes=vmem * 2**20),
        cost_estimate=pl.CostEstimate(
            flops=flops, bytes_accessed=2**20, transcendentals=transcendentals
        ),
    )


def body(frames, projection, lengths, cotangent):
    x = frames[0]
    me = lax.axis_index("seq")
    core = lax.axis_index("core")
    fsdp = lax.axis_index("zh") * 2 + core
    half = ROWS // 2
    normed, mine = call(
        prepare_kernel,
        (shape((ROWS, D)), shape((384, 768))),
        [SM, VM, ANY],
        scratch=[pltpu.VMEM((6, 384, GW), BF), pltpu.SemaphoreType.DMA((6,))],
    )((me % 4)[None].astype(jnp.int32), x, projection)
    upstream = cotangent[0].reshape(ROWS, SEQ, GW).transpose(1, 0, 2)
    index = [(me // 4 ^ dz) * 4 + (me % 4 + dy) % 4 for dz, dy in OFFSETS]
    place = jnp.stack(index + [core]).astype(jnp.int32)
    owners = jnp.stack([fsdp ^ i for i in range(4)]).astype(jnp.int32)

    below, above, other = send(normed, UP), send(normed, DOWN), send(normed, ACROSS)
    over, beside = swap(mine), sibling(mine)
    upstream, place, owners, below, above, other, over, beside = tie(
        (upstream, place, owners, below, above, other, over, beside)
    )
    far = [send(below[:half], UP), send(above[half:], DOWN)]
    columns = [mine, beside, over, sibling(over)]

    def project(rows, group):
        count = sum(r.shape[0] for r in rows)
        return call(
            functools.partial(project_kernel, len(rows)),
            shape((count, 384)),
            [SM, SM] + [VM] * (4 + len(rows)),
            2 * count * D * 384,
        )(owners, group, *columns, *rows)

    here = (me // 4)[None].astype(jnp.int32)
    near = project([normed, below, above], 1 - here)
    _, far, other, upstream = tie((near, far, other, upstream))
    near_got = send(near, ACROSS)
    upstream = lax.all_to_all(upstream, "seq", 0, 0, tiled=True).reshape(T, GW)
    other_below, other_above = send(other, UP), send(other, DOWN)
    last = project(far, 1 - here)
    last, far, weight = tie((last, far, projection))
    far_got = send(last, ACROSS)
    kept = project([normed, below, above, *far], here)
    weight_over = swap(weight)

    def attend(head):
        return call(
            functools.partial(attention_kernel, head),
            shape((T, 256)),
            [SM, SM] + [VM] * 4,
            HEAD_FLOPS[head],
            [
                pltpu.VMEM((T, 128), BF),
                pltpu.VMEM((T, 128), BF),
                pltpu.VMEM((HD + 16, T), BF),
                pltpu.VMEM((HD, T), BF),
                pltpu.VMEM((HD, T), BF),
                pltpu.VMEM((HD, T), BF),
                pltpu.VMEM((2, T, BQ), F32),
                pltpu.VMEM((2, T, BQ), BF),
                pltpu.VMEM((T, 128), F32),
            ],
            T * T,
        )(place, lengths, kept, near_got, far_got, upstream)

    def send_back(grads):
        return lax.all_to_all(grads.reshape(SEQ, ROWS, 256), "seq", 0, 0, tiled=True)

    first = attend(0)
    first, other_below, other_above, weight = tie((first, other_below, other_above, weight))
    back0 = send_back(first)
    other_far = [send(other_below[:half], UP), send(other_above[half:], DOWN)]
    beside = sibling(weight)
    second = attend(1)
    second, back0, weight_over, beside, other_far = tie(
        (second, back0, weight_over, beside, other_far)
    )
    blocks = [normed, below, above, *far, other, other_below, other_above, *other_far]
    back1 = send_back(second)
    keep, out = call(
        weight_gradient_kernel,
        (shape((768, 384), F32), shape((768, 384))),
        [SM, VM, VM] + [ANY] * len(blocks),
        2 * T * D * 384,
        [
            pltpu.VMEM((384, D), F32),
            pltpu.VMEM((T, D), BF),
            pltpu.SemaphoreType.DMA((len(blocks),)),
        ],
    )(place, first, second, *blocks)
    got = sibling(out)
    partial = call(add_kernel, shape((64, 12, 384)), [VM, VM])(keep, got)
    partial, back1, weight_over = tie((partial, back1, weight_over))
    weights = [projection, beside, weight_over, sibling(weight_over)]
    partial = lax.all_to_all(partial, ("dp", "zh", "seq"), 0, 0, tiled=True)
    context, input_gradient = call(
        input_gradient_kernel,
        (shape((ROWS, 1024)), shape((ROWS, D), F32)),
        [SM, VM, VM] + [ANY] * 4 + [VM],
        2 * ROWS * D * 3072,
        [
            pltpu.VMEM((ROWS, 3072), BF),
            pltpu.VMEM((4, 384, 3072), BF),
            pltpu.SemaphoreType.DMA((4,)),
        ],
    )(owners, back0, back1, *weights, x)
    partial, context, input_gradient = tie((partial, context, input_gradient))
    projection_gradient = call(combine_kernel, shape((12, 3072), F32), [VM])(partial)
    return (context[None], input_gradient[None], projection_gradient)


def solution(mesh):
    split = jax.sharding.Mesh(mesh.devices.reshape(4, 2, 2, 8), ("dp", "zh", "core", "seq"))
    record = ("dp", "zh", "core")
    placed = (P(record, "seq", None), P(("zh", "core"), None), P(record), P(record, "seq", None))
    return jax.shard_map(
        body,
        mesh=split,
        in_specs=placed,
        out_specs=(P(record, "seq", None), P(record, "seq", None), P((*record, "seq"), None)),
        check_vma=False,
    )
```

```python
import functools

import jax
import jax.numpy as jnp
from jax import lax
from jax.experimental import pallas as pl
from jax.experimental.pallas import tpu as pltpu
from jax.sharding import PartitionSpec as P

BF = jnp.bfloat16
F32 = jnp.float32
D = 1536
HD = 64
T = 2048
ROWS = 256
SEQ = 8
GW = 128
EPS = 1e-05
BQ = 256
CH = 512
NC = T // CH
VM = pl.BlockSpec(memory_space=pltpu.VMEM)
SM = pl.BlockSpec(memory_space=pltpu.SMEM)
ANY = pl.BlockSpec(memory_space=pl.ANY)


def dot(a, b, dims=((1,), (0,))):
    return lax.dot_general(a, b, (dims, ((), ())), preferred_element_type=F32)


def standardize(x):
    centered = x - jnp.mean(x, axis=1, keepdims=True)
    inv_std = lax.rsqrt(jnp.mean(centered * centered, axis=1, keepdims=True) + EPS)
    return centered * inv_std, inv_std


def fetch(pairs, sems):
    copies = [pltpu.make_async_copy(a, b, sems.at[i]) for i, (a, b) in enumerate(pairs)]
    for copy in copies:
        copy.start()
    return copies


def prepare_kernel(y_ref, x_ref, w_ref, normed_ref, columns_ref, held, sems):
    pairs = []
    for z in range(2):
        for kind in range(3):
            first = pl.multiple_of(kind * 1024 + (z * 4 + y_ref[0]) * GW, GW)
            pairs.append((w_ref.at[:, pl.ds(first, GW)], held.at[z * 3 + kind]))
    copies = fetch(pairs, sems)
    normed_ref[...] = standardize(x_ref[...].astype(F32))[0].astype(BF)
    for copy in copies:
        copy.wait()
    for z in range(2):
        k, v = (held[z * 3 + kind].astype(F32) for kind in (1, 2))
        low = lax.broadcasted_iota(jnp.int32, k.shape, 1) < HD
        at = z * 384
        columns_ref[:, at : at + 128] = jnp.where(low, k, pltpu.roll(v, HD, 1)).astype(BF)
        columns_ref[:, at + 128 : at + 256] = jnp.where(low, pltpu.roll(k, HD, 1), v).astype(BF)
        columns_ref[:, at + 256 : at + 384] = held[z * 3]


def project_kernel(n, owner_ref, group_ref, *refs):
    weights, blocks, outs = refs[:4], refs[4 : 4 + n], refs[4 + n :]
    for j, out_ref in enumerate(outs):
        cols = pl.ds(pl.multiple_of(group_ref[j] * 384, 384), 384)
        first = 0
        for block in blocks:
            count = block.shape[0]
            total = None
            for f in range(4):
                rows = pl.ds(pl.multiple_of(owner_ref[f] * 384, 384), 384)
                t = dot(block[:, rows], weights[f][:, cols])
                total = t if total is None else total + t
            out_ref[first : first + count, :] = total.astype(BF)
            first += count


def attention_kernel(
    head, pos_ref, len_ref, kept_ref, far_ref, other_ref, last_ref, up_ref, out_ref, kv, ka, vt, kt, qt, ut, s_ref, e_ref, acc
):
    length = len_ref[0]
    hrows = slice(head * HD, (head + 1) * HD)
    lane = lax.broadcasted_iota(jnp.int32, (BQ, 128), 1)
    for b in range(SEQ):
        r = slice(b * BQ, (b + 1) * BQ)
        source, at = (
            (kept_ref, 0), (kept_ref, 1), (kept_ref, 2), (far_ref, 0),
            (kept_ref, 3), (other_ref, 0), (other_ref, 1), (last_ref, 0),
        )[b]
        own = slice(at * BQ, (at + 1) * BQ)
        first = pl.multiple_of(pos_ref[b] * BQ, BQ)
        mine = source[own, head * 128 : (head + 1) * 128]
        kv[r, :] = mine
        keys = mine.astype(F32)
        row = lax.broadcasted_iota(jnp.int32, (BQ, 128), 0) + first
        bias = jnp.where(lane == HD, jnp.where(row < length, 0.0, -1e30), 0.0)
        ka[r, :] = jnp.where(lane < HD, keys, bias).astype(BF)
        flipped = keys.T.astype(BF)
        kt[:, r] = flipped[0:HD]
        vt[0:HD, r] = flipped[HD:128]
        vt[HD : HD + 16, r] = jnp.ones((16, BQ), BF)
        qt[:, r] = (source[own, 256:384].astype(F32) * 0.125).T[hrows].astype(BF)
        u = jnp.where(row < length, up_ref[pl.ds(first, BQ), :].astype(F32), 0.0)
        ut[:, r] = u.T[hrows].astype(BF)
    acc[...] = jnp.zeros_like(acc)
    zeros = jnp.zeros((HD, BQ), BF)
    ones_row = jnp.where(lax.broadcasted_iota(jnp.int32, (HD, BQ), 0) == 0, 1.0, 0.0).astype(BF)
    nt = ((1,), (1,))

    def step(i, carry):
        contexts, ups, queries, inners = [], [], [], []
        starts = [pl.multiple_of((2 * i + j) * BQ, BQ) for j in range(2)]
        for j in range(2):
            cols = pl.ds(starts[j], BQ)
            qh = qt[:, cols]
            qa = jnp.concatenate([qh, ones_row], axis=0)
            peak = None
            for c in range(NC):
                r = slice(c * CH, (c + 1) * CH)
                s = dot(ka[r, :], qa)
                s_ref[j, r, :] = s
                t = jnp.max(s.reshape(CH // 8, 8, BQ), axis=0)
                peak = t if peak is None else jnp.maximum(peak, t)
            peak = jnp.max(peak, axis=0, keepdims=True)
            total = None
            for c in range(NC):
                r = slice(c * CH, (c + 1) * CH)
                e = jnp.exp(s_ref[j, r, :] - peak).astype(BF)
                e_ref[j, r, :] = e
                t = dot(vt[:, r], e)
                total = t if total is None else total + t
            inverse = 1.0 / total[HD : HD + 1]
            context = total[0:HD] * inverse
            up = (ut[:, cols].astype(F32) * inverse).astype(BF)
            inner = jnp.sum(up.astype(F32) * context, axis=0, keepdims=True)
            contexts.append(context)
            ups.append(jnp.concatenate([zeros, up], axis=0))
            queries.append(jnp.concatenate([qh, zeros], axis=0))
            inners.append(inner)
        dq = [None, None]
        for c in range(NC):
            r = slice(c * CH, (c + 1) * CH)
            total = acc[r, :]
            for j in range(2):
                dp = dot(kv[r, :], ups[j])
                e = e_ref[j, r, :]
                ds = (e.astype(F32) * (dp - inners[j])).astype(BF)
                t = dot(kt[:, r], ds)
                dq[j] = t if dq[j] is None else dq[j] + t
                total = total + (dot(ds, queries[j], nt) + dot(e, ups[j], nt))
            acc[r, :] = total
        for j in range(2):
            first = pl.multiple_of(pos_ref[2 * i + j] * BQ, BQ)
            col = lax.broadcasted_iota(jnp.int32, (HD, BQ), 1) + first
            context = jnp.where(col < length, contexts[j], 0.0)
            both = jnp.concatenate([dq[j] * 0.125, context], axis=0)
            out_ref[pl.ds(first, BQ), 0:128] = both.T.astype(BF)
        return carry

    lax.fori_loop(0, T // BQ // 2, step, 0)
    for b in range(SEQ):
        rows = pl.ds(pl.multiple_of(pos_ref[b] * BQ, BQ), BQ)
        out_ref[rows, 128:256] = acc[b * BQ : (b + 1) * BQ, :].astype(BF)


def weight_gradient_kernel(pos_ref, first_ref, second_ref, *refs):
    sources, (keep_ref, send_ref, flipped_ref, held, sems) = refs[:-5], refs[-5:]
    at = [sum(b.shape[0] for b in sources[:i]) for i in range(len(sources))]
    spots = [pl.ds(a, b.shape[0]) for a, b in zip(at, sources)]
    copies = fetch([(b, held.at[spot]) for b, spot in zip(sources, spots)], sems)
    for b in range(SEQ):
        rows = pl.ds(pl.multiple_of(pos_ref[b] * ROWS, ROWS), ROWS)
        cols = slice(b * ROWS, (b + 1) * ROWS)
        both = [g[rows, :].astype(F32).T.astype(BF) for g in (first_ref, second_ref)]
        parts = [g[128:256] for g in both] + [g[0:HD] for g in both]
        flipped_ref[:, cols] = jnp.concatenate(parts, axis=0)
    for copy in copies:
        copy.wait()
    core = pos_ref[SEQ]
    for c in range(4):
        flipped = dot(flipped_ref[...], held[:, c * 384 : (c + 1) * 384]).T
        halves = [[flipped[i * 96 : (i + 1) * 96] for i in (k, k + 2)] for k in range(2)]
        for k in range(2):
            for i in range(2):
                r = slice((c * 2 + i) * 96, (c * 2 + i + 1) * 96)

                @pl.when(core == k)
                def _():
                    keep_ref[r, :] = halves[k][i]

                @pl.when(core != k)
                def _():
                    send_ref[r, :] = halves[k][i].astype(BF)


def join(first, second, part):
    low = lax.broadcasted_iota(jnp.int32, first.shape, first.ndim - 1) < HD
    if part == 0:
        return jnp.where(low, first, pltpu.roll(second, HD, first.ndim - 1))
    return jnp.where(low, pltpu.roll(first, HD, first.ndim - 1), second)


def add_kernel(keep_ref, got_ref, out_ref):
    for i in range(64 // 8):
        rows = slice(i * 96, (i + 1) * 96)
        t = keep_ref[rows, :] + got_ref[rows, :].astype(F32)
        for s in range(SEQ):
            out_ref[i * SEQ + s] = t[s * 12 : (s + 1) * 12].astype(BF)


def combine_kernel(parts_ref, out_ref):
    for s in range(SEQ):
        total = None
        for r in range(8):
            t = parts_ref[r * SEQ + s].astype(F32)
            total = t if total is None else total + t
        at = s * GW
        low, high = total[:, 0:128], total[:, 128:256]
        out_ref[:, at : at + GW] = total[:, 256:384]
        out_ref[:, 1024 + at : 1024 + at + GW] = join(low, high, 0)
        out_ref[:, 2048 + at : 2048 + at + GW] = join(low, high, 1)


def input_gradient_kernel(
    pos_ref, first_ref, second_ref, w0, w1, w2, w3, x_ref, ctx_ref, out_ref, packed, held, sems
):
    copies = fetch([(w, held.at[f]) for f, w in enumerate((w0, w1, w2, w3))], sems)
    for s in range(SEQ):
        at = s * GW
        a = [first_ref[s, :, i * 128 : (i + 1) * 128].astype(F32) for i in range(2)]
        b = [second_ref[s, :, i * 128 : (i + 1) * 128].astype(F32) for i in range(2)]
        ctx_ref[:, at : at + GW] = join(a[0], b[0], 1).astype(BF)
        packed[:, at : at + GW] = join(a[0], b[0], 0).astype(BF)
        packed[:, 1024 + at : 1024 + at + GW] = join(a[1], b[1], 0).astype(BF)
        packed[:, 2048 + at : 2048 + at + GW] = join(a[1], b[1], 1).astype(BF)
    for f in range(4):
        to = pl.ds(pl.multiple_of(pos_ref[f] * 384, 384), 384)
        copies[f].wait()
        out_ref[:, to] = dot(packed[...], held[f], ((1,), (1,)))
    standard, inv_std = standardize(x_ref[...].astype(F32))
    ng = out_ref[...]
    row_mean = jnp.mean(ng, axis=1, keepdims=True)
    projected = jnp.mean(ng * standard, axis=1, keepdims=True)
    out_ref[...] = inv_std * (ng - row_mean - standard * projected)


def shape(dims, dtype=BF):
    return jax.ShapeDtypeStruct(dims, dtype)


UP = [(i, (i // 4) * 4 + (i % 4 + 1) % 4) for i in range(8)]
DOWN = [(i, (i // 4) * 4 + (i % 4 + 3) % 4) for i in range(8)]
FAR = [(i, (i // 4) * 4 + (i % 4 + 2) % 4) for i in range(8)]
ACROSS = [(i, i ^ 4) for i in range(8)]
SWAP = [(f * 8 + s, (f ^ 1) * 8 + (s ^ 4)) for f in range(2) for s in range(8)]
OFFSETS = [(dz, dy) for dz in range(2) for dy in (0, 3, 1, 2)]
HEAD_FLOPS = (10**9, 10**10)
tie = lax.optimization_barrier


def send(v, way):
    return lax.ppermute(v, "seq", way)


def sibling(v):
    return lax.ppermute(v, "core", [(0, 1), (1, 0)])


def swap(v):
    return lax.ppermute(v, ("zh", "seq"), SWAP)


def call(kernel, out, in_specs, flops=0, scratch=(), transcendentals=0, vmem=56):
    return pl.pallas_call(
        kernel,
        out_shape=out,
        in_specs=in_specs,
        out_specs=jax.tree.map(lambda _: VM, out),
        scratch_shapes=list(scratch),
        compiler_params=pltpu.CompilerParams(vmem_limit_bytes=vmem * 2**20),
        cost_estimate=pl.CostEstimate(
            flops=flops, bytes_accessed=2**20, transcendentals=transcendentals
        ),
    )


def body(frames, projection, lengths, cotangent):
    x = frames[0]
    me = lax.axis_index("seq")
    core = lax.axis_index("core")
    fsdp = lax.axis_index("zh") * 2 + core
    half = ROWS // 2
    normed, mine = call(
        prepare_kernel,
        (shape((ROWS, D)), shape((384, 768))),
        [SM, VM, ANY],
        scratch=[pltpu.VMEM((6, 384, GW), BF), pltpu.SemaphoreType.DMA((6,))],
    )((me % 4)[None].astype(jnp.int32), x, projection)
    upstream = cotangent[0].reshape(ROWS, SEQ, GW).transpose(1, 0, 2)
    index = [(me // 4 ^ dz) * 4 + (me % 4 + dy) % 4 for dz, dy in OFFSETS]
    place = jnp.stack(index + [core]).astype(jnp.int32)
    owners = jnp.stack([fsdp ^ i for i in range(4)]).astype(jnp.int32)

    below, above, other = send(normed, UP), send(normed, DOWN), send(normed, ACROSS)
    over, beside = swap(mine), sibling(mine)
    upstream, place, owners, below, above, other, over, beside = tie(
        (upstream, place, owners, below, above, other, over, beside)
    )
    far = [send(below[:half], UP), send(above[half:], DOWN)]
    columns = [mine, beside, over, sibling(over)]

    def project(rows, groups, count):
        height = sum(r.shape[0] for r in rows)
        return call(
            functools.partial(project_kernel, len(rows)),
            (shape((height, 384)),) * count,
            [SM, SM] + [VM] * (4 + len(rows)),
        )(owners, groups, *columns, *rows)

    here = me // 4
    groups = jnp.stack([1 - here, here]).astype(jnp.int32)
    (near,) = project([below, above], groups, 1)
    near_got = send(near, ACROSS)
    _, upstream, turned = tie((near, upstream, groups[::-1]))
    (kept,) = project([normed, below, above, other], turned, 1)
    upstream = lax.all_to_all(upstream, "seq", 0, 0, tiled=True).reshape(T, GW)
    _, far = tie((kept, far))
    last, far_kept = project(far, groups, 2)
    far_got = send(last, ACROSS)
    _, weight, other_late = tie((last, projection, other))
    other_below, other_above = send(other_late, UP), send(other_late, DOWN)
    other_far = send(other_late, FAR)
    weight_over = swap(weight)

    def attend(head):
        return call(
            functools.partial(attention_kernel, head),
            shape((T, 256)),
            [SM, SM] + [VM] * 5,
            HEAD_FLOPS[head],
            [
                pltpu.VMEM((T, 128), BF),
                pltpu.VMEM((T, 128), BF),
                pltpu.VMEM((HD + 16, T), BF),
                pltpu.VMEM((HD, T), BF),
                pltpu.VMEM((HD, T), BF),
                pltpu.VMEM((HD, T), BF),
                pltpu.VMEM((2, T, BQ), F32),
                pltpu.VMEM((2, T, BQ), BF),
                pltpu.VMEM((T, 128), F32),
            ],
            T * T,
        )(place, lengths, kept, far_kept, near_got, far_got, upstream)

    def send_back(grads):
        return lax.all_to_all(grads.reshape(SEQ, ROWS, 256), "seq", 0, 0, tiled=True)

    first = attend(0)
    first, weight = tie((first, weight))
    back0 = send_back(first)
    beside = sibling(weight)
    second = attend(1)
    second, back0, weight_over, beside, other_below, other_above, other_far = tie(
        (second, back0, weight_over, beside, other_below, other_above, other_far)
    )
    blocks = [normed, below, above, *far, other, other_below, other_above, other_far]
    back1 = send_back(second)
    keep, out = call(
        weight_gradient_kernel,
        (shape((768, 384), F32), shape((768, 384))),
        [SM, VM, VM] + [ANY] * len(blocks),
        2 * T * D * 384,
        [
            pltpu.VMEM((384, T), BF),
            pltpu.VMEM((T, D), BF),
            pltpu.SemaphoreType.DMA((len(blocks),)),
        ],
    )(place, first, second, *blocks)
    got = sibling(out)
    partial = call(add_kernel, shape((64, 12, 384)), [VM, VM])(keep, got)
    partial, back1, weight_over = tie((partial, back1, weight_over))
    weights = [projection, beside, weight_over, sibling(weight_over)]
    partial = lax.all_to_all(partial, ("dp", "zh", "seq"), 0, 0, tiled=True)
    context, input_gradient = call(
        input_gradient_kernel,
        (shape((ROWS, 1024)), shape((ROWS, D), F32)),
        [SM, VM, VM] + [ANY] * 4 + [VM],
        2 * ROWS * D * 3072,
        [
            pltpu.VMEM((ROWS, 3072), BF),
            pltpu.VMEM((4, 384, 3072), BF),
            pltpu.SemaphoreType.DMA((4,)),
        ],
    )(owners, back0, back1, *weights, x)
    partial, context, input_gradient = tie((partial, context, input_gradient))
    projection_gradient = call(combine_kernel, shape((12, 3072), F32), [VM])(partial)
    return (context[None], input_gradient[None], projection_gradient)


def solution(mesh):
    split = jax.sharding.Mesh(mesh.devices.reshape(4, 2, 2, 8), ("dp", "zh", "core", "seq"))
    record = ("dp", "zh", "core")
    placed = (P(record, "seq", None), P(("zh", "core"), None), P(record), P(record, "seq", None))
    return jax.shard_map(
        body,
        mesh=split,
        in_specs=placed,
        out_specs=(P(record, "seq", None), P(record, "seq", None), P((*record, "seq"), None)),
        check_vma=False,
    )
```

```python
import functools

import jax
import jax.numpy as jnp
from jax import lax
from jax.experimental import pallas as pl
from jax.experimental.pallas import tpu as pltpu
from jax.sharding import PartitionSpec as P

BF = jnp.bfloat16
F32 = jnp.float32
D = 1536
HD = 64
T = 2048
ROWS = 256
SEQ = 8
GW = 128
EPS = 1e-05
BQ = 256
CH = 512
NC = T // CH
VM = pl.BlockSpec(memory_space=pltpu.VMEM)
SM = pl.BlockSpec(memory_space=pltpu.SMEM)
ANY = pl.BlockSpec(memory_space=pl.ANY)


def dot(a, b, dims=((1,), (0,))):
    return lax.dot_general(a, b, (dims, ((), ())), preferred_element_type=F32)


def standardize(x):
    centered = x - jnp.mean(x, axis=1, keepdims=True)
    inv_std = lax.rsqrt(jnp.mean(centered * centered, axis=1, keepdims=True) + EPS)
    return centered * inv_std, inv_std


def fetch(pairs, sems):
    copies = [pltpu.make_async_copy(a, b, sems.at[i]) for i, (a, b) in enumerate(pairs)]
    for copy in copies:
        copy.start()
    return copies


def prepare_kernel(y_ref, x_ref, w_ref, normed_ref, columns_ref, held, sems):
    pairs = []
    for z in range(2):
        for kind in range(3):
            first = pl.multiple_of(kind * 1024 + (z * 4 + y_ref[0]) * GW, GW)
            pairs.append((w_ref.at[:, pl.ds(first, GW)], held.at[z * 3 + kind]))
    copies = fetch(pairs, sems)
    normed_ref[...] = standardize(x_ref[...].astype(F32))[0].astype(BF)
    for copy in copies:
        copy.wait()
    for z in range(2):
        k, v = (held[z * 3 + kind].astype(F32) for kind in (1, 2))
        low = lax.broadcasted_iota(jnp.int32, k.shape, 1) < HD
        at = z * 384
        columns_ref[:, at : at + 128] = jnp.where(low, k, pltpu.roll(v, HD, 1)).astype(BF)
        columns_ref[:, at + 128 : at + 256] = jnp.where(low, pltpu.roll(k, HD, 1), v).astype(BF)
        columns_ref[:, at + 256 : at + 384] = held[z * 3]


def project_kernel(n, owner_ref, group_ref, *refs):
    weights, blocks, outs = refs[:4], refs[4 : 4 + n], refs[4 + n :]
    for j, out_ref in enumerate(outs):
        cols = pl.ds(pl.multiple_of(group_ref[j] * 384, 384), 384)
        first = 0
        for block in blocks:
            count = block.shape[0]
            total = None
            for f in range(4):
                rows = pl.ds(pl.multiple_of(owner_ref[f] * 384, 384), 384)
                t = dot(block[:, rows], weights[f][:, cols])
                total = t if total is None else total + t
            out_ref[first : first + count, :] = total.astype(BF)
            first += count


def attention_kernel(
    head, pos_ref, len_ref, kept_ref, far_ref, other_ref, last_ref, up_ref, out_ref, kv, ka, vt, kt, qt, ut, s_ref, e_ref, acc
):
    length = len_ref[0]
    hrows = slice(head * HD, (head + 1) * HD)
    lane = lax.broadcasted_iota(jnp.int32, (BQ, 128), 1)
    for b in range(SEQ):
        r = slice(b * BQ, (b + 1) * BQ)
        source, at = (
            (kept_ref, 0), (kept_ref, 1), (kept_ref, 2), (far_ref, 0),
            (kept_ref, 3), (other_ref, 0), (other_ref, 1), (last_ref, 0),
        )[b]
        own = slice(at * BQ, (at + 1) * BQ)
        first = pl.multiple_of(pos_ref[b] * BQ, BQ)
        mine = source[own, head * 128 : (head + 1) * 128]
        kv[r, :] = mine
        keys = mine.astype(F32)
        row = lax.broadcasted_iota(jnp.int32, (BQ, 128), 0) + first
        bias = jnp.where(lane == HD, jnp.where(row < length, 0.0, -1e30), 0.0)
        ka[r, :] = jnp.where(lane < HD, keys, bias).astype(BF)
        flipped = keys.T.astype(BF)
        kt[:, r] = flipped[0:HD]
        vt[0:HD, r] = flipped[HD:128]
        vt[HD : HD + 16, r] = jnp.ones((16, BQ), BF)
        qt[:, r] = (source[own, 256:384].astype(F32) * 0.125).T[hrows].astype(BF)
        u = jnp.where(row < length, up_ref[pl.ds(first, BQ), :].astype(F32), 0.0)
        ut[:, r] = u.T[hrows].astype(BF)
    acc[...] = jnp.zeros_like(acc)
    zeros = jnp.zeros((HD, BQ), BF)
    ones_row = jnp.where(lax.broadcasted_iota(jnp.int32, (HD, BQ), 0) == 0, 1.0, 0.0).astype(BF)
    nt = ((1,), (1,))

    def step(i, carry):
        contexts, ups, queries, inners = [], [], [], []
        starts = [pl.multiple_of((2 * i + j) * BQ, BQ) for j in range(2)]
        for j in range(2):
            cols = pl.ds(starts[j], BQ)
            qh = qt[:, cols]
            qa = jnp.concatenate([qh, ones_row], axis=0)
            peak = None
            for c in range(NC):
                r = slice(c * CH, (c + 1) * CH)
                s = dot(ka[r, :], qa)
                s_ref[j, r, :] = s
                t = jnp.max(s.reshape(CH // 8, 8, BQ), axis=0)
                peak = t if peak is None else jnp.maximum(peak, t)
            peak = jnp.max(peak, axis=0, keepdims=True)
            total = None
            for c in range(NC):
                r = slice(c * CH, (c + 1) * CH)
                e = jnp.exp(s_ref[j, r, :] - peak).astype(BF)
                e_ref[j, r, :] = e
                t = dot(vt[:, r], e)
                total = t if total is None else total + t
            inverse = 1.0 / total[HD : HD + 1]
            context = total[0:HD] * inverse
            up = (ut[:, cols].astype(F32) * inverse).astype(BF)
            inner = jnp.sum(up.astype(F32) * context, axis=0, keepdims=True)
            contexts.append(context)
            ups.append(jnp.concatenate([zeros, up], axis=0))
            queries.append(jnp.concatenate([qh, zeros], axis=0))
            inners.append(inner)
        dq = [None, None]
        for c in range(NC):
            r = slice(c * CH, (c + 1) * CH)
            total = acc[r, :]
            for j in range(2):
                dp = dot(kv[r, :], ups[j])
                e = e_ref[j, r, :]
                ds = (e.astype(F32) * (dp - inners[j])).astype(BF)
                t = dot(kt[:, r], ds)
                dq[j] = t if dq[j] is None else dq[j] + t
                total = total + (dot(ds, queries[j], nt) + dot(e, ups[j], nt))
            acc[r, :] = total
        for j in range(2):
            first = pl.multiple_of(pos_ref[2 * i + j] * BQ, BQ)
            col = lax.broadcasted_iota(jnp.int32, (HD, BQ), 1) + first
            context = jnp.where(col < length, contexts[j], 0.0)
            both = jnp.concatenate([dq[j] * 0.125, context], axis=0)
            out_ref[pl.ds(first, BQ), 0:128] = both.T.astype(BF)
        return carry

    lax.fori_loop(0, T // BQ // 2, step, 0)
    for b in range(SEQ):
        rows = pl.ds(pl.multiple_of(pos_ref[b] * BQ, BQ), BQ)
        out_ref[rows, 128:256] = acc[b * BQ : (b + 1) * BQ, :].astype(BF)


def weight_gradient_kernel(pos_ref, first_ref, second_ref, *refs):
    sources, (keep_ref, send_ref, flipped_ref, held, acc, sems) = refs[:-6], refs[-6:]
    at = [sum(b.shape[0] for b in sources[:i]) for i in range(len(sources))]
    spots = [pl.ds(a, b.shape[0]) for a, b in zip(at, sources)]
    copies = fetch([(b, held.at[spot]) for b, spot in zip(sources, spots)], sems)
    for b in range(SEQ):
        rows = pl.ds(pl.multiple_of(pos_ref[b] * ROWS, ROWS), ROWS)
        cols = slice(b * ROWS, (b + 1) * ROWS)
        both = [g[rows, :].astype(F32).T.astype(BF) for g in (first_ref, second_ref)]
        parts = [g[128:256] for g in both] + [g[0:HD] for g in both]
        flipped_ref[:, cols] = jnp.concatenate(parts, axis=0)
    for half in range(2):
        rows = slice(half * T // 2, (half + 1) * T // 2)
        for i, copy in enumerate(copies):
            if at[i] // (T // 2) == half:
                copy.wait()
        for c in range(3):
            cs = slice(c * 512, (c + 1) * 512)
            t = dot(flipped_ref[:, rows], held[rows, cs])
            acc[:, cs] = t if half == 0 else acc[:, cs] + t
    core = pos_ref[SEQ]
    for c in range(4):
        flipped = acc[:, c * 384 : (c + 1) * 384].T
        halves = [[flipped[i * 96 : (i + 1) * 96] for i in (k, k + 2)] for k in range(2)]
        for k in range(2):
            for i in range(2):
                r = slice((c * 2 + i) * 96, (c * 2 + i + 1) * 96)

                @pl.when(core == k)
                def _():
                    keep_ref[r, :] = halves[k][i]

                @pl.when(core != k)
                def _():
                    send_ref[r, :] = halves[k][i].astype(BF)


def join(first, second, part):
    low = lax.broadcasted_iota(jnp.int32, first.shape, first.ndim - 1) < HD
    if part == 0:
        return jnp.where(low, first, pltpu.roll(second, HD, first.ndim - 1))
    return jnp.where(low, pltpu.roll(first, HD, first.ndim - 1), second)


def add_kernel(keep_ref, got_ref, out_ref):
    for i in range(64 // 8):
        rows = slice(i * 96, (i + 1) * 96)
        t = keep_ref[rows, :] + got_ref[rows, :].astype(F32)
        for s in range(SEQ):
            out_ref[i * SEQ + s] = t[s * 12 : (s + 1) * 12].astype(BF)


def combine_kernel(parts_ref, out_ref):
    for s in range(SEQ):
        total = None
        for r in range(8):
            t = parts_ref[r * SEQ + s].astype(F32)
            total = t if total is None else total + t
        at = s * GW
        low, high = total[:, 0:128], total[:, 128:256]
        out_ref[:, at : at + GW] = total[:, 256:384]
        out_ref[:, 1024 + at : 1024 + at + GW] = join(low, high, 0)
        out_ref[:, 2048 + at : 2048 + at + GW] = join(low, high, 1)


def input_gradient_kernel(
    pos_ref, first_ref, second_ref, w0, w1, w2, w3, x_ref, ctx_ref, out_ref, packed, held, sems
):
    copies = fetch([(w, held.at[f]) for f, w in enumerate((w0, w1, w2, w3))], sems)
    for s in range(SEQ):
        at = s * GW
        a = [first_ref[s, :, i * 128 : (i + 1) * 128].astype(F32) for i in range(2)]
        b = [second_ref[s, :, i * 128 : (i + 1) * 128].astype(F32) for i in range(2)]
        ctx_ref[:, at : at + GW] = join(a[0], b[0], 1).astype(BF)
        packed[:, at : at + GW] = join(a[0], b[0], 0).astype(BF)
        packed[:, 1024 + at : 1024 + at + GW] = join(a[1], b[1], 0).astype(BF)
        packed[:, 2048 + at : 2048 + at + GW] = join(a[1], b[1], 1).astype(BF)
    for f in range(4):
        to = pl.ds(pl.multiple_of(pos_ref[f] * 384, 384), 384)
        copies[f].wait()
        out_ref[:, to] = dot(packed[...], held[f], ((1,), (1,)))
    standard, inv_std = standardize(x_ref[...].astype(F32))
    ng = out_ref[...]
    row_mean = jnp.mean(ng, axis=1, keepdims=True)
    projected = jnp.mean(ng * standard, axis=1, keepdims=True)
    out_ref[...] = inv_std * (ng - row_mean - standard * projected)


def shape(dims, dtype=BF):
    return jax.ShapeDtypeStruct(dims, dtype)


UP = [(i, (i // 4) * 4 + (i % 4 + 1) % 4) for i in range(8)]
DOWN = [(i, (i // 4) * 4 + (i % 4 + 3) % 4) for i in range(8)]
FAR = [(i, (i // 4) * 4 + (i % 4 + 2) % 4) for i in range(8)]
ACROSS = [(i, i ^ 4) for i in range(8)]
SWAP = [(f * 8 + s, (f ^ 1) * 8 + (s ^ 4)) for f in range(2) for s in range(8)]
OFFSETS = [(dz, dy) for dz in range(2) for dy in (0, 3, 1, 2)]
HEAD_FLOPS = (10**9, 10**10)
tie = lax.optimization_barrier


def send(v, way):
    return lax.ppermute(v, "seq", way)


def sibling(v):
    return lax.ppermute(v, "core", [(0, 1), (1, 0)])


def swap(v):
    return lax.ppermute(v, ("zh", "seq"), SWAP)


def call(kernel, out, in_specs, flops=0, scratch=(), transcendentals=0, vmem=56):
    return pl.pallas_call(
        kernel,
        out_shape=out,
        in_specs=in_specs,
        out_specs=jax.tree.map(lambda _: VM, out),
        scratch_shapes=list(scratch),
        compiler_params=pltpu.CompilerParams(vmem_limit_bytes=vmem * 2**20),
        cost_estimate=pl.CostEstimate(
            flops=flops, bytes_accessed=2**20, transcendentals=transcendentals
        ),
    )


def body(frames, projection, lengths, cotangent):
    x = frames[0]
    me = lax.axis_index("seq")
    core = lax.axis_index("core")
    fsdp = lax.axis_index("zh") * 2 + core
    half = ROWS // 2
    normed, mine = call(
        prepare_kernel,
        (shape((ROWS, D)), shape((384, 768))),
        [SM, VM, ANY],
        scratch=[pltpu.VMEM((6, 384, GW), BF), pltpu.SemaphoreType.DMA((6,))],
    )((me % 4)[None].astype(jnp.int32), x, projection)
    upstream = cotangent[0].reshape(ROWS, SEQ, GW).transpose(1, 0, 2)
    index = [(me // 4 ^ dz) * 4 + (me % 4 + dy) % 4 for dz, dy in OFFSETS]
    place = jnp.stack(index + [core]).astype(jnp.int32)
    owners = jnp.stack([fsdp ^ i for i in range(4)]).astype(jnp.int32)

    beside, other = sibling(mine), send(normed, ACROSS)
    above, below = send(normed, DOWN), send(normed, UP)
    over = swap(mine)
    upstream = lax.all_to_all(tie((upstream, normed))[0], "seq", 0, 0, tiled=True).reshape(T, GW)
    beside, other, above, below, over, upstream, place, owners = tie(
        (beside, other, above, below, over, upstream, place, owners)
    )
    far = [send(below[:half], UP), send(above[half:], DOWN)]
    columns = [mine, beside, over, sibling(over)]

    def project(rows, groups, count):
        height = sum(r.shape[0] for r in rows)
        return call(
            functools.partial(project_kernel, len(rows)),
            (shape((height, 384)),) * count,
            [SM, SM] + [VM] * (4 + len(rows)),
        )(owners, groups, *columns, *rows)

    here = me // 4
    groups = jnp.stack([1 - here, here]).astype(jnp.int32)
    (near,) = project([below, above], groups, 1)
    near_got = send(near, ACROSS)
    _, turned = tie((near, groups[::-1]))
    (kept,) = project([normed, below, above, other], turned, 1)
    _, far = tie((kept, far))
    last, far_kept = project(far, groups, 2)
    _, weight, other_late, near_got = tie((last, projection, other, near_got))
    other_below, other_above = send(other_late, UP), send(other_late, DOWN)
    weight_over = swap(weight)
    far_got = send(last, ACROSS)

    def attend(head):
        return call(
            functools.partial(attention_kernel, head),
            shape((T, 256)),
            [SM, SM] + [VM] * 5,
            HEAD_FLOPS[head],
            [
                pltpu.VMEM((T, 128), BF),
                pltpu.VMEM((T, 128), BF),
                pltpu.VMEM((HD + 16, T), BF),
                pltpu.VMEM((HD, T), BF),
                pltpu.VMEM((HD, T), BF),
                pltpu.VMEM((HD, T), BF),
                pltpu.VMEM((2, T, BQ), F32),
                pltpu.VMEM((2, T, BQ), BF),
                pltpu.VMEM((T, 128), F32),
            ],
            T * T,
        )(place, lengths, kept, far_kept, near_got, far_got, upstream)

    def send_back(grads):
        return lax.all_to_all(grads.reshape(SEQ, ROWS, 256), "seq", 0, 0, tiled=True)

    first = attend(0)
    other_below, other_above, other_late, first, weight = tie(
        (other_below, other_above, other_late, first, weight)
    )
    other_far = send(other_late, FAR)
    back0 = send_back(first)
    beside = sibling(weight)
    second = attend(1)
    second, back0, weight_over, beside, other_far = tie(
        (second, back0, weight_over, beside, other_far)
    )
    blocks = [normed, below, above, *far, other, other_below, other_above, other_far]
    back1 = send_back(second)
    keep, out = call(
        weight_gradient_kernel,
        (shape((768, 384), F32), shape((768, 384))),
        [SM, VM, VM] + [ANY] * len(blocks),
        2 * T * D * 384,
        [
            pltpu.VMEM((384, T), BF),
            pltpu.VMEM((T, D), BF),
            pltpu.VMEM((384, D), F32),
            pltpu.SemaphoreType.DMA((len(blocks),)),
        ],
    )(place, first, second, *blocks)
    got = sibling(out)
    partial = call(add_kernel, shape((64, 12, 384)), [VM, VM])(keep, got)
    partial, back1, weight_over = tie((partial, back1, weight_over))
    weights = [projection, beside, weight_over, sibling(weight_over)]
    partial = lax.all_to_all(partial, ("dp", "zh", "seq"), 0, 0, tiled=True)
    context, input_gradient = call(
        input_gradient_kernel,
        (shape((ROWS, 1024)), shape((ROWS, D), F32)),
        [SM, VM, VM] + [ANY] * 4 + [VM],
        2 * ROWS * D * 3072,
        [
            pltpu.VMEM((ROWS, 3072), BF),
            pltpu.VMEM((4, 384, 3072), BF),
            pltpu.SemaphoreType.DMA((4,)),
        ],
    )(owners, back0, back1, *weights, x)
    partial, context, input_gradient = tie((partial, context, input_gradient))
    projection_gradient = call(combine_kernel, shape((12, 3072), F32), [VM])(partial)
    return (context[None], input_gradient[None], projection_gradient)


def solution(mesh):
    split = jax.sharding.Mesh(mesh.devices.reshape(4, 2, 2, 8), ("dp", "zh", "core", "seq"))
    record = ("dp", "zh", "core")
    placed = (P(record, "seq", None), P(("zh", "core"), None), P(record), P(record, "seq", None))
    return jax.shard_map(
        body,
        mesh=split,
        in_specs=placed,
        out_specs=(P(record, "seq", None), P(record, "seq", None), P((*record, "seq"), None)),
        check_vma=False,
    )
```

```python
import functools

import jax
import jax.numpy as jnp
from jax import lax
from jax.experimental import pallas as pl
from jax.experimental.pallas import tpu as pltpu
from jax.sharding import PartitionSpec as P

BF = jnp.bfloat16
F32 = jnp.float32
D = 1536
HD = 64
T = 2048
ROWS = 256
SEQ = 8
GW = 128
EPS = 1e-05
BQ = 256
CH = 512
NC = T // CH
VM = pl.BlockSpec(memory_space=pltpu.VMEM)
SM = pl.BlockSpec(memory_space=pltpu.SMEM)
ANY = pl.BlockSpec(memory_space=pl.ANY)


def dot(a, b, dims=((1,), (0,))):
    return lax.dot_general(a, b, (dims, ((), ())), preferred_element_type=F32)


def standardize(x):
    centered = x - jnp.mean(x, axis=1, keepdims=True)
    inv_std = lax.rsqrt(jnp.mean(centered * centered, axis=1, keepdims=True) + EPS)
    return centered * inv_std, inv_std


def fetch(pairs, sems):
    copies = [pltpu.make_async_copy(a, b, sems.at[i]) for i, (a, b) in enumerate(pairs)]
    for copy in copies:
        copy.start()
    return copies


def prepare_kernel(y_ref, x_ref, w_ref, normed_ref, columns_ref, held, sems):
    pairs = []
    for z in range(2):
        for kind in range(3):
            first = pl.multiple_of(kind * 1024 + (z * 4 + y_ref[0]) * GW, GW)
            pairs.append((w_ref.at[:, pl.ds(first, GW)], held.at[z * 3 + kind]))
    copies = fetch(pairs, sems)
    normed_ref[...] = standardize(x_ref[...].astype(F32))[0].astype(BF)
    for copy in copies:
        copy.wait()
    for z in range(2):
        k, v = (held[z * 3 + kind].astype(F32) for kind in (1, 2))
        low = lax.broadcasted_iota(jnp.int32, k.shape, 1) < HD
        at = z * 384
        columns_ref[:, at : at + 128] = jnp.where(low, k, pltpu.roll(v, HD, 1)).astype(BF)
        columns_ref[:, at + 128 : at + 256] = jnp.where(low, pltpu.roll(k, HD, 1), v).astype(BF)
        columns_ref[:, at + 256 : at + 384] = held[z * 3]


def project_kernel(n, owner_ref, group_ref, *refs):
    weights, blocks, outs = refs[:4], refs[4 : 4 + n], refs[4 + n :]
    for j, out_ref in enumerate(outs):
        cols = pl.ds(pl.multiple_of(group_ref[j] * 384, 384), 384)
        first = 0
        for block in blocks:
            count = block.shape[0]
            total = None
            for f in range(4):
                rows = pl.ds(pl.multiple_of(owner_ref[f] * 384, 384), 384)
                t = dot(block[:, rows], weights[f][:, cols])
                total = t if total is None else total + t
            out_ref[first : first + count, :] = total.astype(BF)
            first += count


def attention_kernel(
    head, pos_ref, len_ref, kept_ref, far_ref, other_ref, last_ref, up_ref, out_ref, kv, ka, vt, kt, qt, ut, s_ref, e_ref, acc
):
    length = len_ref[0]
    hrows = slice(head * HD, (head + 1) * HD)
    lane = lax.broadcasted_iota(jnp.int32, (BQ, 128), 1)
    for b in range(SEQ):
        r = slice(b * BQ, (b + 1) * BQ)
        source, at = (
            (kept_ref, 0), (kept_ref, 1), (kept_ref, 2), (far_ref, 0),
            (kept_ref, 3), (other_ref, 0), (other_ref, 1), (last_ref, 0),
        )[b]
        own = slice(at * BQ, (at + 1) * BQ)
        first = pl.multiple_of(pos_ref[b] * BQ, BQ)
        mine = source[own, head * 128 : (head + 1) * 128]
        kv[r, :] = mine
        keys = mine.astype(F32)
        row = lax.broadcasted_iota(jnp.int32, (BQ, 128), 0) + first
        bias = jnp.where(lane == HD, jnp.where(row < length, 0.0, -1e30), 0.0)
        ka[r, :] = jnp.where(lane < HD, keys, bias).astype(BF)
        flipped = keys.T.astype(BF)
        kt[:, r] = flipped[0:HD]
        vt[0:HD, r] = flipped[HD:128]
        vt[HD : HD + 16, r] = jnp.ones((16, BQ), BF)
        qt[:, r] = (source[own, 256:384].astype(F32) * 0.125).T[hrows].astype(BF)
        u = jnp.where(row < length, up_ref[pl.ds(first, BQ), :].astype(F32), 0.0)
        ut[:, r] = u.T[hrows].astype(BF)
    acc[...] = jnp.zeros_like(acc)
    zeros = jnp.zeros((HD, BQ), BF)
    ones_row = jnp.where(lax.broadcasted_iota(jnp.int32, (HD, BQ), 0) == 0, 1.0, 0.0).astype(BF)
    nt = ((1,), (1,))

    def step(i, carry):
        contexts, ups, queries, inners = [], [], [], []
        starts = [pl.multiple_of((2 * i + j) * BQ, BQ) for j in range(2)]
        for j in range(2):
            cols = pl.ds(starts[j], BQ)
            qh = qt[:, cols]
            qa = jnp.concatenate([qh, ones_row], axis=0)
            peak = None
            for c in range(NC):
                r = slice(c * CH, (c + 1) * CH)
                s = dot(ka[r, :], qa)
                s_ref[j, r, :] = s
                t = jnp.max(s.reshape(CH // 8, 8, BQ), axis=0)
                peak = t if peak is None else jnp.maximum(peak, t)
            peak = jnp.max(peak, axis=0, keepdims=True)
            total = None
            for c in range(NC):
                r = slice(c * CH, (c + 1) * CH)
                e = jnp.exp(s_ref[j, r, :] - peak).astype(BF)
                e_ref[j, r, :] = e
                t = dot(vt[:, r], e)
                total = t if total is None else total + t
            inverse = 1.0 / total[HD : HD + 1]
            context = total[0:HD] * inverse
            up = (ut[:, cols].astype(F32) * inverse).astype(BF)
            inner = jnp.sum(up.astype(F32) * context, axis=0, keepdims=True)
            contexts.append(context)
            ups.append(jnp.concatenate([zeros, up], axis=0))
            queries.append(jnp.concatenate([qh, zeros], axis=0))
            inners.append(inner)
        dq = [None, None]
        for c in range(NC):
            r = slice(c * CH, (c + 1) * CH)
            total = acc[r, :]
            for j in range(2):
                dp = dot(kv[r, :], ups[j])
                e = e_ref[j, r, :]
                ds = (e.astype(F32) * (dp - inners[j])).astype(BF)
                t = dot(kt[:, r], ds)
                dq[j] = t if dq[j] is None else dq[j] + t
                total = total + (dot(ds, queries[j], nt) + dot(e, ups[j], nt))
            acc[r, :] = total
        for j in range(2):
            first = pl.multiple_of(pos_ref[2 * i + j] * BQ, BQ)
            col = lax.broadcasted_iota(jnp.int32, (HD, BQ), 1) + first
            context = jnp.where(col < length, contexts[j], 0.0)
            both = jnp.concatenate([dq[j] * 0.125, context], axis=0)
            out_ref[pl.ds(first, BQ), 0:128] = both.T.astype(BF)
        return carry

    lax.fori_loop(0, T // BQ // 2, step, 0)
    for b in range(SEQ):
        rows = pl.ds(pl.multiple_of(pos_ref[b] * BQ, BQ), BQ)
        out_ref[rows, 128:256] = acc[b * BQ : (b + 1) * BQ, :].astype(BF)


def weight_gradient_kernel(pos_ref, first_ref, second_ref, *refs):
    sources, (keep_ref, send_ref, flipped_ref, held, acc, sems) = refs[:-6], refs[-6:]
    at = [sum(b.shape[0] for b in sources[:i]) for i in range(len(sources))]
    spots = [pl.ds(a, b.shape[0]) for a, b in zip(at, sources)]
    copies = fetch([(b, held.at[spot]) for b, spot in zip(sources, spots)], sems)
    for b in range(SEQ):
        rows = pl.ds(pl.multiple_of(pos_ref[b] * ROWS, ROWS), ROWS)
        cols = slice(b * ROWS, (b + 1) * ROWS)
        both = [g[rows, :].astype(F32).T.astype(BF) for g in (first_ref, second_ref)]
        parts = [g[128:256] for g in both] + [g[0:HD] for g in both]
        flipped_ref[:, cols] = jnp.concatenate(parts, axis=0)
    for half in range(2):
        rows = slice(half * T // 2, (half + 1) * T // 2)
        for i, copy in enumerate(copies):
            if at[i] // (T // 2) == half:
                copy.wait()
        for c in range(3):
            cs = slice(c * 512, (c + 1) * 512)
            t = dot(flipped_ref[:, rows], held[rows, cs])
            acc[:, cs] = t if half == 0 else acc[:, cs] + t
    core = pos_ref[SEQ]
    for c in range(4):
        flipped = acc[:, c * 384 : (c + 1) * 384].T
        halves = [[flipped[i * 96 : (i + 1) * 96] for i in (k, k + 2)] for k in range(2)]
        for k in range(2):
            for i in range(2):
                r = slice((c * 2 + i) * 96, (c * 2 + i + 1) * 96)

                @pl.when(core == k)
                def _():
                    keep_ref[r, :] = halves[k][i]

                @pl.when(core != k)
                def _():
                    send_ref[r, :] = halves[k][i].astype(BF)


def join(first, second, part):
    low = lax.broadcasted_iota(jnp.int32, first.shape, first.ndim - 1) < HD
    if part == 0:
        return jnp.where(low, first, pltpu.roll(second, HD, first.ndim - 1))
    return jnp.where(low, pltpu.roll(first, HD, first.ndim - 1), second)


def add_kernel(keep_ref, got_ref, out_ref):
    for i in range(64 // 8):
        rows = slice(i * 96, (i + 1) * 96)
        t = keep_ref[rows, :] + got_ref[rows, :].astype(F32)
        for s in range(SEQ):
            out_ref[i * SEQ + s] = t[s * 12 : (s + 1) * 12].astype(BF)


def combine_kernel(parts_ref, out_ref):
    for s in range(SEQ):
        total = None
        for r in range(8):
            t = parts_ref[r * SEQ + s].astype(F32)
            total = t if total is None else total + t
        at = s * GW
        low, high = total[:, 0:128], total[:, 128:256]
        out_ref[:, at : at + GW] = total[:, 256:384]
        out_ref[:, 1024 + at : 1024 + at + GW] = join(low, high, 0)
        out_ref[:, 2048 + at : 2048 + at + GW] = join(low, high, 1)


def input_gradient_kernel(
    pos_ref, first_ref, second_ref, w0, w1, w2, w3, w4, w5, x_ref, ctx_ref, out_ref, packed, held, sems
):
    halves = [held.at[f, :, pl.ds(p * 1536, 1536)] for f in (2, 3) for p in range(2)]
    copies = fetch(list(zip((w0, w1, w2, w3, w4, w5), [held.at[0], held.at[1]] + halves)), sems)
    for s in range(SEQ):
        at = s * GW
        a = [first_ref[s, :, i * 128 : (i + 1) * 128].astype(F32) for i in range(2)]
        b = [second_ref[s, :, i * 128 : (i + 1) * 128].astype(F32) for i in range(2)]
        ctx_ref[:, at : at + GW] = join(a[0], b[0], 1).astype(BF)
        packed[:, at : at + GW] = join(a[0], b[0], 0).astype(BF)
        packed[:, 1024 + at : 1024 + at + GW] = join(a[1], b[1], 0).astype(BF)
        packed[:, 2048 + at : 2048 + at + GW] = join(a[1], b[1], 1).astype(BF)
    nt = ((1,), (1,))
    for f in range(4):
        to = pl.ds(pl.multiple_of(pos_ref[f] * 384, 384), 384)
        if f < 2:
            copies[f].wait()
            out_ref[:, to] = dot(packed[...], held[f], nt)
        else:
            total = None
            for p in range(2):
                copies[2 * f - 2 + p].wait()
                cols = pl.ds(pl.multiple_of((pos_ref[4] ^ p) * 1536, 1536), 1536)
                t = dot(packed[:, cols], held[f, :, p * 1536 : (p + 1) * 1536], nt)
                total = t if p == 0 else total + t
            out_ref[:, to] = total
    standard, inv_std = standardize(x_ref[...].astype(F32))
    ng = out_ref[...]
    row_mean = jnp.mean(ng, axis=1, keepdims=True)
    projected = jnp.mean(ng * standard, axis=1, keepdims=True)
    out_ref[...] = inv_std * (ng - row_mean - standard * projected)


def shape(dims, dtype=BF):
    return jax.ShapeDtypeStruct(dims, dtype)


UP = [(i, (i // 4) * 4 + (i % 4 + 1) % 4) for i in range(8)]
DOWN = [(i, (i // 4) * 4 + (i % 4 + 3) % 4) for i in range(8)]
ACROSS = [(i, i ^ 4) for i in range(8)]
SWAP = [(f * 8 + s, (f ^ 1) * 8 + (s ^ 4)) for f in range(2) for s in range(8)]
OFFSETS = [(dz, dy) for dz in range(2) for dy in (0, 3, 1, 2)]
HEAD_FLOPS = (10**9, 10**10)
tie = lax.optimization_barrier


def send(v, way):
    return lax.ppermute(v, "seq", way)


def sibling(v):
    return lax.ppermute(v, "core", [(0, 1), (1, 0)])


def swap(v):
    return lax.ppermute(v, ("zh", "seq"), SWAP)


def call(kernel, out, in_specs, flops=0, scratch=(), transcendentals=0, vmem=56):
    return pl.pallas_call(
        kernel,
        out_shape=out,
        in_specs=in_specs,
        out_specs=jax.tree.map(lambda _: VM, out),
        scratch_shapes=list(scratch),
        compiler_params=pltpu.CompilerParams(vmem_limit_bytes=vmem * 2**20),
        cost_estimate=pl.CostEstimate(
            flops=flops, bytes_accessed=2**20, transcendentals=transcendentals
        ),
    )


def body(frames, projection, lengths, cotangent):
    x = frames[0]
    me = lax.axis_index("seq")
    core = lax.axis_index("core")
    fsdp = lax.axis_index("zh") * 2 + core
    half = ROWS // 2
    normed, mine = call(
        prepare_kernel,
        (shape((ROWS, D)), shape((384, 768))),
        [SM, VM, ANY],
        scratch=[pltpu.VMEM((6, 384, GW), BF), pltpu.SemaphoreType.DMA((6,))],
    )((me % 4)[None].astype(jnp.int32), x, projection)
    upstream = cotangent[0].reshape(ROWS, SEQ, GW).transpose(1, 0, 2)
    index = [(me // 4 ^ dz) * 4 + (me % 4 + dy) % 4 for dz, dy in OFFSETS]
    place = jnp.stack(index + [core]).astype(jnp.int32)
    owners = jnp.stack([fsdp ^ i for i in range(4)] + [lax.axis_index("dp") % 2]).astype(jnp.int32)

    beside, other = sibling(mine), send(normed, ACROSS)
    above, below = send(normed, DOWN), send(normed, UP)
    over = swap(mine)
    upstream = lax.all_to_all(tie((upstream, normed))[0], "seq", 0, 0, tiled=True).reshape(T, GW)
    parity = lax.axis_index("dp") % 2
    weight_half = lax.dynamic_slice_in_dim(projection, parity * 1536, 1536, 1)
    beside, other, above, below, over, upstream, place, owners, weight_half = tie(
        (beside, other, above, below, over, upstream, place, owners, weight_half)
    )
    far = [send(below[:half], UP), send(above[half:], DOWN)]
    columns = [mine, beside, over, sibling(over)]

    def project(rows, groups, count):
        height = sum(r.shape[0] for r in rows)
        return call(
            functools.partial(project_kernel, len(rows)),
            (shape((height, 384)),) * count,
            [SM, SM] + [VM] * (4 + len(rows)),
        )(owners, groups, *columns, *rows)

    here = me // 4
    groups = jnp.stack([1 - here, here]).astype(jnp.int32)
    (near,) = project([below, above], groups, 1)
    near_got = send(near, ACROSS)
    _, turned = tie((near, groups[::-1]))
    (kept,) = project([normed, below, above, other], turned, 1)
    _, far = tie((kept, far))
    last, far_kept = project(far, groups, 2)
    _, other_late, near_got = tie((last, other, near_got))
    other_below, other_above = send(other_late, UP), send(other_late, DOWN)
    weight_half = swap(weight_half)
    far_got, far_late = tie((send(last, ACROSS), far))
    other_far = [send(v, ACROSS) for v in far_late]

    def attend(head):
        return call(
            functools.partial(attention_kernel, head),
            shape((T, 256)),
            [SM, SM] + [VM] * 5,
            HEAD_FLOPS[head],
            [
                pltpu.VMEM((T, 128), BF),
                pltpu.VMEM((T, 128), BF),
                pltpu.VMEM((HD + 16, T), BF),
                pltpu.VMEM((HD, T), BF),
                pltpu.VMEM((HD, T), BF),
                pltpu.VMEM((HD, T), BF),
                pltpu.VMEM((2, T, BQ), F32),
                pltpu.VMEM((2, T, BQ), BF),
                pltpu.VMEM((T, 128), F32),
            ],
            T * T,
        )(place, lengths, kept, far_kept, near_got, far_got, upstream)

    def send_back(grads):
        return lax.all_to_all(grads.reshape(SEQ, ROWS, 256), "seq", 0, 0, tiled=True)

    first = attend(0)
    other_below, other_above, other_far, first, weight, weight_half = tie(
        (other_below, other_above, other_far, first, projection, weight_half)
    )
    weight_rest = lax.ppermute(weight_half, "dp", [(i, i ^ 1) for i in range(4)])
    back0 = send_back(first)
    beside = sibling(weight)
    second = attend(1)
    second, back0, beside = tie((second, back0, beside))
    blocks = [normed, below, above, *far, other, other_below, other_above, *other_far]
    back1 = send_back(second)
    keep, out = call(
        weight_gradient_kernel,
        (shape((768, 384), F32), shape((768, 384))),
        [SM, VM, VM] + [ANY] * len(blocks),
        2 * T * D * 384,
        [
            pltpu.VMEM((384, T), BF),
            pltpu.VMEM((T, D), BF),
            pltpu.VMEM((384, D), F32),
            pltpu.SemaphoreType.DMA((len(blocks),)),
        ],
    )(place, first, second, *blocks)
    got = sibling(out)
    partial = call(add_kernel, shape((64, 12, 384)), [VM, VM])(keep, got)
    partial, back1, weight_half, weight_rest = tie((partial, back1, weight_half, weight_rest))
    weights = [projection, beside, weight_half, weight_rest]
    weights += [sibling(weight_half), sibling(weight_rest)]
    partial = lax.all_to_all(partial, ("dp", "zh", "seq"), 0, 0, tiled=True)
    context, input_gradient = call(
        input_gradient_kernel,
        (shape((ROWS, 1024)), shape((ROWS, D), F32)),
        [SM, VM, VM] + [ANY] * 6 + [VM],
        2 * ROWS * D * 3072,
        [
            pltpu.VMEM((ROWS, 3072), BF),
            pltpu.VMEM((4, 384, 3072), BF),
            pltpu.SemaphoreType.DMA((6,)),
        ],
    )(owners, back0, back1, *weights, x)
    partial, context, input_gradient = tie((partial, context, input_gradient))
    projection_gradient = call(combine_kernel, shape((12, 3072), F32), [VM])(partial)
    return (context[None], input_gradient[None], projection_gradient)


def solution(mesh):
    split = jax.sharding.Mesh(mesh.devices.reshape(4, 2, 2, 8), ("dp", "zh", "core", "seq"))
    record = ("dp", "zh", "core")
    placed = (P(record, "seq", None), P(("zh", "core"), None), P(record), P(record, "seq", None))
    return jax.shard_map(
        body,
        mesh=split,
        in_specs=placed,
        out_specs=(P(record, "seq", None), P(record, "seq", None), P((*record, "seq"), None)),
        check_vma=False,
    )
```

```python
import functools

import jax
import jax.numpy as jnp
from jax import lax
from jax.experimental import pallas as pl
from jax.experimental.pallas import tpu as pltpu
from jax.sharding import PartitionSpec as P

BF = jnp.bfloat16
F32 = jnp.float32
D = 1536
HD = 64
T = 2048
ROWS = 256
SEQ = 8
GW = 128
EPS = 1e-05
BQ = 256
CH = 512
NC = T // CH
VM = pl.BlockSpec(memory_space=pltpu.VMEM)
SM = pl.BlockSpec(memory_space=pltpu.SMEM)
ANY = pl.BlockSpec(memory_space=pl.ANY)


def dot(a, b, dims=((1,), (0,))):
    return lax.dot_general(a, b, (dims, ((), ())), preferred_element_type=F32)


def standardize(x):
    centered = x - jnp.mean(x, axis=1, keepdims=True)
    inv_std = lax.rsqrt(jnp.mean(centered * centered, axis=1, keepdims=True) + EPS)
    return centered * inv_std, inv_std


def fetch(pairs, sems):
    copies = [pltpu.make_async_copy(a, b, sems.at[i]) for i, (a, b) in enumerate(pairs)]
    for copy in copies:
        copy.start()
    return copies


def prepare_kernel(y_ref, x_ref, w_ref, normed_ref, columns_ref, held, sems):
    pairs = []
    for z in range(2):
        for kind in range(3):
            first = pl.multiple_of(kind * 1024 + (z * 4 + y_ref[0]) * GW, GW)
            pairs.append((w_ref.at[:, pl.ds(first, GW)], held.at[z * 3 + kind]))
    copies = fetch(pairs, sems)
    normed_ref[...] = standardize(x_ref[...].astype(F32))[0].astype(BF)
    for copy in copies:
        copy.wait()
    for z in range(2):
        k, v = (held[z * 3 + kind].astype(F32) for kind in (1, 2))
        low = lax.broadcasted_iota(jnp.int32, k.shape, 1) < HD
        at = z * 384
        columns_ref[:, at : at + 128] = jnp.where(low, k, pltpu.roll(v, HD, 1)).astype(BF)
        columns_ref[:, at + 128 : at + 256] = jnp.where(low, pltpu.roll(k, HD, 1), v).astype(BF)
        columns_ref[:, at + 256 : at + 384] = held[z * 3]


def project_kernel(n, owner_ref, group_ref, *refs):
    weights, blocks, outs = refs[:4], refs[4 : 4 + n], refs[4 + n : -3]
    held_weight, held, sems = refs[-3:]
    pairs = []
    for j in range(len(outs)):
        cols = pl.ds(pl.multiple_of(group_ref[j] * 384, 384), 384)
        for f in range(4):
            rows = pl.ds(pl.multiple_of(owner_ref[f] * 384, 384), 384)
            pairs.append((weights[f].at[:, cols], held_weight.at[j, rows, :]))
    at = [sum(b.shape[0] for b in blocks[:i]) for i in range(n)]
    spots = [pl.ds(a, b.shape[0]) for a, b in zip(at, blocks)]
    pairs += [(b, held.at[spot]) for b, spot in zip(blocks, spots)]
    copies = fetch(pairs, sems)
    for copy in copies[: -n]:
        copy.wait()
    for i in range(n):
        copies[i - n].wait()
        for j, out_ref in enumerate(outs):
            out_ref[spots[i], :] = dot(held[spots[i], :], held_weight[j]).astype(BF)


def attention_kernel(
    head, pos_ref, len_ref, kept_ref, far_ref, other_ref, last_ref, up_ref, out_ref, kv, ka, vt, kt, qt, ut, s_ref, e_ref, acc
):
    length = len_ref[0]
    hrows = slice(head * HD, (head + 1) * HD)
    lane = lax.broadcasted_iota(jnp.int32, (BQ, 128), 1)
    for b in range(SEQ):
        r = slice(b * BQ, (b + 1) * BQ)
        source, at = (
            (kept_ref, 0), (kept_ref, 1), (kept_ref, 2), (far_ref, 0),
            (kept_ref, 3), (other_ref, 0), (other_ref, 1), (last_ref, 0),
        )[b]
        own = slice(at * BQ, (at + 1) * BQ)
        first = pl.multiple_of(pos_ref[b] * BQ, BQ)
        mine = source[own, head * 128 : (head + 1) * 128]
        kv[r, :] = mine
        keys = mine.astype(F32)
        row = lax.broadcasted_iota(jnp.int32, (BQ, 128), 0) + first
        bias = jnp.where(lane == HD, jnp.where(row < length, 0.0, -1e30), 0.0)
        ka[r, :] = jnp.where(lane < HD, keys, bias).astype(BF)
        flipped = keys.T.astype(BF)
        kt[:, r] = flipped[0:HD]
        vt[0:HD, r] = flipped[HD:128]
        vt[HD : HD + 16, r] = jnp.ones((16, BQ), BF)
        qt[:, r] = (source[own, 256:384].astype(F32) * 0.125).T[hrows].astype(BF)
        u = jnp.where(row < length, up_ref[pl.ds(first, BQ), :].astype(F32), 0.0)
        ut[:, r] = u.T[hrows].astype(BF)
    acc[...] = jnp.zeros_like(acc)
    zeros = jnp.zeros((HD, BQ), BF)
    ones_row = jnp.where(lax.broadcasted_iota(jnp.int32, (HD, BQ), 0) == 0, 1.0, 0.0).astype(BF)
    nt = ((1,), (1,))

    def scores(start, j, c):
        r = slice(c * CH, (c + 1) * CH)
        qa = jnp.concatenate([qt[:, pl.ds(start, BQ)], ones_row], axis=0)
        s = dot(ka[r, :], qa)
        s_ref[j, r, :] = s
        return jnp.max(s.reshape(CH // 8, 8, BQ), axis=0)

    def weigh(peak, j, c):
        r = slice(c * CH, (c + 1) * CH)
        e = jnp.exp(s_ref[j, r, :] - peak).astype(BF)
        e_ref[j, r, :] = e
        return dot(vt[:, r], e)

    def finish(total, start):
        cols = pl.ds(start, BQ)
        inverse = 1.0 / total[HD : HD + 1]
        context = total[0:HD] * inverse
        up = (ut[:, cols].astype(F32) * inverse).astype(BF)
        inner = jnp.sum(up.astype(F32) * context, axis=0, keepdims=True)
        up = jnp.concatenate([zeros, up], axis=0)
        query = jnp.concatenate([qt[:, cols], zeros], axis=0)
        return context, up, query, inner

    def back(state, j, c):
        r = slice(c * CH, (c + 1) * CH)
        context, up, query, inner = state
        e = e_ref[j, r, :]
        ds = (e.astype(F32) * (dot(kv[r, :], up) - inner)).astype(BF)
        acc[r, :] += dot(ds, query, nt) + dot(e, up, nt)
        return dot(kt[:, r], ds)

    def write(block, context, dq):
        first = pl.multiple_of(pos_ref[block] * BQ, BQ)
        col = lax.broadcasted_iota(jnp.int32, (HD, BQ), 1) + first
        context = jnp.where(col < length, context, 0.0)
        both = jnp.concatenate([dq * 0.125, context], axis=0)
        out_ref[pl.ds(first, BQ), 0:128] = both.T.astype(BF)

    def add(a, b):
        return b if a is None else a + b

    def top(peak):
        return jnp.max(peak, axis=0, keepdims=True)

    def step(i, peak):
        starts = [pl.multiple_of((2 * i + j) * BQ, BQ) for j in range(2)]
        after = pl.multiple_of(lax.rem(2 * i + 2, SEQ) * BQ, BQ)
        peak, peak1, total, total1 = top(peak), None, None, None
        for c in range(NC):
            t = scores(starts[1], 1, c)
            peak1 = t if c == 0 else jnp.maximum(peak1, t)
            total = add(total, weigh(peak, 0, c))
        state = finish(total, starts[0])
        peak1, dq = top(peak1), None
        for c in range(NC):
            total1 = add(total1, weigh(peak1, 1, c))
            dq = add(dq, back(state, 0, c))
        state1 = finish(total1, starts[1])
        write(2 * i, state[0], dq)
        dq = None
        for c in range(NC):
            t = scores(after, 0, c)
            peak = t if c == 0 else jnp.maximum(peak, t)
            dq = add(dq, back(state1, 1, c))
        write(2 * i + 1, state1[0], dq)
        return peak

    peak = None
    for c in range(NC):
        t = scores(0, 0, c)
        peak = t if c == 0 else jnp.maximum(peak, t)
    lax.fori_loop(0, SEQ // 2, step, peak)
    for b in range(SEQ):
        rows = pl.ds(pl.multiple_of(pos_ref[b] * BQ, BQ), BQ)
        out_ref[rows, 128:256] = acc[b * BQ : (b + 1) * BQ, :].astype(BF)


def weight_gradient_kernel(pos_ref, first_ref, second_ref, *refs):
    sources, (keep_ref, send_ref, flipped_ref, held, acc, sems) = refs[:-6], refs[-6:]
    at = [sum(b.shape[0] for b in sources[:i]) for i in range(len(sources))]
    spots = [pl.ds(a, b.shape[0]) for a, b in zip(at, sources)]
    copies = fetch([(b, held.at[spot]) for b, spot in zip(sources, spots)], sems)
    for b in range(SEQ):
        rows = pl.ds(pl.multiple_of(pos_ref[b] * ROWS, ROWS), ROWS)
        cols = slice(b * ROWS, (b + 1) * ROWS)
        both = [g[rows, :].astype(F32).T.astype(BF) for g in (first_ref, second_ref)]
        parts = [g[128:256] for g in both] + [g[0:HD] for g in both]
        flipped_ref[:, cols] = jnp.concatenate(parts, axis=0)
    for half in range(2):
        rows = slice(half * T // 2, (half + 1) * T // 2)
        for i, copy in enumerate(copies):
            if at[i] // (T // 2) == half:
                copy.wait()
        for c in range(3):
            cs = slice(c * 512, (c + 1) * 512)
            t = dot(flipped_ref[:, rows], held[rows, cs])
            acc[:, cs] = t if half == 0 else acc[:, cs] + t
    core = pos_ref[SEQ]
    for c in range(4):
        flipped = acc[:, c * 384 : (c + 1) * 384].T
        halves = [[flipped[i * 96 : (i + 1) * 96] for i in (k, k + 2)] for k in range(2)]
        for k in range(2):
            for i in range(2):
                r = slice((c * 2 + i) * 96, (c * 2 + i + 1) * 96)

                @pl.when(core == k)
                def _():
                    keep_ref[r, :] = halves[k][i]

                @pl.when(core != k)
                def _():
                    send_ref[r, :] = halves[k][i].astype(BF)


def join(first, second, part):
    low = lax.broadcasted_iota(jnp.int32, first.shape, first.ndim - 1) < HD
    if part == 0:
        return jnp.where(low, first, pltpu.roll(second, HD, first.ndim - 1))
    return jnp.where(low, pltpu.roll(first, HD, first.ndim - 1), second)


def add_kernel(keep_ref, got_ref, out_ref):
    for i in range(64 // 8):
        rows = slice(i * 96, (i + 1) * 96)
        t = keep_ref[rows, :] + got_ref[rows, :].astype(F32)
        for s in range(SEQ):
            out_ref[i * SEQ + s] = t[s * 12 : (s + 1) * 12].astype(BF)


def combine_kernel(parts_ref, out_ref):
    for s in range(SEQ):
        total = None
        for r in range(8):
            t = parts_ref[r * SEQ + s].astype(F32)
            total = t if total is None else total + t
        at = s * GW
        low, high = total[:, 0:128], total[:, 128:256]
        out_ref[:, at : at + GW] = total[:, 256:384]
        out_ref[:, 1024 + at : 1024 + at + GW] = join(low, high, 0)
        out_ref[:, 2048 + at : 2048 + at + GW] = join(low, high, 1)


def input_gradient_kernel(
    pos_ref, first_ref, second_ref, w0, w1, w2, w3, w4, w5, x_ref, ctx_ref, out_ref, packed, held, sems
):
    halves = [held.at[f, :, pl.ds(p * 1536, 1536)] for f in (2, 3) for p in range(2)]
    copies = fetch(list(zip((w0, w1, w2, w3, w4, w5), [held.at[0], held.at[1]] + halves)), sems)
    for s in range(SEQ):
        at = s * GW
        a = [first_ref[s, :, i * 128 : (i + 1) * 128].astype(F32) for i in range(2)]
        b = [second_ref[s, :, i * 128 : (i + 1) * 128].astype(F32) for i in range(2)]
        ctx_ref[:, at : at + GW] = join(a[0], b[0], 1).astype(BF)
        packed[:, at : at + GW] = join(a[0], b[0], 0).astype(BF)
        packed[:, 1024 + at : 1024 + at + GW] = join(a[1], b[1], 0).astype(BF)
        packed[:, 2048 + at : 2048 + at + GW] = join(a[1], b[1], 1).astype(BF)
    nt = ((1,), (1,))
    for f in range(4):
        to = pl.ds(pl.multiple_of(pos_ref[f] * 384, 384), 384)
        if f < 2:
            copies[f].wait()
            out_ref[:, to] = dot(packed[...], held[f], nt)
        else:
            total = None
            for p in range(2):
                copies[2 * f - 2 + p].wait()
                cols = pl.ds(pl.multiple_of((pos_ref[4] ^ p) * 1536, 1536), 1536)
                t = dot(packed[:, cols], held[f, :, p * 1536 : (p + 1) * 1536], nt)
                total = t if p == 0 else total + t
            out_ref[:, to] = total
    standard, inv_std = standardize(x_ref[...].astype(F32))
    ng = out_ref[...]
    row_mean = jnp.mean(ng, axis=1, keepdims=True)
    projected = jnp.mean(ng * standard, axis=1, keepdims=True)
    out_ref[...] = inv_std * (ng - row_mean - standard * projected)


def shape(dims, dtype=BF):
    return jax.ShapeDtypeStruct(dims, dtype)


UP = [(i, (i // 4) * 4 + (i % 4 + 1) % 4) for i in range(8)]
DOWN = [(i, (i // 4) * 4 + (i % 4 + 3) % 4) for i in range(8)]
ACROSS = [(i, i ^ 4) for i in range(8)]
SWAP = [(f * 8 + s, (f ^ 1) * 8 + (s ^ 4)) for f in range(2) for s in range(8)]
OFFSETS = [(dz, dy) for dz in range(2) for dy in (0, 3, 1, 2)]
HEAD_FLOPS = (10**9, 10**10)
tie = lax.optimization_barrier


def send(v, way):
    return lax.ppermute(v, "seq", way)


def sibling(v):
    return lax.ppermute(v, "core", [(0, 1), (1, 0)])


def swap(v):
    return lax.ppermute(v, ("zh", "seq"), SWAP)


def call(kernel, out, in_specs, flops=0, scratch=(), transcendentals=0, vmem=56):
    return pl.pallas_call(
        kernel,
        out_shape=out,
        in_specs=in_specs,
        out_specs=jax.tree.map(lambda _: VM, out),
        scratch_shapes=list(scratch),
        compiler_params=pltpu.CompilerParams(vmem_limit_bytes=vmem * 2**20),
        cost_estimate=pl.CostEstimate(
            flops=flops, bytes_accessed=2**20, transcendentals=transcendentals
        ),
    )


def body(frames, projection, lengths, cotangent):
    x = frames[0]
    me = lax.axis_index("seq")
    core = lax.axis_index("core")
    fsdp = lax.axis_index("zh") * 2 + core
    half = ROWS // 2
    normed, mine = call(
        prepare_kernel,
        (shape((ROWS, D)), shape((384, 768))),
        [SM, VM, ANY],
        scratch=[pltpu.VMEM((6, 384, GW), BF), pltpu.SemaphoreType.DMA((6,))],
    )((me % 4)[None].astype(jnp.int32), x, projection)
    upstream = cotangent[0].reshape(ROWS, SEQ, GW).transpose(1, 0, 2)
    index = [(me // 4 ^ dz) * 4 + (me % 4 + dy) % 4 for dz, dy in OFFSETS]
    place = jnp.stack(index + [core]).astype(jnp.int32)
    owners = jnp.stack([fsdp ^ i for i in range(4)] + [lax.axis_index("dp") % 2]).astype(jnp.int32)

    beside, other = sibling(mine), send(normed, ACROSS)
    above, below = send(normed, DOWN), send(normed, UP)
    over = swap(mine)
    upstream = lax.all_to_all(tie((upstream, normed))[0], "seq", 0, 0, tiled=True).reshape(T, GW)
    parity = lax.axis_index("dp") % 2
    weight_half = lax.dynamic_slice_in_dim(projection, parity * 1536, 1536, 1)
    beside, other, above, below, over, upstream, place, owners, weight_half = tie(
        (beside, other, above, below, over, upstream, place, owners, weight_half)
    )
    far = [send(below[:half], UP), send(above[half:], DOWN)]
    columns = [mine, beside, over, sibling(over)]

    def project(rows, groups, count):
        height = sum(r.shape[0] for r in rows)
        return call(
            functools.partial(project_kernel, len(rows)),
            (shape((height, 384)),) * count,
            [SM, SM] + [ANY] * (4 + len(rows)),
            scratch=[
                pltpu.VMEM((count, D, 384), BF),
                pltpu.VMEM((height, D), BF),
                pltpu.SemaphoreType.DMA((4 * count + len(rows),)),
            ],
        )(owners, groups, *columns, *rows)

    here = me // 4
    groups = jnp.stack([1 - here, here]).astype(jnp.int32)
    (near,) = project([below, above], groups, 1)
    near_got = send(near, ACROSS)
    _, turned = tie((near, groups[::-1]))
    (kept,) = project([normed, below, above, other], turned, 1)
    _, far = tie((kept, far))
    last, far_kept = project(far, groups, 2)
    _, other_late, near_got = tie((last, other, near_got))
    other_below, other_above = send(other_late, UP), send(other_late, DOWN)
    weight_half = swap(weight_half)
    far_got, far_late = tie((send(last, ACROSS), far))
    other_far = [send(v, ACROSS) for v in far_late]

    def attend(head):
        return call(
            functools.partial(attention_kernel, head),
            shape((T, 256)),
            [SM, SM] + [VM] * 5,
            HEAD_FLOPS[head],
            [
                pltpu.VMEM((T, 128), BF),
                pltpu.VMEM((T, 128), BF),
                pltpu.VMEM((HD + 16, T), BF),
                pltpu.VMEM((HD, T), BF),
                pltpu.VMEM((HD, T), BF),
                pltpu.VMEM((HD, T), BF),
                pltpu.VMEM((2, T, BQ), F32),
                pltpu.VMEM((2, T, BQ), BF),
                pltpu.VMEM((T, 128), F32),
            ],
            T * T,
        )(place, lengths, kept, far_kept, near_got, far_got, upstream)

    def send_back(grads):
        return lax.all_to_all(grads.reshape(SEQ, ROWS, 256), "seq", 0, 0, tiled=True)

    first = attend(0)
    other_below, other_above, other_far, first, weight, weight_half = tie(
        (other_below, other_above, other_far, first, projection, weight_half)
    )
    weight_rest = lax.ppermute(weight_half, "dp", [(i, i ^ 1) for i in range(4)])
    back0 = send_back(first)
    beside = sibling(weight)
    second = attend(1)
    second, back0, beside = tie((second, back0, beside))
    blocks = [normed, below, above, *far, other, other_below, other_above, *other_far]
    back1 = send_back(second)
    keep, out = call(
        weight_gradient_kernel,
        (shape((768, 384), F32), shape((768, 384))),
        [SM, VM, VM] + [ANY] * len(blocks),
        2 * T * D * 384,
        [
            pltpu.VMEM((384, T), BF),
            pltpu.VMEM((T, D), BF),
            pltpu.VMEM((384, D), F32),
            pltpu.SemaphoreType.DMA((len(blocks),)),
        ],
    )(place, first, second, *blocks)
    got = sibling(out)
    partial = call(add_kernel, shape((64, 12, 384)), [VM, VM])(keep, got)
    partial, back1, weight_half, weight_rest = tie((partial, back1, weight_half, weight_rest))
    weights = [projection, beside, weight_half, weight_rest]
    weights += [sibling(weight_half), sibling(weight_rest)]
    partial = lax.all_to_all(partial, ("dp", "zh", "seq"), 0, 0, tiled=True)
    context, input_gradient = call(
        input_gradient_kernel,
        (shape((ROWS, 1024)), shape((ROWS, D), F32)),
        [SM, VM, VM] + [ANY] * 6 + [VM],
        2 * ROWS * D * 3072,
        [
            pltpu.VMEM((ROWS, 3072), BF),
            pltpu.VMEM((4, 384, 3072), BF),
            pltpu.SemaphoreType.DMA((6,)),
        ],
    )(owners, back0, back1, *weights, x)
    partial, context, input_gradient = tie((partial, context, input_gradient))
    projection_gradient = call(combine_kernel, shape((12, 3072), F32), [VM])(partial)
    return (context[None], input_gradient[None], projection_gradient)


def solution(mesh):
    split = jax.sharding.Mesh(mesh.devices.reshape(4, 2, 2, 8), ("dp", "zh", "core", "seq"))
    record = ("dp", "zh", "core")
    placed = (P(record, "seq", None), P(("zh", "core"), None), P(record), P(record, "seq", None))
    return jax.shard_map(
        body,
        mesh=split,
        in_specs=placed,
        out_specs=(P(record, "seq", None), P(record, "seq", None), P((*record, "seq"), None)),
        check_vma=False,
    )
```

```python
import functools

import jax
import jax.numpy as jnp
from jax import lax
from jax.experimental import pallas as pl
from jax.experimental.pallas import tpu as pltpu
from jax.sharding import PartitionSpec as P

BF = jnp.bfloat16
F32 = jnp.float32
D = 1536
HD = 64
T = 2048
ROWS = 256
SEQ = 8
GW = 128
EPS = 1e-05
BQ = 256
AQ = 512
CH = 256
NC = T // CH
VM = pl.BlockSpec(memory_space=pltpu.VMEM)
SM = pl.BlockSpec(memory_space=pltpu.SMEM)
ANY = pl.BlockSpec(memory_space=pl.ANY)


def dot(a, b, dims=((1,), (0,))):
    return lax.dot_general(a, b, (dims, ((), ())), preferred_element_type=F32)


def standardize(x):
    centered = x - jnp.mean(x, axis=1, keepdims=True)
    inv_std = lax.rsqrt(jnp.mean(centered * centered, axis=1, keepdims=True) + EPS)
    return centered * inv_std, inv_std


def fetch(pairs, sems):
    copies = [pltpu.make_async_copy(a, b, sems.at[i]) for i, (a, b) in enumerate(pairs)]
    for copy in copies:
        copy.start()
    return copies


def prepare_kernel(y_ref, x_ref, w_ref, normed_ref, columns_ref, held, sems):
    pairs = []
    for z in range(2):
        for kind in range(3):
            first = pl.multiple_of(kind * 1024 + (z * 4 + y_ref[0]) * GW, GW)
            pairs.append((w_ref.at[:, pl.ds(first, GW)], held.at[z * 3 + kind]))
    copies = fetch(pairs, sems)
    normed_ref[...] = standardize(x_ref[...].astype(F32))[0].astype(BF)
    for copy in copies:
        copy.wait()
    for z in range(2):
        k, v = (held[z * 3 + kind].astype(F32) for kind in (1, 2))
        low = lax.broadcasted_iota(jnp.int32, k.shape, 1) < HD
        at = z * 384
        columns_ref[:, at : at + 128] = jnp.where(low, k, pltpu.roll(v, HD, 1)).astype(BF)
        columns_ref[:, at + 128 : at + 256] = jnp.where(low, pltpu.roll(k, HD, 1), v).astype(BF)
        columns_ref[:, at + 256 : at + 384] = held[z * 3]


def project_kernel(n, owner_ref, group_ref, *refs):
    weights, blocks, outs = refs[:4], refs[4 : 4 + n], refs[4 + n : -3]
    held_weight, held, sems = refs[-3:]
    pairs = []
    for j in range(len(outs)):
        cols = pl.ds(pl.multiple_of(group_ref[j] * 384, 384), 384)
        for f in range(4):
            rows = pl.ds(pl.multiple_of(owner_ref[f] * 384, 384), 384)
            pairs.append((weights[f].at[:, cols], held_weight.at[j, rows, :]))
    at = [sum(b.shape[0] for b in blocks[:i]) for i in range(n)]
    spots = [pl.ds(a, b.shape[0]) for a, b in zip(at, blocks)]
    pairs += [(b, held.at[spot]) for b, spot in zip(blocks, spots)]
    copies = fetch(pairs, sems)
    for copy in copies[: -n]:
        copy.wait()
    for i in range(n):
        copies[i - n].wait()
        for j, out_ref in enumerate(outs[:2]):
            out_ref[spots[i], :] = dot(held[spots[i], :], held_weight[j]).astype(BF)


def attention_kernel(
    head, pos_ref, len_ref, kept_ref, far_ref, other_ref, last_ref, up_ref, out_ref, kv, ka, vt, kt, qt, ut, s_ref, e_ref, acc
):
    length = len_ref[0]
    hrows = slice(head * HD, (head + 1) * HD)
    lane = lax.broadcasted_iota(jnp.int32, (BQ, 128), 1)
    for b in range(SEQ):
        r = slice(b * BQ, (b + 1) * BQ)
        source, at = (
            (kept_ref, 0), (kept_ref, 1), (kept_ref, 2), (far_ref, 0),
            (kept_ref, 3), (other_ref, 0), (other_ref, 1), (last_ref, 0),
        )[b]
        own = slice(at * BQ, (at + 1) * BQ)
        first = pl.multiple_of(pos_ref[b] * BQ, BQ)
        mine = source[own, head * 128 : (head + 1) * 128]
        kv[r, :] = mine
        keys = mine.astype(F32)
        row = lax.broadcasted_iota(jnp.int32, (BQ, 128), 0) + first
        bias = jnp.where(lane == HD, jnp.where(row < length, 0.0, -1e30), 0.0)
        ka[r, :] = jnp.where(lane < HD, keys, bias).astype(BF)
        flipped = keys.T.astype(BF)
        kt[:, r] = flipped[0:HD]
        vt[0:HD, r] = flipped[HD:128]
        vt[HD : HD + 16, r] = jnp.ones((16, BQ), BF)
        qt[:, r] = (source[own, 256:384].astype(F32) * 0.125).T[hrows].astype(BF)
        u = jnp.where(row < length, up_ref[pl.ds(first, BQ), :].astype(F32), 0.0)
        ut[:, r] = u.T[hrows].astype(BF)
    acc[...] = jnp.zeros_like(acc)
    zeros = jnp.zeros((HD, AQ), BF)
    ones_row = jnp.where(lax.broadcasted_iota(jnp.int32, (HD, AQ), 0) == 0, 1.0, 0.0).astype(BF)
    nt = ((1,), (1,))

    def scores(start, j, c):
        r = slice(c * CH, (c + 1) * CH)
        qa = jnp.concatenate([qt[:, pl.ds(start, AQ)], ones_row], axis=0)
        s = dot(ka[r, :], qa)
        s_ref[j, r, :] = s
        return jnp.max(s.reshape(CH // 8, 8, AQ), axis=0)

    def weigh(peak, j, c):
        r = slice(c * CH, (c + 1) * CH)
        e = jnp.exp(s_ref[j, r, :] - peak).astype(BF)
        e_ref[j, r, :] = e
        return dot(vt[:, r], e)

    def finish(total, start):
        cols = pl.ds(start, AQ)
        inverse = 1.0 / total[HD : HD + 1]
        context = total[0:HD] * inverse
        up = (ut[:, cols].astype(F32) * inverse).astype(BF)
        inner = jnp.sum(up.astype(F32) * context, axis=0, keepdims=True)
        up = jnp.concatenate([zeros, up], axis=0)
        query = jnp.concatenate([qt[:, cols], zeros], axis=0)
        return context, up, query, inner

    def back(state, j, c):
        r = slice(c * CH, (c + 1) * CH)
        context, up, query, inner = state
        e = e_ref[j, r, :]
        ds = (e.astype(F32) * (dot(kv[r, :], up) - inner)).astype(BF)
        acc[r, :] += dot(ds, query, nt) + dot(e, up, nt)
        return dot(kt[:, r], ds)

    def write(block, context, dq):
        for p in range(AQ // BQ):
            part = slice(p * BQ, (p + 1) * BQ)
            first = pl.multiple_of(pos_ref[block * (AQ // BQ) + p] * BQ, BQ)
            col = lax.broadcasted_iota(jnp.int32, (HD, BQ), 1) + first
            kept = jnp.where(col < length, context[:, part], 0.0)
            both = jnp.concatenate([dq[:, part] * 0.125, kept], axis=0)
            out_ref[pl.ds(first, BQ), 0:128] = both.T.astype(BF)

    def add(a, b):
        return b if a is None else a + b

    def top(peak):
        return jnp.max(peak, axis=0, keepdims=True)

    def step(i, peak):
        starts = [pl.multiple_of((2 * i + j) * AQ, AQ) for j in range(2)]
        after = pl.multiple_of(lax.rem(2 * i + 2, T // AQ) * AQ, AQ)
        peak, peak1, total, total1 = top(peak), None, None, None
        for c in range(NC):
            t = scores(starts[1], 1, c)
            peak1 = t if c == 0 else jnp.maximum(peak1, t)
            total = add(total, weigh(peak, 0, c))
        state = finish(total, starts[0])
        peak1, dq = top(peak1), None
        for c in range(NC):
            total1 = add(total1, weigh(peak1, 1, c))
            dq = add(dq, back(state, 0, c))
        state1 = finish(total1, starts[1])
        write(2 * i, state[0], dq)
        dq = None
        for c in range(NC):
            t = scores(after, 0, c)
            peak = t if c == 0 else jnp.maximum(peak, t)
            dq = add(dq, back(state1, 1, c))
        write(2 * i + 1, state1[0], dq)
        return peak

    peak = None
    for c in range(NC):
        t = scores(0, 0, c)
        peak = t if c == 0 else jnp.maximum(peak, t)
    lax.fori_loop(0, T // AQ // 2, step, peak)
    for b in range(SEQ):
        rows = pl.ds(pl.multiple_of(pos_ref[b] * BQ, BQ), BQ)
        out_ref[rows, 128:256] = acc[b * BQ : (b + 1) * BQ, :].astype(BF)


def weight_gradient_kernel(pos_ref, first_ref, second_ref, *refs):
    sources, (keep_ref, send_ref, flipped_ref, held, acc, sems) = refs[:-6], refs[-6:]
    at = [sum(b.shape[0] for b in sources[:i]) for i in range(len(sources))]
    spots = [pl.ds(a, b.shape[0]) for a, b in zip(at, sources)]
    copies = fetch([(b, held.at[spot]) for b, spot in zip(sources, spots)], sems)
    for b in range(SEQ):
        rows = pl.ds(pl.multiple_of(pos_ref[b] * ROWS, ROWS), ROWS)
        cols = slice(b * ROWS, (b + 1) * ROWS)
        both = [g[rows, :].astype(F32).T.astype(BF) for g in (first_ref, second_ref)]
        parts = [g[128:256] for g in both] + [g[0:HD] for g in both]
        flipped_ref[:, cols] = jnp.concatenate(parts, axis=0)
    for half in range(2):
        rows = slice(half * T // 2, (half + 1) * T // 2)
        for i, copy in enumerate(copies):
            if at[i] // (T // 2) == half:
                copy.wait()
        for c in range(3):
            cs = slice(c * 512, (c + 1) * 512)
            t = dot(flipped_ref[:, rows], held[rows, cs])
            acc[:, cs] = t if half == 0 else acc[:, cs] + t
    core = pos_ref[SEQ]
    for c in range(4):
        flipped = acc[:, c * 384 : (c + 1) * 384].T
        halves = [[flipped[i * 96 : (i + 1) * 96] for i in (k, k + 2)] for k in range(2)]
        for k in range(2):
            for i in range(2):
                r = slice((c * 2 + i) * 96, (c * 2 + i + 1) * 96)

                @pl.when(core == k)
                def _():
                    keep_ref[r, :] = halves[k][i]

                @pl.when(core != k)
                def _():
                    send_ref[r, :] = halves[k][i].astype(BF)


def join(first, second, part):
    low = lax.broadcasted_iota(jnp.int32, first.shape, first.ndim - 1) < HD
    if part == 0:
        return jnp.where(low, first, pltpu.roll(second, HD, first.ndim - 1))
    return jnp.where(low, pltpu.roll(first, HD, first.ndim - 1), second)


def add_kernel(keep_ref, got_ref, out_ref):
    for i in range(64 // 8):
        rows = slice(i * 96, (i + 1) * 96)
        t = keep_ref[rows, :] + got_ref[rows, :].astype(F32)
        for s in range(SEQ):
            out_ref[i * SEQ + s] = t[s * 12 : (s + 1) * 12].astype(BF)


def combine_kernel(parts_ref, out_ref):
    for s in range(SEQ):
        total = None
        for r in range(8):
            t = parts_ref[r * SEQ + s].astype(F32)
            total = t if total is None else total + t
        at = s * GW
        low, high = total[:, 0:128], total[:, 128:256]
        out_ref[:, at : at + GW] = total[:, 256:384]
        out_ref[:, 1024 + at : 1024 + at + GW] = join(low, high, 0)
        out_ref[:, 2048 + at : 2048 + at + GW] = join(low, high, 1)


def input_gradient_kernel(
    pos_ref, first_ref, second_ref, w0, w1, w2, w3, w4, w5, x_ref, ctx_ref, out_ref, packed, held, sems
):
    halves = [held.at[f, :, pl.ds(p * 1536, 1536)] for f in (2, 3) for p in range(2)]
    copies = fetch(list(zip((w0, w1, w2, w3, w4, w5), [held.at[0], held.at[1]] + halves)), sems)
    for s in range(SEQ):
        at = s * GW
        a = [first_ref[s, :, i * 128 : (i + 1) * 128].astype(F32) for i in range(2)]
        b = [second_ref[s, :, i * 128 : (i + 1) * 128].astype(F32) for i in range(2)]
        ctx_ref[:, at : at + GW] = join(a[0], b[0], 1).astype(BF)
        packed[:, at : at + GW] = join(a[0], b[0], 0).astype(BF)
        packed[:, 1024 + at : 1024 + at + GW] = join(a[1], b[1], 0).astype(BF)
        packed[:, 2048 + at : 2048 + at + GW] = join(a[1], b[1], 1).astype(BF)
    nt = ((1,), (1,))
    for f in range(4):
        to = pl.ds(pl.multiple_of(pos_ref[f] * 384, 384), 384)
        if f < 2:
            copies[f].wait()
            out_ref[:, to] = dot(packed[...], held[f], nt)
        else:
            total = None
            for p in range(2):
                copies[2 * f - 2 + p].wait()
                cols = pl.ds(pl.multiple_of((pos_ref[4] ^ p) * 1536, 1536), 1536)
                t = dot(packed[:, cols], held[f, :, p * 1536 : (p + 1) * 1536], nt)
                total = t if p == 0 else total + t
            out_ref[:, to] = total
    standard, inv_std = standardize(x_ref[...].astype(F32))
    ng = out_ref[...]
    row_mean = jnp.mean(ng, axis=1, keepdims=True)
    projected = jnp.mean(ng * standard, axis=1, keepdims=True)
    out_ref[...] = inv_std * (ng - row_mean - standard * projected)


def shape(dims, dtype=BF):
    return jax.ShapeDtypeStruct(dims, dtype)


UP = [(i, (i // 4) * 4 + (i % 4 + 1) % 4) for i in range(8)]
DOWN = [(i, (i // 4) * 4 + (i % 4 + 3) % 4) for i in range(8)]
ACROSS = [(i, i ^ 4) for i in range(8)]
SWAP = [(f * 8 + s, (f ^ 1) * 8 + (s ^ 4)) for f in range(2) for s in range(8)]
OFFSETS = [(dz, dy) for dz in range(2) for dy in (0, 3, 1, 2)]
HEAD_FLOPS = (10**9, 10**10)
tie = lax.optimization_barrier


def send(v, way):
    return lax.ppermute(v, "seq", way)


def sibling(v):
    return lax.ppermute(v, "core", [(0, 1), (1, 0)])


def swap(v):
    return lax.ppermute(v, ("zh", "seq"), SWAP)


def call(kernel, out, in_specs, flops=0, scratch=(), transcendentals=0, vmem=56):
    return pl.pallas_call(
        kernel,
        out_shape=out,
        in_specs=in_specs,
        out_specs=jax.tree.map(lambda _: VM, out),
        scratch_shapes=list(scratch),
        compiler_params=pltpu.CompilerParams(vmem_limit_bytes=vmem * 2**20),
        cost_estimate=pl.CostEstimate(
            flops=flops, bytes_accessed=2**20, transcendentals=transcendentals
        ),
    )


def body(frames, projection, lengths, cotangent):
    x = frames[0]
    me = lax.axis_index("seq")
    core = lax.axis_index("core")
    fsdp = lax.axis_index("zh") * 2 + core
    half = ROWS // 2
    normed, mine = call(
        prepare_kernel,
        (shape((ROWS, D)), shape((384, 768))),
        [SM, VM, ANY],
        scratch=[pltpu.VMEM((6, 384, GW), BF), pltpu.SemaphoreType.DMA((6,))],
    )((me % 4)[None].astype(jnp.int32), x, projection)
    upstream = cotangent[0].reshape(ROWS, SEQ, GW).transpose(1, 0, 2)
    index = [(me // 4 ^ dz) * 4 + (me % 4 + dy) % 4 for dz, dy in OFFSETS]
    place = jnp.stack(index + [core]).astype(jnp.int32)
    owners = jnp.stack([fsdp ^ i for i in range(4)] + [lax.axis_index("dp") % 2]).astype(jnp.int32)

    beside, other = sibling(mine), send(normed, ACROSS)
    above, below = send(normed, DOWN), send(normed, UP)
    over = swap(mine)
    upstream = lax.all_to_all(tie((upstream, normed))[0], "seq", 0, 0, tiled=True).reshape(T, GW)
    here = me // 4
    groups = jnp.stack([1 - here, here, 1 - here]).astype(jnp.int32)
    parity = lax.axis_index("dp") % 2
    weight_half = lax.dynamic_slice_in_dim(projection, parity * 1536, 1536, 1)
    beside, other, above, below, over, upstream, place, owners, weight_half, groups, turned = tie(
        (beside, other, above, below, over, upstream, place, owners, weight_half, groups, groups[1:])
    )
    far = [send(below[:half], UP), send(above[half:], DOWN)]
    columns = [mine, beside, over, sibling(over)]

    def project(rows, groups, count):
        height = sum(r.shape[0] for r in rows)
        return call(
            functools.partial(project_kernel, len(rows)),
            (shape((height, 384)),) * count,
            [SM, SM] + [ANY] * (4 + len(rows)),
            scratch=[
                pltpu.VMEM((count, D, 384), BF),
                pltpu.VMEM((height, D), BF),
                pltpu.SemaphoreType.DMA((4 * count + len(rows),)),
            ],
        )(owners, groups, *columns, *rows)

    (near,) = project([below, above], groups, 1)
    near_got = send(near, ACROSS)
    _, turned = tie((near, turned))
    (kept,) = project([normed, below, above, other], turned, 1)
    _, far = tie((kept, far))
    last, far_kept = project(far, groups, 2)
    _, other_late, near_got = tie((last, other, near_got))
    other_below, other_above = send(other_late, UP), send(other_late, DOWN)
    weight_half = swap(weight_half)
    far_got, far_late = tie((send(last, ACROSS), far))
    other_far = [send(v, ACROSS) for v in far_late]

    def attend(head):
        return call(
            functools.partial(attention_kernel, head),
            shape((T, 256)),
            [SM, SM] + [VM] * 5,
            HEAD_FLOPS[head],
            [
                pltpu.VMEM((T, 128), BF),
                pltpu.VMEM((T, 128), BF),
                pltpu.VMEM((HD + 16, T), BF),
                pltpu.VMEM((HD, T), BF),
                pltpu.VMEM((HD, T), BF),
                pltpu.VMEM((HD, T), BF),
                pltpu.VMEM((2, T, AQ), F32),
                pltpu.VMEM((2, T, AQ), BF),
                pltpu.VMEM((T, 128), F32),
            ],
            T * T,
        )(place, lengths, kept, far_kept, near_got, far_got, upstream)

    def send_back(grads):
        return lax.all_to_all(grads.reshape(SEQ, ROWS, 256), "seq", 0, 0, tiled=True)

    first = attend(0)
    other_below, other_above, other_far, first, weight, weight_half = tie(
        (other_below, other_above, other_far, first, projection, weight_half)
    )
    weight_rest = lax.ppermute(weight_half, "dp", [(i, i ^ 1) for i in range(4)])
    back0 = send_back(first)
    beside = sibling(weight)
    second = attend(1)
    second, back0, beside = tie((second, back0, beside))
    blocks = [normed, below, above, *far, other, other_below, other_above, *other_far]
    back1 = send_back(second)
    keep, out = call(
        weight_gradient_kernel,
        (shape((768, 384), F32), shape((768, 384))),
        [SM, VM, VM] + [ANY] * len(blocks),
        2 * T * D * 384,
        [
            pltpu.VMEM((384, T), BF),
            pltpu.VMEM((T, D), BF),
            pltpu.VMEM((384, D), F32),
            pltpu.SemaphoreType.DMA((len(blocks),)),
        ],
    )(place, first, second, *blocks)
    got = sibling(out)
    partial = call(add_kernel, shape((64, 12, 384)), [VM, VM])(keep, got)
    partial, back1, weight_half, weight_rest = tie((partial, back1, weight_half, weight_rest))
    weights = [projection, beside, weight_half, weight_rest]
    weights += [sibling(weight_half), sibling(weight_rest)]
    partial = lax.all_to_all(partial, ("dp", "zh", "seq"), 0, 0, tiled=True)
    context, input_gradient = call(
        input_gradient_kernel,
        (shape((ROWS, 1024)), shape((ROWS, D), F32)),
        [SM, VM, VM] + [ANY] * 6 + [VM],
        2 * ROWS * D * 3072,
        [
            pltpu.VMEM((ROWS, 3072), BF),
            pltpu.VMEM((4, 384, 3072), BF),
            pltpu.SemaphoreType.DMA((6,)),
        ],
    )(owners, back0, back1, *weights, x)
    partial, context, input_gradient = tie((partial, context, input_gradient))
    projection_gradient = call(combine_kernel, shape((12, 3072), F32), [VM])(partial)
    return (context[None], input_gradient[None], projection_gradient)


def solution(mesh):
    split = jax.sharding.Mesh(mesh.devices.reshape(4, 2, 2, 8), ("dp", "zh", "core", "seq"))
    record = ("dp", "zh", "core")
    placed = (P(record, "seq", None), P(("zh", "core"), None), P(record), P(record, "seq", None))
    return jax.shard_map(
        body,
        mesh=split,
        in_specs=placed,
        out_specs=(P(record, "seq", None), P(record, "seq", None), P((*record, "seq"), None)),
        check_vma=False,
    )
```

```python
import functools

import jax
import jax.numpy as jnp
from jax import lax
from jax.experimental import pallas as pl
from jax.experimental.pallas import tpu as pltpu
from jax.sharding import PartitionSpec as P

BF = jnp.bfloat16
F32 = jnp.float32
D = 1536
HD = 64
T = 2048
ROWS = 256
SEQ = 8
GW = 128
EPS = 1e-05
BQ = 256
AQ = 512
CH = 256
NC = T // CH
VM = pl.BlockSpec(memory_space=pltpu.VMEM)
SM = pl.BlockSpec(memory_space=pltpu.SMEM)
ANY = pl.BlockSpec(memory_space=pl.ANY)


def dot(a, b, dims=((1,), (0,))):
    return lax.dot_general(a, b, (dims, ((), ())), preferred_element_type=F32)


def standardize(x):
    centered = x - jnp.mean(x, axis=1, keepdims=True)
    inv_std = lax.rsqrt(jnp.mean(centered * centered, axis=1, keepdims=True) + EPS)
    return centered * inv_std, inv_std


def fetch(pairs, sems):
    copies = [pltpu.make_async_copy(a, b, sems.at[i]) for i, (a, b) in enumerate(pairs)]
    for copy in copies:
        copy.start()
    return copies


def prepare_kernel(y_ref, x_ref, w_ref, normed_ref, columns_ref, held, sems):
    pairs = []
    for z in range(2):
        for kind in range(3):
            first = pl.multiple_of(kind * 1024 + (z * 4 + y_ref[0]) * GW, GW)
            pairs.append((w_ref.at[:, pl.ds(first, GW)], held.at[z * 3 + kind]))
    copies = fetch(pairs, sems)
    normed_ref[...] = standardize(x_ref[...].astype(F32))[0].astype(BF)
    for copy in copies:
        copy.wait()
    for z in range(2):
        k, v = (held[z * 3 + kind].astype(F32) for kind in (1, 2))
        low = lax.broadcasted_iota(jnp.int32, k.shape, 1) < HD
        at = z * 384
        columns_ref[:, at : at + 128] = jnp.where(low, k, pltpu.roll(v, HD, 1)).astype(BF)
        columns_ref[:, at + 128 : at + 256] = jnp.where(low, pltpu.roll(k, HD, 1), v).astype(BF)
        columns_ref[:, at + 256 : at + 384] = held[z * 3]


def project_kernel(n, owner_ref, group_ref, *refs):
    weights, blocks, outs = refs[:4], refs[4 : 4 + n], refs[4 + n : -3]
    held_weight, held, sems = refs[-3:]
    pairs = []
    for j in range(len(outs)):
        cols = pl.ds(pl.multiple_of(group_ref[j] * 384, 384), 384)
        for f in range(4):
            rows = pl.ds(pl.multiple_of(owner_ref[f] * 384, 384), 384)
            pairs.append((weights[f].at[:, cols], held_weight.at[j, rows, :]))
    at = [sum(b.shape[0] for b in blocks[:i]) for i in range(n)]
    spots = [pl.ds(a, b.shape[0]) for a, b in zip(at, blocks)]
    pairs += [(b, held.at[spot]) for b, spot in zip(blocks, spots)]
    copies = fetch(pairs, sems)
    for copy in copies[: -n]:
        copy.wait()
    for i in range(n):
        copies[i - n].wait()
        for j, out_ref in enumerate(outs[:2]):
            out_ref[spots[i], :] = dot(held[spots[i], :], held_weight[j]).astype(BF)


def attention_kernel(
    head, pos_ref, len_ref, kept_ref, far_ref, other_ref, last_ref, up_ref, out_ref, kv, ka, vt, kt, qt, ut, s_ref, e_ref, acc
):
    length = len_ref[0]
    hrows = slice(head * HD, (head + 1) * HD)
    lane = lax.broadcasted_iota(jnp.int32, (BQ, 128), 1)
    for b in range(SEQ):
        r = slice(b * BQ, (b + 1) * BQ)
        source, at = (
            (kept_ref, 0), (kept_ref, 1), (kept_ref, 2), (far_ref, 0),
            (kept_ref, 3), (other_ref, 0), (other_ref, 1), (last_ref, 0),
        )[b]
        own = slice(at * BQ, (at + 1) * BQ)
        first = pl.multiple_of(pos_ref[b] * BQ, BQ)
        mine = source[own, head * 128 : (head + 1) * 128]
        kv[r, :] = mine
        keys = mine.astype(F32)
        row = lax.broadcasted_iota(jnp.int32, (BQ, 128), 0) + first
        bias = jnp.where(lane == HD, jnp.where(row < length, 0.0, -1e30), 0.0)
        ka[r, :] = jnp.where(lane < HD, keys, bias).astype(BF)
        flipped = keys.T.astype(BF)
        kt[:, r] = flipped[0:HD]
        vt[0:HD, r] = flipped[HD:128]
        vt[HD : HD + 16, r] = jnp.ones((16, BQ), BF)
        qt[:, r] = (source[own, 256:384].astype(F32) * 0.125).T[hrows].astype(BF)
        u = jnp.where(row < length, up_ref[pl.ds(first, BQ), :].astype(F32), 0.0)
        ut[:, r] = u.T[hrows].astype(BF)
    acc[...] = jnp.zeros_like(acc)
    zeros = jnp.zeros((HD, AQ), BF)
    ones_row = jnp.where(lax.broadcasted_iota(jnp.int32, (HD, AQ), 0) == 0, 1.0, 0.0).astype(BF)
    nt = ((1,), (1,))

    def scores(start, j, c):
        r = slice(c * CH, (c + 1) * CH)
        qa = jnp.concatenate([qt[:, pl.ds(start, AQ)], ones_row], axis=0)
        s = dot(ka[r, :], qa)
        s_ref[j, r, :] = s
        return jnp.max(s.reshape(CH // 8, 8, AQ), axis=0)

    def weigh(peak, j, c):
        r = slice(c * CH, (c + 1) * CH)
        e = jnp.exp(s_ref[j, r, :] - peak).astype(BF)
        e_ref[j, r, :] = e
        return dot(vt[:, r], e)

    def finish(total, start):
        cols = pl.ds(start, AQ)
        inverse = 1.0 / total[HD : HD + 1]
        context = total[0:HD] * inverse
        up = (ut[:, cols].astype(F32) * inverse).astype(BF)
        inner = jnp.sum(up.astype(F32) * context, axis=0, keepdims=True)
        up = jnp.concatenate([zeros, up], axis=0)
        query = jnp.concatenate([qt[:, cols], zeros], axis=0)
        return context, up, query, inner

    def back(state, j, c):
        r = slice(c * CH, (c + 1) * CH)
        context, up, query, inner = state
        e = e_ref[j, r, :]
        ds = (e.astype(F32) * (dot(kv[r, :], up) - inner)).astype(BF)
        acc[r, :] += dot(ds, query, nt) + dot(e, up, nt)
        return dot(kt[:, r], ds)

    def write(block, context, dq):
        for p in range(AQ // BQ):
            part = slice(p * BQ, (p + 1) * BQ)
            first = pl.multiple_of(pos_ref[block * (AQ // BQ) + p] * BQ, BQ)
            col = lax.broadcasted_iota(jnp.int32, (HD, BQ), 1) + first
            kept = jnp.where(col < length, context[:, part], 0.0)
            both = jnp.concatenate([dq[:, part] * 0.125, kept], axis=0)
            out_ref[pl.ds(first, BQ), 0:128] = both.T.astype(BF)

    def add(a, b):
        return b if a is None else a + b

    def top(peak):
        return jnp.max(peak, axis=0, keepdims=True)

    def step(i, peak):
        starts = [pl.multiple_of((2 * i + j) * AQ, AQ) for j in range(2)]
        after = pl.multiple_of(lax.rem(2 * i + 2, T // AQ) * AQ, AQ)
        peak, peak1, total, total1 = top(peak), None, None, None
        for c in range(NC):
            t = scores(starts[1], 1, c)
            peak1 = t if c == 0 else jnp.maximum(peak1, t)
            total = add(total, weigh(peak, 0, c))
        state = finish(total, starts[0])
        peak1, dq = top(peak1), None
        for c in range(NC):
            total1 = add(total1, weigh(peak1, 1, c))
            dq = add(dq, back(state, 0, c))
        state1 = finish(total1, starts[1])
        write(2 * i, state[0], dq)
        dq = None
        for c in range(NC):
            t = scores(after, 0, c)
            peak = t if c == 0 else jnp.maximum(peak, t)
            dq = add(dq, back(state1, 1, c))
        write(2 * i + 1, state1[0], dq)
        return peak

    peak = None
    for c in range(NC):
        t = scores(0, 0, c)
        peak = t if c == 0 else jnp.maximum(peak, t)
    lax.fori_loop(0, T // AQ // 2, step, peak)
    for b in range(SEQ):
        rows = pl.ds(pl.multiple_of(pos_ref[b] * BQ, BQ), BQ)
        out_ref[rows, 128:256] = acc[b * BQ : (b + 1) * BQ, :].astype(BF)


def weight_gradient_kernel(pos_ref, first_ref, second_ref, *refs):
    sources, (keep_ref, send_ref, flipped_ref, held, acc, sems) = refs[:-6], refs[-6:]
    at = [sum(b.shape[0] for b in sources[:i]) for i in range(len(sources))]
    spots = [pl.ds(a, b.shape[0]) for a, b in zip(at, sources)]
    copies = fetch([(b, held.at[spot]) for b, spot in zip(sources, spots)], sems)
    for b in range(SEQ):
        rows = pl.ds(pl.multiple_of(pos_ref[b] * ROWS, ROWS), ROWS)
        cols = slice(b * ROWS, (b + 1) * ROWS)
        both = [g[rows, :].astype(F32).T.astype(BF) for g in (first_ref, second_ref)]
        parts = [g[128:256] for g in both] + [g[0:HD] for g in both]
        flipped_ref[:, cols] = jnp.concatenate(parts, axis=0)
    for half in range(2):
        rows = slice(half * T // 2, (half + 1) * T // 2)
        for i, copy in enumerate(copies):
            if at[i] // (T // 2) == half:
                copy.wait()
        for c in range(3):
            cs = slice(c * 512, (c + 1) * 512)
            t = dot(flipped_ref[:, rows], held[rows, cs])
            acc[:, cs] = t if half == 0 else acc[:, cs] + t
    core = pos_ref[SEQ]
    for c in range(4):
        flipped = acc[:, c * 384 : (c + 1) * 384].T
        halves = [[flipped[i * 96 : (i + 1) * 96] for i in (k, k + 2)] for k in range(2)]
        for k in range(2):
            for i in range(2):
                r = slice((c * 2 + i) * 96, (c * 2 + i + 1) * 96)

                @pl.when(core == k)
                def _():
                    keep_ref[r, :] = halves[k][i]

                @pl.when(core != k)
                def _():
                    send_ref[r, :] = halves[k][i].astype(BF)


def join(first, second, part):
    low = lax.broadcasted_iota(jnp.int32, first.shape, first.ndim - 1) < HD
    if part == 0:
        return jnp.where(low, first, pltpu.roll(second, HD, first.ndim - 1))
    return jnp.where(low, pltpu.roll(first, HD, first.ndim - 1), second)


def add_kernel(keep_ref, got_ref, out_ref):
    for i in range(64 // 8):
        rows = slice(i * 96, (i + 1) * 96)
        t = keep_ref[rows, :] + got_ref[rows, :].astype(F32)
        for s in range(SEQ):
            out_ref[i * SEQ + s] = t[s * 12 : (s + 1) * 12].astype(BF)


def combine_kernel(parts_ref, out_ref):
    for s in range(SEQ):
        total = None
        for r in range(8):
            t = parts_ref[r * SEQ + s].astype(F32)
            total = t if total is None else total + t
        at = s * GW
        low, high = total[:, 0:128], total[:, 128:256]
        out_ref[:, at : at + GW] = total[:, 256:384]
        out_ref[:, 1024 + at : 1024 + at + GW] = join(low, high, 0)
        out_ref[:, 2048 + at : 2048 + at + GW] = join(low, high, 1)


def input_gradient_kernel(
    pos_ref, first_ref, second_ref, w0, w1, w2, w3, w4, w5, x_ref, ctx_ref, out_ref, packed, held, sems
):
    halves = [held.at[f, :, pl.ds(p * 1536, 1536)] for f in (2, 3) for p in range(2)]
    copies = fetch(list(zip((w0, w1, w2, w3, w4, w5), [held.at[0], held.at[1]] + halves)), sems)
    for s in range(SEQ):
        at = s * GW
        a = [first_ref[s, :, i * 128 : (i + 1) * 128].astype(F32) for i in range(2)]
        b = [second_ref[s, :, i * 128 : (i + 1) * 128].astype(F32) for i in range(2)]
        ctx_ref[:, at : at + GW] = join(a[0], b[0], 1).astype(BF)
        packed[:, at : at + GW] = join(a[0], b[0], 0).astype(BF)
        packed[:, 1024 + at : 1024 + at + GW] = join(a[1], b[1], 0).astype(BF)
        packed[:, 2048 + at : 2048 + at + GW] = join(a[1], b[1], 1).astype(BF)
    nt = ((1,), (1,))
    for f in range(4):
        to = pl.ds(pl.multiple_of(pos_ref[f] * 384, 384), 384)
        if f < 2:
            copies[f].wait()
            out_ref[:, to] = dot(packed[...], held[f], nt)
        else:
            total = None
            for p in range(2):
                copies[2 * f - 2 + p].wait()
                cols = pl.ds(pl.multiple_of((pos_ref[4] ^ p) * 1536, 1536), 1536)
                t = dot(packed[:, cols], held[f, :, p * 1536 : (p + 1) * 1536], nt)
                total = t if p == 0 else total + t
            out_ref[:, to] = total
    standard, inv_std = standardize(x_ref[...].astype(F32))
    ng = out_ref[...]
    row_mean = jnp.mean(ng, axis=1, keepdims=True)
    projected = jnp.mean(ng * standard, axis=1, keepdims=True)
    out_ref[...] = inv_std * (ng - row_mean - standard * projected)


def shape(dims, dtype=BF):
    return jax.ShapeDtypeStruct(dims, dtype)


UP = [(i, (i // 4) * 4 + (i % 4 + 1) % 4) for i in range(8)]
DOWN = [(i, (i // 4) * 4 + (i % 4 + 3) % 4) for i in range(8)]
ACROSS = [(i, i ^ 4) for i in range(8)]
SWAP = [(f * 8 + s, (f ^ 1) * 8 + (s ^ 4)) for f in range(2) for s in range(8)]
OFFSETS = [(dz, dy) for dz in range(2) for dy in (0, 3, 1, 2)]
HEAD_FLOPS = (10**9, 10**10)
tie = lax.optimization_barrier


def send(v, way):
    return lax.ppermute(v, "seq", way)


def sibling(v):
    return lax.ppermute(v, "core", [(0, 1), (1, 0)])


def swap(v):
    return lax.ppermute(v, ("zh", "seq"), SWAP)


def call(kernel, out, in_specs, flops=0, scratch=(), transcendentals=0, vmem=56):
    return pl.pallas_call(
        kernel,
        out_shape=out,
        in_specs=in_specs,
        out_specs=jax.tree.map(lambda _: VM, out),
        scratch_shapes=list(scratch),
        compiler_params=pltpu.CompilerParams(vmem_limit_bytes=vmem * 2**20),
        cost_estimate=pl.CostEstimate(
            flops=flops, bytes_accessed=2**20, transcendentals=transcendentals
        ),
    )


def body(frames, projection, lengths, cotangent):
    x = frames[0]
    me = lax.axis_index("seq")
    core = lax.axis_index("core")
    fsdp = lax.axis_index("zh") * 2 + core
    half = ROWS // 2
    normed, mine = call(
        prepare_kernel,
        (shape((ROWS, D)), shape((384, 768))),
        [SM, VM, ANY],
        scratch=[pltpu.VMEM((6, 384, GW), BF), pltpu.SemaphoreType.DMA((6,))],
    )((me % 4)[None].astype(jnp.int32), x, projection)
    upstream = cotangent[0].reshape(ROWS, SEQ, GW).transpose(1, 0, 2)
    index = [(me // 4 ^ dz) * 4 + (me % 4 + dy) % 4 for dz, dy in OFFSETS]
    place = jnp.stack(index + [core]).astype(jnp.int32)
    owners = jnp.stack([fsdp ^ i for i in range(4)] + [lax.axis_index("dp") % 2]).astype(jnp.int32)

    beside, other = sibling(mine), send(normed, ACROSS)
    above, below = send(normed, DOWN), send(normed, UP)
    over = swap(mine)
    upstream = lax.all_to_all(tie((upstream, normed))[0], "seq", 0, 0, tiled=True).reshape(T, GW)
    here = me // 4
    groups = jnp.stack([1 - here, here, 1 - here]).astype(jnp.int32)
    parity = lax.axis_index("dp") % 2
    weight_half = lax.dynamic_slice_in_dim(projection, parity * 1536, 1536, 1)
    beside, other, above, below, over, upstream, place, owners, weight_half, groups, turned = tie(
        (beside, other, above, below, over, upstream, place, owners, weight_half, groups, groups[1:])
    )
    far = [send(below[:half], UP), send(above[half:], DOWN)]
    columns = [mine, beside, over, sibling(over)]

    def project(rows, groups, count):
        height = sum(r.shape[0] for r in rows)
        return call(
            functools.partial(project_kernel, len(rows)),
            (shape((height, 384)),) * count,
            [SM, SM] + [ANY] * (4 + len(rows)),
            scratch=[
                pltpu.VMEM((count, D, 384), BF),
                pltpu.VMEM((height, D), BF),
                pltpu.SemaphoreType.DMA((4 * count + len(rows),)),
            ],
        )(owners, groups, *columns, *rows)

    (near,) = project([below, above], groups, 1)
    near_got = send(near, ACROSS)
    _, far = tie((near, far))
    last, far_kept = project(far, groups, 2)
    _, turned = tie((last, turned))
    (kept,) = project([normed, below, above, other], turned, 1)
    _, other_late = tie((last, other))
    other_below, other_above = send(other_late, UP), send(other_late, DOWN)
    weight_half = swap(weight_half)
    far_got, far_late, kept = tie((send(last, ACROSS), far, kept))
    other_far = [send(v, ACROSS) for v in far_late]

    def attend(head):
        return call(
            functools.partial(attention_kernel, head),
            shape((T, 256)),
            [SM, SM] + [VM] * 5,
            HEAD_FLOPS[head],
            [
                pltpu.VMEM((T, 128), BF),
                pltpu.VMEM((T, 128), BF),
                pltpu.VMEM((HD + 16, T), BF),
                pltpu.VMEM((HD, T), BF),
                pltpu.VMEM((HD, T), BF),
                pltpu.VMEM((HD, T), BF),
                pltpu.VMEM((2, T, AQ), F32),
                pltpu.VMEM((2, T, AQ), BF),
                pltpu.VMEM((T, 128), F32),
            ],
            T * T,
        )(place, lengths, kept, far_kept, near_got, far_got, upstream)

    def send_back(grads):
        return lax.all_to_all(grads.reshape(SEQ, ROWS, 256), "seq", 0, 0, tiled=True)

    first = attend(0)
    other_below, other_above, other_far, first, weight, weight_half = tie(
        (other_below, other_above, other_far, first, projection, weight_half)
    )
    weight_rest = lax.ppermute(weight_half, "dp", [(i, i ^ 1) for i in range(4)])
    back0 = send_back(first)
    beside = sibling(weight)
    second = attend(1)
    second, back0, beside = tie((second, back0, beside))
    blocks = [normed, below, above, *far, other, other_below, other_above, *other_far]
    back1 = send_back(second)
    keep, out = call(
        weight_gradient_kernel,
        (shape((768, 384), F32), shape((768, 384))),
        [SM, VM, VM] + [ANY] * len(blocks),
        2 * T * D * 384,
        [
            pltpu.VMEM((384, T), BF),
            pltpu.VMEM((T, D), BF),
            pltpu.VMEM((384, D), F32),
            pltpu.SemaphoreType.DMA((len(blocks),)),
        ],
    )(place, first, second, *blocks)
    got = sibling(out)
    partial = call(add_kernel, shape((64, 12, 384)), [VM, VM])(keep, got)
    partial, back1, weight_half, weight_rest = tie((partial, back1, weight_half, weight_rest))
    weights = [projection, beside, weight_half, weight_rest]
    weights += [sibling(weight_half), sibling(weight_rest)]
    partial = lax.all_to_all(partial, ("dp", "zh", "seq"), 0, 0, tiled=True)
    context, input_gradient = call(
        input_gradient_kernel,
        (shape((ROWS, 1024)), shape((ROWS, D), F32)),
        [SM, VM, VM] + [ANY] * 6 + [VM],
        2 * ROWS * D * 3072,
        [
            pltpu.VMEM((ROWS, 3072), BF),
            pltpu.VMEM((4, 384, 3072), BF),
            pltpu.SemaphoreType.DMA((6,)),
        ],
    )(owners, back0, back1, *weights, x)
    partial, context, input_gradient = tie((partial, context, input_gradient))
    projection_gradient = call(combine_kernel, shape((12, 3072), F32), [VM])(partial)
    return (context[None], input_gradient[None], projection_gradient)


def solution(mesh):
    split = jax.sharding.Mesh(mesh.devices.reshape(4, 2, 2, 8), ("dp", "zh", "core", "seq"))
    record = ("dp", "zh", "core")
    placed = (P(record, "seq", None), P(("zh", "core"), None), P(record), P(record, "seq", None))
    return jax.shard_map(
        body,
        mesh=split,
        in_specs=placed,
        out_specs=(P(record, "seq", None), P(record, "seq", None), P((*record, "seq"), None)),
        check_vma=False,
    )
```

```python
import functools

import jax
import jax.numpy as jnp
from jax import lax
from jax.experimental import pallas as pl
from jax.experimental.pallas import tpu as pltpu
from jax.sharding import PartitionSpec as P

BF = jnp.bfloat16
F32 = jnp.float32
D = 1536
HD = 64
T = 2048
ROWS = 256
SEQ = 8
GW = 128
EPS = 1e-05
BQ = 256
AQ = 512
CH = 256
NC = T // CH
VM = pl.BlockSpec(memory_space=pltpu.VMEM)
SM = pl.BlockSpec(memory_space=pltpu.SMEM)
ANY = pl.BlockSpec(memory_space=pl.ANY)


def dot(a, b, dims=((1,), (0,))):
    return lax.dot_general(a, b, (dims, ((), ())), preferred_element_type=F32)


def standardize(x):
    centered = x - jnp.mean(x, axis=1, keepdims=True)
    inv_std = lax.rsqrt(jnp.mean(centered * centered, axis=1, keepdims=True) + EPS)
    return centered * inv_std, inv_std


def fetch(pairs, sems):
    copies = [pltpu.make_async_copy(a, b, sems.at[i]) for i, (a, b) in enumerate(pairs)]
    for copy in copies:
        copy.start()
    return copies


def prepare_kernel(y_ref, x_ref, w_ref, normed_ref, columns_ref, held, sems):
    pairs = []
    for z in range(2):
        for kind in range(3):
            first = pl.multiple_of(kind * 1024 + (z * 4 + y_ref[0]) * GW, GW)
            pairs.append((w_ref.at[:, pl.ds(first, GW)], held.at[z * 3 + kind]))
    copies = fetch(pairs, sems)
    normed_ref[...] = standardize(x_ref[...].astype(F32))[0].astype(BF)
    for copy in copies:
        copy.wait()
    for z in range(2):
        k, v = (held[z * 3 + kind].astype(F32) for kind in (1, 2))
        low = lax.broadcasted_iota(jnp.int32, k.shape, 1) < HD
        at = z * 384
        columns_ref[:, at : at + 128] = jnp.where(low, k, pltpu.roll(v, HD, 1)).astype(BF)
        columns_ref[:, at + 128 : at + 256] = jnp.where(low, pltpu.roll(k, HD, 1), v).astype(BF)
        columns_ref[:, at + 256 : at + 384] = held[z * 3]


def project_kernel(n, owner_ref, group_ref, *refs):
    weights, blocks, outs = refs[:4], refs[4 : 4 + n], refs[4 + n : -3]
    held_weight, held, sems = refs[-3:]
    pairs = []
    for j in range(len(outs)):
        cols = pl.ds(pl.multiple_of(group_ref[j] * 384, 384), 384)
        for f in range(4):
            rows = pl.ds(pl.multiple_of(owner_ref[f] * 384, 384), 384)
            pairs.append((weights[f].at[:, cols], held_weight.at[j, rows, :]))
    at = [sum(b.shape[0] for b in blocks[:i]) for i in range(n)]
    spots = [pl.ds(a, b.shape[0]) for a, b in zip(at, blocks)]
    pairs += [(b, held.at[spot]) for b, spot in zip(blocks, spots)]
    copies = fetch(pairs, sems)
    for copy in copies[: -n]:
        copy.wait()
    for i in range(n):
        copies[i - n].wait()
        for j, out_ref in enumerate(outs[:2]):
            out_ref[spots[i], :] = dot(held[spots[i], :], held_weight[j]).astype(BF)


def attention_kernel(
    head, pos_ref, len_ref, kept_ref, far_ref, other_ref, last_ref, up_ref, out_ref, kv, ka, vt, kt, qt, ut, s_ref, e_ref, acc
):
    length = len_ref[0]
    hrows = slice(head * HD, (head + 1) * HD)
    lane = lax.broadcasted_iota(jnp.int32, (BQ, 128), 1)
    for b in range(SEQ):
        r = slice(b * BQ, (b + 1) * BQ)
        source, at = (
            (kept_ref, 0), (kept_ref, 1), (kept_ref, 2), (far_ref, 0),
            (kept_ref, 3), (other_ref, 0), (other_ref, 1), (last_ref, 0),
        )[b]
        own = slice(at * BQ, (at + 1) * BQ)
        first = pl.multiple_of(pos_ref[b] * BQ, BQ)
        mine = source[own, head * 128 : (head + 1) * 128]
        kv[r, :] = mine
        keys = mine.astype(F32)
        row = lax.broadcasted_iota(jnp.int32, (BQ, 128), 0) + first
        bias = jnp.where(lane == HD, jnp.where(row < length, 0.0, -1e30), 0.0)
        ka[r, :] = jnp.where(lane < HD, keys, bias).astype(BF)
        flipped = keys.T.astype(BF)
        kt[:, r] = flipped[0:HD]
        vt[0:HD, r] = flipped[HD:128]
        vt[HD : HD + 16, r] = jnp.ones((16, BQ), BF)
        qt[:, r] = (source[own, 256:384].astype(F32) * 0.125).T[hrows].astype(BF)
        u = jnp.where(row < length, up_ref[pl.ds(first, BQ), :].astype(F32), 0.0)
        ut[:, r] = u.T[hrows].astype(BF)
    acc[...] = jnp.zeros_like(acc)
    zeros = jnp.zeros((HD, AQ), BF)
    ones_row = jnp.where(lax.broadcasted_iota(jnp.int32, (HD, AQ), 0) == 0, 1.0, 0.0).astype(BF)
    nt = ((1,), (1,))

    def scores(start, j, c):
        r = slice(c * CH, (c + 1) * CH)
        qa = jnp.concatenate([qt[:, pl.ds(start, AQ)], ones_row], axis=0)
        s = dot(ka[r, :], qa)
        s_ref[j, r, :] = s
        return jnp.max(s.reshape(CH // 8, 8, AQ), axis=0)

    def weigh(peak, j, c):
        r = slice(c * CH, (c + 1) * CH)
        e = jnp.exp(s_ref[j, r, :] - peak).astype(BF)
        e_ref[j, r, :] = e
        return dot(vt[:, r], e)

    def finish(total, start):
        cols = pl.ds(start, AQ)
        inverse = 1.0 / total[HD : HD + 1]
        context = total[0:HD] * inverse
        up = (ut[:, cols].astype(F32) * inverse).astype(BF)
        inner = jnp.sum(up.astype(F32) * context, axis=0, keepdims=True)
        up = jnp.concatenate([zeros, up], axis=0)
        query = jnp.concatenate([qt[:, cols], zeros], axis=0)
        return context, up, query, inner

    def back(state, j, c):
        r = slice(c * CH, (c + 1) * CH)
        context, up, query, inner = state
        e = e_ref[j, r, :]
        ds = (e.astype(F32) * (dot(kv[r, :], up) - inner)).astype(BF)
        acc[r, :] += dot(ds, query, nt) + dot(e, up, nt)
        return dot(kt[:, r], ds)

    def write(block, context, dq):
        for p in range(AQ // BQ):
            part = slice(p * BQ, (p + 1) * BQ)
            first = pl.multiple_of(pos_ref[block * (AQ // BQ) + p] * BQ, BQ)
            col = lax.broadcasted_iota(jnp.int32, (HD, BQ), 1) + first
            kept = jnp.where(col < length, context[:, part], 0.0)
            both = jnp.concatenate([dq[:, part] * 0.125, kept], axis=0)
            out_ref[pl.ds(first, BQ), 0:128] = both.T.astype(BF)

    def add(a, b):
        return b if a is None else a + b

    def top(peak):
        return jnp.max(peak, axis=0, keepdims=True)

    def step(i, peak):
        starts = [pl.multiple_of((2 * i + j) * AQ, AQ) for j in range(2)]
        after = pl.multiple_of(lax.rem(2 * i + 2, T // AQ) * AQ, AQ)
        peak, peak1, total, total1 = top(peak), None, None, None
        for c in range(NC):
            t = scores(starts[1], 1, c)
            peak1 = t if c == 0 else jnp.maximum(peak1, t)
            total = add(total, weigh(peak, 0, c))
        state = finish(total, starts[0])
        peak1, dq = top(peak1), None
        for c in range(NC):
            total1 = add(total1, weigh(peak1, 1, c))
            dq = add(dq, back(state, 0, c))
        state1 = finish(total1, starts[1])
        write(2 * i, state[0], dq)
        dq = None
        for c in range(NC):
            t = scores(after, 0, c)
            peak = t if c == 0 else jnp.maximum(peak, t)
            dq = add(dq, back(state1, 1, c))
        write(2 * i + 1, state1[0], dq)
        return peak

    peak = None
    for c in range(NC):
        t = scores(0, 0, c)
        peak = t if c == 0 else jnp.maximum(peak, t)
    lax.fori_loop(0, T // AQ // 2, step, peak)
    for b in range(SEQ):
        rows = pl.ds(pl.multiple_of(pos_ref[b] * BQ, BQ), BQ)
        out_ref[rows, 128:256] = acc[b * BQ : (b + 1) * BQ, :].astype(BF)


def weight_gradient_kernel(pos_ref, first_ref, second_ref, *refs):
    sources, (keep_ref, send_ref, flipped_ref, held, acc, sems) = refs[:-6], refs[-6:]
    at = [sum(b.shape[0] for b in sources[:i]) for i in range(len(sources))]
    spots = [pl.ds(a, b.shape[0]) for a, b in zip(at, sources)]
    copies = fetch([(b, held.at[spot]) for b, spot in zip(sources, spots)], sems)
    for b in range(SEQ):
        rows = pl.ds(pl.multiple_of(pos_ref[b] * ROWS, ROWS), ROWS)
        cols = slice(b * ROWS, (b + 1) * ROWS)
        both = [g[rows, :].astype(F32).T.astype(BF) for g in (first_ref, second_ref)]
        parts = [g[128:256] for g in both] + [g[0:HD] for g in both]
        flipped_ref[:, cols] = jnp.concatenate(parts, axis=0)
    for half in range(2):
        rows = slice(half * T // 2, (half + 1) * T // 2)
        for i, copy in enumerate(copies):
            if at[i] // (T // 2) == half:
                copy.wait()
        for c in range(3):
            cs = slice(c * 512, (c + 1) * 512)
            t = dot(flipped_ref[:, rows], held[rows, cs])
            acc[:, cs] = t if half == 0 else acc[:, cs] + t
    core = pos_ref[SEQ]
    for c in range(4):
        flipped = acc[:, c * 384 : (c + 1) * 384].T
        halves = [[flipped[i * 96 : (i + 1) * 96] for i in (k, k + 2)] for k in range(2)]
        for k in range(2):
            for i in range(2):
                r = slice((c * 2 + i) * 96, (c * 2 + i + 1) * 96)

                @pl.when(core == k)
                def _():
                    keep_ref[r, :] = halves[k][i]

                @pl.when(core != k)
                def _():
                    send_ref[r, :] = halves[k][i].astype(BF)


def join(first, second, part):
    low = lax.broadcasted_iota(jnp.int32, first.shape, first.ndim - 1) < HD
    if part == 0:
        return jnp.where(low, first, pltpu.roll(second, HD, first.ndim - 1))
    return jnp.where(low, pltpu.roll(first, HD, first.ndim - 1), second)


def add_kernel(keep_ref, got_ref, out_ref):
    for i in range(64 // 8):
        rows = slice(i * 96, (i + 1) * 96)
        t = keep_ref[rows, :] + got_ref[rows, :].astype(F32)
        for s in range(SEQ):
            part = t[s * 12 : (s + 1) * 12]
            part = jnp.concatenate([part[:, k * GW : (k + 1) * GW] for k in range(3)], axis=0)
            out_ref[i * SEQ + s] = part.astype(BF)


def combine_kernel(parts_ref, out_ref):
    for s in range(SEQ):
        total = None
        for r in range(8):
            t = parts_ref[r * SEQ + s].astype(F32)
            total = t if total is None else total + t
        at = s * GW
        low, high = total[0:12], total[12:24]
        out_ref[:, at : at + GW] = total[24:36]
        out_ref[:, 1024 + at : 1024 + at + GW] = join(low, high, 0)
        out_ref[:, 2048 + at : 2048 + at + GW] = join(low, high, 1)


def input_gradient_kernel(
    pos_ref, first_ref, second_ref, w0, w1, w2, w3, w4, w5, x_ref, ctx_ref, out_ref, packed, held, sems
):
    halves = [held.at[f, :, pl.ds(p * 1536, 1536)] for f in (2, 3) for p in range(2)]
    copies = fetch(list(zip((w0, w1, w2, w3, w4, w5), [held.at[0], held.at[1]] + halves)), sems)
    for s in range(SEQ):
        at = s * GW
        a = [first_ref[s, :, i * 128 : (i + 1) * 128].astype(F32) for i in range(2)]
        b = [second_ref[s, :, i * 128 : (i + 1) * 128].astype(F32) for i in range(2)]
        ctx_ref[:, at : at + GW] = join(a[0], b[0], 1).astype(BF)
        packed[:, at : at + GW] = join(a[0], b[0], 0).astype(BF)
        packed[:, 1024 + at : 1024 + at + GW] = join(a[1], b[1], 0).astype(BF)
        packed[:, 2048 + at : 2048 + at + GW] = join(a[1], b[1], 1).astype(BF)
    nt = ((1,), (1,))
    for f in range(4):
        to = pl.ds(pl.multiple_of(pos_ref[f] * 384, 384), 384)
        if f < 2:
            copies[f].wait()
            out_ref[:, to] = dot(packed[...], held[f], nt)
        else:
            total = None
            for p in range(2):
                copies[2 * f - 2 + p].wait()
                cols = pl.ds(pl.multiple_of((pos_ref[4] ^ p) * 1536, 1536), 1536)
                t = dot(packed[:, cols], held[f, :, p * 1536 : (p + 1) * 1536], nt)
                total = t if p == 0 else total + t
            out_ref[:, to] = total
    standard, inv_std = standardize(x_ref[...].astype(F32))
    ng = out_ref[...]
    row_mean = jnp.mean(ng, axis=1, keepdims=True)
    projected = jnp.mean(ng * standard, axis=1, keepdims=True)
    out_ref[...] = inv_std * (ng - row_mean - standard * projected)


def shape(dims, dtype=BF):
    return jax.ShapeDtypeStruct(dims, dtype)


UP = [(i, (i // 4) * 4 + (i % 4 + 1) % 4) for i in range(8)]
DOWN = [(i, (i // 4) * 4 + (i % 4 + 3) % 4) for i in range(8)]
ACROSS = [(i, i ^ 4) for i in range(8)]
SWAP = [(f * 8 + s, (f ^ 1) * 8 + (s ^ 4)) for f in range(2) for s in range(8)]
OFFSETS = [(dz, dy) for dz in range(2) for dy in (0, 3, 1, 2)]
HEAD_FLOPS = (10**9, 10**10)
tie = lax.optimization_barrier


def send(v, way):
    return lax.ppermute(v, "seq", way)


def sibling(v):
    return lax.ppermute(v, "core", [(0, 1), (1, 0)])


def swap(v):
    return lax.ppermute(v, ("zh", "seq"), SWAP)


def call(kernel, out, in_specs, flops=0, scratch=(), transcendentals=0, vmem=56):
    return pl.pallas_call(
        kernel,
        out_shape=out,
        in_specs=in_specs,
        out_specs=jax.tree.map(lambda _: VM, out),
        scratch_shapes=list(scratch),
        compiler_params=pltpu.CompilerParams(vmem_limit_bytes=vmem * 2**20),
        cost_estimate=pl.CostEstimate(
            flops=flops, bytes_accessed=2**20, transcendentals=transcendentals
        ),
    )


def body(frames, projection, lengths, cotangent):
    x = frames[0]
    me = lax.axis_index("seq")
    core = lax.axis_index("core")
    fsdp = lax.axis_index("zh") * 2 + core
    half = ROWS // 2
    normed, mine = call(
        prepare_kernel,
        (shape((ROWS, D)), shape((384, 768))),
        [SM, VM, ANY],
        scratch=[pltpu.VMEM((6, 384, GW), BF), pltpu.SemaphoreType.DMA((6,))],
    )((me % 4)[None].astype(jnp.int32), x, projection)
    upstream = cotangent[0].reshape(ROWS, SEQ, GW).transpose(1, 0, 2)
    index = [(me // 4 ^ dz) * 4 + (me % 4 + dy) % 4 for dz, dy in OFFSETS]
    place = jnp.stack(index + [core]).astype(jnp.int32)
    owners = jnp.stack([fsdp ^ i for i in range(4)] + [lax.axis_index("dp") % 2]).astype(jnp.int32)

    beside, other = sibling(mine), send(normed, ACROSS)
    above, below = send(normed, DOWN), send(normed, UP)
    over = swap(mine)
    upstream = lax.all_to_all(tie((upstream, normed))[0], "seq", 0, 0, tiled=True).reshape(T, GW)
    here = me // 4
    groups = jnp.stack([1 - here, here, 1 - here]).astype(jnp.int32)
    parity = lax.axis_index("dp") % 2
    weight_half = lax.dynamic_slice_in_dim(projection, parity * 1536, 1536, 1)
    beside, other, above, below, over, upstream, place, owners, weight_half, groups, turned = tie(
        (beside, other, above, below, over, upstream, place, owners, weight_half, groups, groups[1:])
    )
    far = [send(below[:half], UP), send(above[half:], DOWN)]
    columns = [mine, beside, over, sibling(over)]

    def project(rows, groups, count):
        height = sum(r.shape[0] for r in rows)
        return call(
            functools.partial(project_kernel, len(rows)),
            (shape((height, 384)),) * count,
            [SM, SM] + [ANY] * (4 + len(rows)),
            scratch=[
                pltpu.VMEM((count, D, 384), BF),
                pltpu.VMEM((height, D), BF),
                pltpu.SemaphoreType.DMA((4 * count + len(rows),)),
            ],
        )(owners, groups, *columns, *rows)

    (near,) = project([below, above], groups, 1)
    near_got = send(near, ACROSS)
    _, far = tie((near, far))
    last, far_kept = project(far, groups, 2)
    _, turned = tie((last, turned))
    (kept,) = project([normed, below, above, other], turned, 1)
    _, other_late = tie((last, other))
    other_below, other_above = send(other_late, UP), send(other_late, DOWN)
    weight_half = swap(weight_half)
    far_got, far_late, kept = tie((send(last, ACROSS), far, kept))
    other_far = [send(v, ACROSS) for v in far_late]

    def attend(head):
        return call(
            functools.partial(attention_kernel, head),
            shape((T, 256)),
            [SM, SM] + [VM] * 5,
            HEAD_FLOPS[head],
            [
                pltpu.VMEM((T, 128), BF),
                pltpu.VMEM((T, 128), BF),
                pltpu.VMEM((HD + 16, T), BF),
                pltpu.VMEM((HD, T), BF),
                pltpu.VMEM((HD, T), BF),
                pltpu.VMEM((HD, T), BF),
                pltpu.VMEM((2, T, AQ), F32),
                pltpu.VMEM((2, T, AQ), BF),
                pltpu.VMEM((T, 128), F32),
            ],
            T * T,
        )(place, lengths, kept, far_kept, near_got, far_got, upstream)

    def send_back(grads):
        return lax.all_to_all(grads.reshape(SEQ, ROWS, 256), "seq", 0, 0, tiled=True)

    first = attend(0)
    other_below, other_above, other_far, first, weight, weight_half = tie(
        (other_below, other_above, other_far, first, projection, weight_half)
    )
    weight_rest = lax.ppermute(weight_half, "dp", [(i, i ^ 1) for i in range(4)])
    back0 = send_back(first)
    beside = sibling(weight)
    second = attend(1)
    second, back0, beside = tie((second, back0, beside))
    blocks = [normed, below, above, *far, other, other_below, other_above, *other_far]
    back1 = send_back(second)
    keep, out = call(
        weight_gradient_kernel,
        (shape((768, 384), F32), shape((768, 384))),
        [SM, VM, VM] + [ANY] * len(blocks),
        2 * T * D * 384,
        [
            pltpu.VMEM((384, T), BF),
            pltpu.VMEM((T, D), BF),
            pltpu.VMEM((384, D), F32),
            pltpu.SemaphoreType.DMA((len(blocks),)),
        ],
    )(place, first, second, *blocks)
    got = sibling(out)
    partial = call(add_kernel, shape((64, 36, GW)), [VM, VM])(keep, got)
    partial, back1, weight_half, weight_rest = tie((partial, back1, weight_half, weight_rest))
    weights = [projection, beside, weight_half, weight_rest]
    weights += [sibling(weight_half), sibling(weight_rest)]
    partial = lax.all_to_all(partial, ("dp", "zh", "seq"), 0, 0, tiled=True)
    context, input_gradient = call(
        input_gradient_kernel,
        (shape((ROWS, 1024)), shape((ROWS, D), F32)),
        [SM, VM, VM] + [ANY] * 6 + [VM],
        2 * ROWS * D * 3072,
        [
            pltpu.VMEM((ROWS, 3072), BF),
            pltpu.VMEM((4, 384, 3072), BF),
            pltpu.SemaphoreType.DMA((6,)),
        ],
    )(owners, back0, back1, *weights, x)
    partial, context, input_gradient = tie((partial, context, input_gradient))
    projection_gradient = call(combine_kernel, shape((12, 3072), F32), [VM])(partial)
    return (context[None], input_gradient[None], projection_gradient)


def solution(mesh):
    split = jax.sharding.Mesh(mesh.devices.reshape(4, 2, 2, 8), ("dp", "zh", "core", "seq"))
    record = ("dp", "zh", "core")
    placed = (P(record, "seq", None), P(("zh", "core"), None), P(record), P(record, "seq", None))
    return jax.shard_map(
        body,
        mesh=split,
        in_specs=placed,
        out_specs=(P(record, "seq", None), P(record, "seq", None), P((*record, "seq"), None)),
        check_vma=False,
    )
```

```python
import functools

import jax
import jax.numpy as jnp
from jax import lax
from jax.experimental import pallas as pl
from jax.experimental.pallas import tpu as pltpu
from jax.sharding import PartitionSpec as P

BF = jnp.bfloat16
F32 = jnp.float32
D = 1536
HD = 64
T = 2048
ROWS = 256
SEQ = 8
GW = 128
EPS = 1e-05
BQ = 256
AQ = 512
CH = 256
NC = T // CH
VM = pl.BlockSpec(memory_space=pltpu.VMEM)
SM = pl.BlockSpec(memory_space=pltpu.SMEM)
ANY = pl.BlockSpec(memory_space=pl.ANY)


def dot(a, b, dims=((1,), (0,))):
    return lax.dot_general(a, b, (dims, ((), ())), preferred_element_type=F32)


def standardize(x):
    centered = x - jnp.mean(x, axis=1, keepdims=True)
    inv_std = lax.rsqrt(jnp.mean(centered * centered, axis=1, keepdims=True) + EPS)
    return centered * inv_std, inv_std


def fetch(pairs, sems):
    copies = [pltpu.make_async_copy(a, b, sems.at[i]) for i, (a, b) in enumerate(pairs)]
    for copy in copies:
        copy.start()
    return copies


def prepare_kernel(y_ref, x_ref, w_ref, normed_ref, columns_ref, held, sems):
    pairs = []
    for z in range(2):
        for kind in range(3):
            first = pl.multiple_of(kind * 1024 + (z * 4 + y_ref[0]) * GW, GW)
            pairs.append((w_ref.at[:, pl.ds(first, GW)], held.at[z * 3 + kind]))
    copies = fetch(pairs, sems)
    normed_ref[...] = standardize(x_ref[...].astype(F32))[0].astype(BF)
    for copy in copies:
        copy.wait()
    for z in range(2):
        k, v = (held[z * 3 + kind].astype(F32) for kind in (1, 2))
        low = lax.broadcasted_iota(jnp.int32, k.shape, 1) < HD
        at = z * 384
        columns_ref[:, at : at + 128] = jnp.where(low, k, pltpu.roll(v, HD, 1)).astype(BF)
        columns_ref[:, at + 128 : at + 256] = jnp.where(low, pltpu.roll(k, HD, 1), v).astype(BF)
        columns_ref[:, at + 256 : at + 384] = held[z * 3]


def project_kernel(n, owner_ref, group_ref, *refs):
    weights, blocks, outs = refs[:4], refs[4 : 4 + n], refs[4 + n : -3]
    held_weight, held, sems = refs[-3:]
    pairs = []
    for j in range(len(outs)):
        cols = pl.ds(pl.multiple_of(group_ref[j] * 384, 384), 384)
        for f in range(4):
            rows = pl.ds(pl.multiple_of(owner_ref[f] * 384, 384), 384)
            pairs.append((weights[f].at[:, cols], held_weight.at[j, rows, :]))
    at = [sum(b.shape[0] for b in blocks[:i]) for i in range(n)]
    spots = [pl.ds(a, b.shape[0]) for a, b in zip(at, blocks)]
    direct = held.shape[0] == 8
    if not direct:
        pairs += [(b, held.at[spot]) for b, spot in zip(blocks, spots)]
    copies = fetch(pairs, sems)
    for copy in copies[: 4 * len(outs)]:
        copy.wait()
    for i in range(n):
        if not direct:
            copies[i - n].wait()
        rows = blocks[i][...] if direct else held[spots[i], :]
        for j, out_ref in enumerate(outs):
            out_ref[spots[i], :] = dot(rows, held_weight[j]).astype(BF)


def attention_kernel(
    head, pos_ref, len_ref, kept_ref, far_ref, other_ref, last_ref, up_ref, out_ref, kv, ka, vt, kt, qt, ut, s_ref, e_ref, acc
):
    length = len_ref[0]
    hrows = slice(head * HD, (head + 1) * HD)
    lane = lax.broadcasted_iota(jnp.int32, (BQ, 128), 1)
    for b in range(SEQ):
        r = slice(b * BQ, (b + 1) * BQ)
        source, at = (
            (kept_ref, 0), (kept_ref, 1), (kept_ref, 2), (far_ref, 0),
            (kept_ref, 3), (other_ref, 0), (other_ref, 1), (last_ref, 0),
        )[b]
        own = slice(at * BQ, (at + 1) * BQ)
        first = pl.multiple_of(pos_ref[b] * BQ, BQ)
        mine = source[own, head * 128 : (head + 1) * 128]
        kv[r, :] = mine
        keys = mine.astype(F32)
        row = lax.broadcasted_iota(jnp.int32, (BQ, 128), 0) + first
        bias = jnp.where(lane == HD, jnp.where(row < length, 0.0, -1e30), 0.0)
        ka[r, :] = jnp.where(lane < HD, keys, bias).astype(BF)
        flipped = keys.T.astype(BF)
        kt[:, r] = flipped[0:HD]
        vt[0:HD, r] = flipped[HD:128]
        vt[HD : HD + 16, r] = jnp.ones((16, BQ), BF)
        qt[:, r] = (source[own, 256:384].astype(F32) * 0.125).T[hrows].astype(BF)
        u = jnp.where(row < length, up_ref[pl.ds(first, BQ), :].astype(F32), 0.0)
        ut[:, r] = u.T[hrows].astype(BF)
    acc[...] = jnp.zeros_like(acc)
    zeros = jnp.zeros((HD, AQ), BF)
    ones_row = jnp.where(lax.broadcasted_iota(jnp.int32, (HD, AQ), 0) == 0, 1.0, 0.0).astype(BF)
    nt = ((1,), (1,))

    def scores(start, j, c):
        r = slice(c * CH, (c + 1) * CH)
        qa = jnp.concatenate([qt[:, pl.ds(start, AQ)], ones_row], axis=0)
        s = dot(ka[r, :], qa)
        s_ref[j, r, :] = s
        return jnp.max(s.reshape(CH // 8, 8, AQ), axis=0)

    def weigh(peak, j, c):
        r = slice(c * CH, (c + 1) * CH)
        e = jnp.exp(s_ref[j, r, :] - peak).astype(BF)
        e_ref[j, r, :] = e
        return dot(vt[:, r], e)

    def finish(total, start):
        cols = pl.ds(start, AQ)
        inverse = 1.0 / total[HD : HD + 1]
        context = total[0:HD] * inverse
        up = (ut[:, cols].astype(F32) * inverse).astype(BF)
        inner = jnp.sum(up.astype(F32) * context, axis=0, keepdims=True)
        up = jnp.concatenate([zeros, up], axis=0)
        query = jnp.concatenate([qt[:, cols], zeros], axis=0)
        return context, up, query, inner

    def back(state, j, c):
        r = slice(c * CH, (c + 1) * CH)
        context, up, query, inner = state
        e = e_ref[j, r, :]
        ds = (e.astype(F32) * (dot(kv[r, :], up) - inner)).astype(BF)
        acc[r, :] += dot(ds, query, nt) + dot(e, up, nt)
        return dot(kt[:, r], ds)

    def write(block, context, dq):
        for p in range(AQ // BQ):
            part = slice(p * BQ, (p + 1) * BQ)
            first = pl.multiple_of(pos_ref[block * (AQ // BQ) + p] * BQ, BQ)
            col = lax.broadcasted_iota(jnp.int32, (HD, BQ), 1) + first
            kept = jnp.where(col < length, context[:, part], 0.0)
            both = jnp.concatenate([dq[:, part] * 0.125, kept], axis=0)
            out_ref[pl.ds(first, BQ), 0:128] = both.T.astype(BF)

    def add(a, b):
        return b if a is None else a + b

    def top(peak):
        return jnp.max(peak, axis=0, keepdims=True)

    def step(i, peak):
        starts = [pl.multiple_of((2 * i + j) * AQ, AQ) for j in range(2)]
        after = pl.multiple_of(lax.rem(2 * i + 2, T // AQ) * AQ, AQ)
        peak, peak1, total, total1 = top(peak), None, None, None
        for c in range(NC):
            t = scores(starts[1], 1, c)
            peak1 = t if c == 0 else jnp.maximum(peak1, t)
            total = add(total, weigh(peak, 0, c))
        state = finish(total, starts[0])
        peak1, dq = top(peak1), None
        for c in range(NC):
            total1 = add(total1, weigh(peak1, 1, c))
            dq = add(dq, back(state, 0, c))
        state1 = finish(total1, starts[1])
        write(2 * i, state[0], dq)
        dq = None
        for c in range(NC):
            t = scores(after, 0, c)
            peak = t if c == 0 else jnp.maximum(peak, t)
            dq = add(dq, back(state1, 1, c))
        write(2 * i + 1, state1[0], dq)
        return peak

    peak = None
    for c in range(NC):
        t = scores(0, 0, c)
        peak = t if c == 0 else jnp.maximum(peak, t)
    lax.fori_loop(0, T // AQ // 2, step, peak)
    for b in range(SEQ):
        rows = pl.ds(pl.multiple_of(pos_ref[b] * BQ, BQ), BQ)
        out_ref[rows, 128:256] = acc[b * BQ : (b + 1) * BQ, :].astype(BF)


def weight_gradient_kernel(pos_ref, first_ref, second_ref, *refs):
    sources, (keep_ref, send_ref, flipped_ref, held, acc, sems) = refs[:-6], refs[-6:]
    at = [sum(b.shape[0] for b in sources[:i]) for i in range(len(sources))]
    spots = [pl.ds(a, b.shape[0]) for a, b in zip(at, sources)]
    copies = fetch([(b, held.at[spot]) for b, spot in zip(sources, spots)], sems)
    for b in range(SEQ):
        rows = pl.ds(pl.multiple_of(pos_ref[b] * ROWS, ROWS), ROWS)
        cols = slice(b * ROWS, (b + 1) * ROWS)
        both = [g[rows, :].astype(F32).T.astype(BF) for g in (first_ref, second_ref)]
        parts = [g[128:256] for g in both] + [g[0:HD] for g in both]
        flipped_ref[:, cols] = jnp.concatenate(parts, axis=0)
    for half in range(2):
        rows = slice(half * T // 2, (half + 1) * T // 2)
        for i, copy in enumerate(copies):
            if at[i] // (T // 2) == half:
                copy.wait()
        for c in range(3):
            cs = slice(c * 512, (c + 1) * 512)
            t = dot(flipped_ref[:, rows], held[rows, cs])
            acc[:, cs] = t if half == 0 else acc[:, cs] + t
    core = pos_ref[SEQ]
    for c in range(4):
        flipped = acc[:, c * 384 : (c + 1) * 384].T
        halves = [[flipped[i * 96 : (i + 1) * 96] for i in (k, k + 2)] for k in range(2)]
        for k in range(2):
            for i in range(2):
                r = slice((c * 2 + i) * 96, (c * 2 + i + 1) * 96)

                @pl.when(core == k)
                def _():
                    keep_ref[r, :] = halves[k][i]

                @pl.when(core != k)
                def _():
                    send_ref[r, :] = halves[k][i].astype(BF)


def join(first, second, part):
    low = lax.broadcasted_iota(jnp.int32, first.shape, first.ndim - 1) < HD
    if part == 0:
        return jnp.where(low, first, pltpu.roll(second, HD, first.ndim - 1))
    return jnp.where(low, pltpu.roll(first, HD, first.ndim - 1), second)


def add_kernel(keep_ref, got_ref, out_ref):
    for i in range(64 // 8):
        rows = slice(i * 96, (i + 1) * 96)
        t = keep_ref[rows, :] + got_ref[rows, :].astype(F32)
        for s in range(SEQ):
            part = t[s * 12 : (s + 1) * 12]
            part = jnp.concatenate([part[:, k * GW : (k + 1) * GW] for k in range(3)], axis=0)
            out_ref[i * SEQ + s] = part.astype(BF)


def combine_kernel(parts_ref, out_ref):
    for s in range(SEQ):
        total = None
        for r in range(8):
            t = parts_ref[r * SEQ + s].astype(F32)
            total = t if total is None else total + t
        at = s * GW
        low, high = total[0:12], total[12:24]
        out_ref[:, at : at + GW] = total[24:36]
        out_ref[:, 1024 + at : 1024 + at + GW] = join(low, high, 0)
        out_ref[:, 2048 + at : 2048 + at + GW] = join(low, high, 1)


def input_gradient_kernel(
    pos_ref, first_ref, second_ref, w0, w1, w2, w3, w4, w5, x_ref, ctx_ref, out_ref, packed, held, sems
):
    halves = [held.at[f, :, pl.ds(p * 1536, 1536)] for f in (2, 3) for p in range(2)]
    copies = fetch(list(zip((w0, w1, w2, w3, w4, w5), [held.at[0], held.at[1]] + halves)), sems)
    for s in range(SEQ):
        at = s * GW
        a = [first_ref[s, :, i * 128 : (i + 1) * 128].astype(F32) for i in range(2)]
        b = [second_ref[s, :, i * 128 : (i + 1) * 128].astype(F32) for i in range(2)]
        ctx_ref[:, at : at + GW] = join(a[0], b[0], 1).astype(BF)
        packed[:, at : at + GW] = join(a[0], b[0], 0).astype(BF)
        packed[:, 1024 + at : 1024 + at + GW] = join(a[1], b[1], 0).astype(BF)
        packed[:, 2048 + at : 2048 + at + GW] = join(a[1], b[1], 1).astype(BF)
    nt = ((1,), (1,))
    for f in range(4):
        to = pl.ds(pl.multiple_of(pos_ref[f] * 384, 384), 384)
        if f < 2:
            copies[f].wait()
            out_ref[:, to] = dot(packed[...], held[f], nt)
        else:
            total = None
            for p in range(2):
                copies[2 * f - 2 + p].wait()
                cols = pl.ds(pl.multiple_of((pos_ref[4] ^ p) * 1536, 1536), 1536)
                t = dot(packed[:, cols], held[f, :, p * 1536 : (p + 1) * 1536], nt)
                total = t if p == 0 else total + t
            out_ref[:, to] = total
    standard, inv_std = standardize(x_ref[...].astype(F32))
    ng = out_ref[...]
    row_mean = jnp.mean(ng, axis=1, keepdims=True)
    projected = jnp.mean(ng * standard, axis=1, keepdims=True)
    out_ref[...] = inv_std * (ng - row_mean - standard * projected)


def shape(dims, dtype=BF):
    return jax.ShapeDtypeStruct(dims, dtype)


UP = [(i, (i // 4) * 4 + (i % 4 + 1) % 4) for i in range(8)]
DOWN = [(i, (i // 4) * 4 + (i % 4 + 3) % 4) for i in range(8)]
ACROSS = [(i, i ^ 4) for i in range(8)]
SWAP = [(f * 8 + s, (f ^ 1) * 8 + (s ^ 4)) for f in range(2) for s in range(8)]
OFFSETS = [(dz, dy) for dz in range(2) for dy in (0, 3, 1, 2)]
HEAD_FLOPS = (10**9, 10**10)
tie = lax.optimization_barrier


def send(v, way):
    return lax.ppermute(v, "seq", way)


def sibling(v):
    return lax.ppermute(v, "core", [(0, 1), (1, 0)])


def swap(v):
    return lax.ppermute(v, ("zh", "seq"), SWAP)


def call(kernel, out, in_specs, flops=0, scratch=(), transcendentals=0, vmem=56):
    return pl.pallas_call(
        kernel,
        out_shape=out,
        in_specs=in_specs,
        out_specs=jax.tree.map(lambda _: VM, out),
        scratch_shapes=list(scratch),
        compiler_params=pltpu.CompilerParams(vmem_limit_bytes=vmem * 2**20),
        cost_estimate=pl.CostEstimate(
            flops=flops, bytes_accessed=2**20, transcendentals=transcendentals
        ),
    )


def body(frames, projection, lengths, cotangent):
    x = frames[0]
    me = lax.axis_index("seq")
    core = lax.axis_index("core")
    fsdp = lax.axis_index("zh") * 2 + core
    half = ROWS // 2
    normed, mine = call(
        prepare_kernel,
        (shape((ROWS, D)), shape((384, 768))),
        [SM, VM, ANY],
        scratch=[pltpu.VMEM((6, 384, GW), BF), pltpu.SemaphoreType.DMA((6,))],
    )((me % 4)[None].astype(jnp.int32), x, projection)
    upstream = cotangent[0].reshape(ROWS, SEQ, GW).transpose(1, 0, 2)
    index = [(me // 4 ^ dz) * 4 + (me % 4 + dy) % 4 for dz, dy in OFFSETS]
    place = jnp.stack(index + [core]).astype(jnp.int32)
    owners = jnp.stack([fsdp ^ i for i in range(4)] + [lax.axis_index("dp") % 2]).astype(jnp.int32)

    beside, other = sibling(mine), send(normed, ACROSS)
    above, below = send(normed, DOWN), send(normed, UP)
    over = swap(mine)
    upstream = lax.all_to_all(tie((upstream, normed))[0], "seq", 0, 0, tiled=True).reshape(T, GW)
    here = me // 4
    groups = jnp.stack([1 - here, here, 1 - here]).astype(jnp.int32)
    parity = lax.axis_index("dp") % 2
    weight_half = lax.dynamic_slice_in_dim(projection, parity * 1536, 1536, 1)
    beside, other, above, below, over, upstream, place, owners, weight_half, groups, turned = tie(
        (beside, other, above, below, over, upstream, place, owners, weight_half, groups, groups[1:])
    )
    far = [send(below[:half], UP), send(above[half:], DOWN)]
    columns = [mine, beside, over, sibling(over)]

    def project(rows, groups, count):
        height = sum(r.shape[0] for r in rows)
        return call(
            functools.partial(project_kernel, len(rows)),
            (shape((height, 384)),) * count,
            [SM, SM] + [ANY] * 4 + [ANY if count == 1 else VM] * len(rows),
            scratch=[
                pltpu.VMEM((count, D, 384), BF),
                pltpu.VMEM((height if count == 1 else 8, D), BF),
                pltpu.SemaphoreType.DMA((4 * count + len(rows),)),
            ],
        )(owners, groups, *columns, *rows)

    (near,) = project([below, above], groups, 1)
    near_got = send(near, ACROSS)
    _, far = tie((near, far))
    last, far_kept = project(far, groups, 2)
    _, turned = tie((last, turned))
    (kept,) = project([normed, below, above, other], turned, 1)
    _, other_late = tie((last, other))
    other_below, other_above = send(other_late, UP), send(other_late, DOWN)
    weight_half = swap(weight_half)
    far_got, far_late, kept = tie((send(last, ACROSS), far, kept))
    other_far = [send(v, ACROSS) for v in far_late]

    def attend(head):
        return call(
            functools.partial(attention_kernel, head),
            shape((T, 256)),
            [SM, SM] + [VM] * 5,
            HEAD_FLOPS[head],
            [
                pltpu.VMEM((T, 128), BF),
                pltpu.VMEM((T, 128), BF),
                pltpu.VMEM((HD + 16, T), BF),
                pltpu.VMEM((HD, T), BF),
                pltpu.VMEM((HD, T), BF),
                pltpu.VMEM((HD, T), BF),
                pltpu.VMEM((2, T, AQ), F32),
                pltpu.VMEM((2, T, AQ), BF),
                pltpu.VMEM((T, 128), F32),
            ],
            T * T,
        )(place, lengths, kept, far_kept, near_got, far_got, upstream)

    def send_back(grads):
        return lax.all_to_all(grads.reshape(SEQ, ROWS, 256), "seq", 0, 0, tiled=True)

    first = attend(0)
    other_below, other_above, other_far, first, weight, weight_half = tie(
        (other_below, other_above, other_far, first, projection, weight_half)
    )
    weight_rest = lax.ppermute(weight_half, "dp", [(i, i ^ 1) for i in range(4)])
    back0 = send_back(first)
    beside = sibling(weight)
    second = attend(1)
    second, back0, beside = tie((second, back0, beside))
    blocks = [normed, below, above, *far, other, other_below, other_above, *other_far]
    back1 = send_back(second)
    keep, out = call(
        weight_gradient_kernel,
        (shape((768, 384), F32), shape((768, 384))),
        [SM, VM, VM] + [ANY] * len(blocks),
        2 * T * D * 384,
        [
            pltpu.VMEM((384, T), BF),
            pltpu.VMEM((T, D), BF),
            pltpu.VMEM((384, D), F32),
            pltpu.SemaphoreType.DMA((len(blocks),)),
        ],
    )(place, first, second, *blocks)
    got = sibling(out)
    partial = call(add_kernel, shape((64, 36, GW)), [VM, VM])(keep, got)
    partial, back1, weight_half, weight_rest = tie((partial, back1, weight_half, weight_rest))
    weights = [projection, beside, weight_half, weight_rest]
    weights += [sibling(weight_half), sibling(weight_rest)]
    partial = lax.all_to_all(partial, ("dp", "zh", "seq"), 0, 0, tiled=True)
    context, input_gradient = call(
        input_gradient_kernel,
        (shape((ROWS, 1024)), shape((ROWS, D), F32)),
        [SM, VM, VM] + [ANY] * 6 + [VM],
        2 * ROWS * D * 3072,
        [
            pltpu.VMEM((ROWS, 3072), BF),
            pltpu.VMEM((4, 384, 3072), BF),
            pltpu.SemaphoreType.DMA((6,)),
        ],
    )(owners, back0, back1, *weights, x)
    partial, context, input_gradient = tie((partial, context, input_gradient))
    projection_gradient = call(combine_kernel, shape((12, 3072), F32), [VM])(partial)
    return (context[None], input_gradient[None], projection_gradient)


def solution(mesh):
    split = jax.sharding.Mesh(mesh.devices.reshape(4, 2, 2, 8), ("dp", "zh", "core", "seq"))
    record = ("dp", "zh", "core")
    placed = (P(record, "seq", None), P(("zh", "core"), None), P(record), P(record, "seq", None))
    return jax.shard_map(
        body,
        mesh=split,
        in_specs=placed,
        out_specs=(P(record, "seq", None), P(record, "seq", None), P((*record, "seq"), None)),
        check_vma=False,
    )
```
